256 devices in a mesh: dp: 8 (over x, core), seq: 32 (over y, z).
Axes of the slice: x: 4, y: 4, z: 8, core: 2. Of those that a mesh axis runs over, the one named last changes fastest.
Arguments:
- hidden: bfloat16 [8, 4096, 2560], P('dp', 'seq'), may hold values from -6 to 6
- b_proj: bfloat16 [8, 4096, 128], P('dp', 'seq'), may hold values from -2 to 2
- c_proj: bfloat16 [8, 4096, 128], P('dp', 'seq'), may hold values from -2 to 2
- dt_raw: float32 [8, 4096, 40], P('dp', 'seq'), may hold values from -3 to 3
- base_ids: int32 [8, 4096], P('dp', 'seq'), may hold values from 0 to 11
- complement: int32 [12], replicated, may hold values from 0 to 11, each once
- a_log: float32 [40], replicated, may hold values from -20 to 0
- d_skip: float32 [40], replicated, may hold values from 0.5 to 1.5
- dt_bias: float32 [40], replicated, may hold values from -1 to 0.5
- base_shift: float32 [12, 40], replicated, may hold values from -2.5 to 2.5
- conv_w: float32 [4, 2560], replicated, may hold values from -3 to 3
- conv_b: float32 [2560], replicated, may hold values from -2 to 2
- grad_out: bfloat16 [8, 4096, 2560], P('dp', 'seq'), may hold values from -6 to 6
Outputs:
- layer_out: bfloat16 [8, 4096, 2560], P('dp', 'seq')
- d_hidden: bfloat16 [8, 4096, 2560], P('dp', 'seq')
- d_b_proj: float32 [8, 4096, 128], P('dp', 'seq')
- d_c_proj: float32 [8, 4096, 128], P('dp', 'seq')
- d_dt_raw: float32 [8, 4096, 40], P('dp', 'seq')
- d_a_log: float32 [40], replicated
- d_d_skip: float32 [40], replicated
- d_dt_bias: float32 [40], replicated
- d_base_shift: float32 [12, 40], replicated
- d_conv_w: float32 [4, 2560], replicated
- d_conv_b: float32 [2560], replicated
The draws below stay inside these ranges and needn't reach their ends.
Inputs may be any that keep to these rules, and one draw needn't show every extreme that they name: `complement`: every id appears once.
All inputs are finite; a program needn't handle non-finite values.
Results may differ from the reference program's by a relative error of at most 0.0015.
Values may be sent and summed in bfloat16 or wider, within the bound.
No kernel may reach another device: no remote copies, remote signals or barrier semaphores. Data moves between devices by JAX's collectives and lax.ppermute only.
A program may use at most 384 MiB of HBM per device.

```python
import jax
import jax.numpy as jnp
from jax import lax

HEADS = 40
STATE = 128
VOCAB = 12
TOK_DEV = 128
CHANNELS = 2560
SEQ = 4096
WINDOWS = 8


def ramp_levels(span):
    window_number = jnp.arange(WINDOWS, dtype=jnp.int32)
    fraction = jnp.arange(SEQ, dtype=jnp.float32) / float(SEQ - 1)
    rising = window_number % 2 == 1
    position = jnp.where(rising[:, None], 1.0 - fraction[None, :], fraction[None, :])
    return jnp.exp(-span * position)


def draw_a_log(key, part):
    key = jax.random.fold_in(key, 7)
    share_key, slow_key, quick_key = jax.random.split(key, 3)
    slow_share = 0.5
    slow_heads = jax.random.uniform(share_key, (HEADS,), jnp.float32) < slow_share
    slow_rate = jax.random.uniform(slow_key, (HEADS,), jnp.float32, 0.5, 3.0) / SEQ
    fast_rate = jax.random.uniform(quick_key, (HEADS,), jnp.float32, 1.0 / 40.0, 1.0 / 12.0)
    rate = jnp.where(slow_heads, slow_rate, fast_rate) / 0.6
    return jnp.log(rate).astype(jnp.float32)


def draw_hidden(key, part):
    key = jax.random.fold_in(key, 11)
    jitter = jnp.clip(jax.random.normal(key, (WINDOWS, SEQ, CHANNELS), jnp.float32), -6.0, 6.0)
    return (jitter * ramp_levels(4.6)[:, :, None]).astype(jnp.bfloat16)


def draw_b_proj(key, part):
    key = jax.random.fold_in(key, 13)
    values_key = jax.random.fold_in(key, 0)
    jitter = jnp.clip(jax.random.normal(values_key, (WINDOWS, SEQ, STATE), jnp.float32), -6.0, 6.0)
    return (0.3 * jitter * ramp_levels(4.6)[:, :, None]).astype(jnp.bfloat16)


def draw_dt_raw(key, part):
    key = jax.random.fold_in(key, 17)
    drawn_key, other_key = jax.random.split(key)
    extent = (WINDOWS, SEQ, HEADS)
    drawn_window = jnp.arange(WINDOWS, dtype=jnp.int32) % 4 < 2
    drawn_values = jax.random.uniform(drawn_key, extent, jnp.float32, -3.0, -1.5)
    other_values = jnp.clip(0.5 * jax.random.normal(other_key, extent, jnp.float32), -3.0, 3.0)
    return jnp.where(drawn_window[:, None, None], drawn_values, other_values).astype(jnp.float32)


def with_ends(values, stream_key, least, largest):
    index_at = [jax.random.randint(jax.random.fold_in(stream_key, axis), (), 0, length) for axis, length in enumerate(values.shape)]
    longest = values.shape.index(max(values.shape))
    beside = index_at[:longest] + [(index_at[longest] + 1) % values.shape[longest]] + index_at[longest + 1:]
    return values.at[tuple(index_at)].set(least).at[tuple(beside)].set(largest)


def levels(key, shape, cuts, smallest, high):
    factor_of = 1.0
    for axis_at, shards_of in cuts:
        heights = jax.random.uniform(jax.random.fold_in(jax.random.fold_in(key, 6), axis_at), (shards_of,), jnp.float32, smallest / len(cuts), high / len(cuts))
        factor_of = factor_of * jnp.repeat(jnp.exp(heights), shape[axis_at] // shards_of).reshape((-1,) + (1,) * (len(shape) - 1 - axis_at))
    return factor_of


def gaussian(rng, shape, spread, limit, pieces=(), kind=jnp.bfloat16):
    array = spread * jax.random.normal(rng, shape, jnp.float32)
    if pieces:
        array = array * levels(rng, shape, pieces, -0.22, 0.18)
    return jnp.clip(array, -limit, limit).astype(kind)


def setup_inputs(seed: int = 0) -> dict:
    streams_of = jax.random.split(jax.random.key(seed), 14)
    return {
        "hidden": draw_hidden(jax.random.fold_in(streams_of[13], 71), 0),
        "b_proj": draw_b_proj(jax.random.fold_in(streams_of[13], 71), 0),
        "c_proj": gaussian(streams_of[2], (WINDOWS, SEQ, STATE), 0.3, 2.0, ((0, 8), (1, 32))),
        "dt_raw": draw_dt_raw(jax.random.fold_in(streams_of[13], 71), 0),
        "base_ids": with_ends(jax.random.randint(streams_of[4], (WINDOWS, SEQ), 0, VOCAB), jax.random.fold_in(streams_of[4], 1), 0, VOCAB - 1).astype(jnp.int32),
        "complement": jax.random.permutation(streams_of[5], VOCAB).astype(jnp.int32),
        "a_log": draw_a_log(jax.random.fold_in(streams_of[13], 71), 0),
        "d_skip": jnp.clip(jax.random.uniform(streams_of[7], (HEADS,), jnp.float32, 0.5, 1.5), 0.5, 1.5),
        "dt_bias": jnp.clip(jax.random.uniform(streams_of[8], (HEADS,), jnp.float32, -1.0, 0.5), -1.0, 0.5),
        "base_shift": gaussian(streams_of[9], (VOCAB, HEADS), 0.5, 2.5, (), jnp.float32),
        "conv_w": gaussian(streams_of[10], (4, CHANNELS), 0.5, 3.0, (), jnp.float32),
        "conv_b": gaussian(streams_of[11], (CHANNELS,), 0.3, 2.0, (), jnp.float32),
        "grad_out": gaussian(streams_of[12], (WINDOWS, SEQ, CHANNELS), 1.0, 6.0, ((0, 8), (1, 32))),
    }


exact_prec = lax.Precision.HIGHEST

def section_one(window, b_part, c_part, dt_part, onehot, a_log, d_skip, dt_bias, base_shift, conv_w, conv_b):
    rows_here = b_part.shape[0]
    head_count = a_log.shape[0]
    pre_act = conv_b + conv_w[0] * window[3:3 + rows_here] + conv_w[1] * window[2:2 + rows_here] + conv_w[2] * window[1:1 + rows_here] + conv_w[3] * window[0:rows_here]
    conv_out = jax.nn.silu(pre_act)
    shifted = jnp.dot(onehot, base_shift, precision=exact_prec)
    step_size = jax.nn.softplus(dt_part + dt_bias + shifted)
    log_decay = -jnp.exp(a_log) * step_size
    cumul = jnp.cumsum(log_decay, axis=0)
    values = conv_out.reshape(rows_here, head_count, -1)
    scores = jnp.dot(c_part, b_part.T, precision=exact_prec)
    lower_mask = jnp.arange(rows_here)[:, None] >= jnp.arange(rows_here)[None, :]
    gap_logs = jnp.where(lower_mask[:, :, None], cumul[:, None, :] - cumul[None, :, :], -jnp.inf)
    weights = scores[:, :, None] * jnp.exp(gap_logs) * step_size[None, :, :]
    inner_out = jnp.einsum('tsh,shp->thp', weights, values, precision=exact_prec)
    local_out = (inner_out + d_skip[None, :, None] * values).reshape(rows_here, -1)
    tail_weight = jnp.exp(cumul[-1][None, :] - cumul) * step_size
    scaled_values = values * tail_weight[:, :, None]
    state_out = jnp.einsum('shp,sn->hpn', scaled_values, b_part, precision=exact_prec)
    return (local_out, state_out, jnp.exp(cumul[-1]), cumul)

def incoming(cumul, c_part, start_state):
    rows_here = c_part.shape[0]
    reached = jnp.einsum('tn,hpn->thp', c_part, start_state, precision=exact_prec)
    return (jnp.exp(cumul)[:, :, None] * reached).reshape(rows_here, -1)

def one_direction(x_seq, b_seq, c_seq, dt_seq, onehot_seq, param_set):
    length, channels = x_seq.shape
    head_count = param_set[0].shape[0]
    block_rows = TOK_DEV
    padded = jnp.concatenate([jnp.zeros((3, channels), jnp.float32), x_seq], axis=0)

    def group_step(carried, position):
        offset = position * block_rows
        window = lax.dynamic_slice_in_dim(padded, offset, block_rows + 3, 0)
        b_part = lax.dynamic_slice_in_dim(b_seq, offset, block_rows, 0)
        c_part = lax.dynamic_slice_in_dim(c_seq, offset, block_rows, 0)
        dt_part = lax.dynamic_slice_in_dim(dt_seq, offset, block_rows, 0)
        hot_part = lax.dynamic_slice_in_dim(onehot_seq, offset, block_rows, 0)
        local_out, state_out, total, cumul = section_one(window, b_part, c_part, dt_part, hot_part, *param_set)
        group_out = local_out + incoming(cumul, c_part, carried)
        return (total[:, None, None] * carried + state_out, group_out)
    init_state = jnp.zeros((head_count, channels // head_count, b_seq.shape[1]), jnp.float32)
    _, group_outs = lax.scan(jax.checkpoint(group_step), init_state, jnp.arange(length // block_rows, dtype=jnp.int32))
    return group_outs.reshape(length, channels)

def layer_pair(x_seq, b_seq, c_seq, dt_seq, param_set, onehot_fwd, onehot_rev):
    forward_out = one_direction(x_seq, b_seq, c_seq, dt_seq, onehot_fwd, param_set)
    reverse_out = one_direction(x_seq[::-1], b_seq[::-1], c_seq[::-1], dt_seq[::-1], onehot_rev[::-1], param_set)
    return forward_out + reverse_out[::-1]

def reference(hidden, b_proj, c_proj, dt_raw, base_ids, complement, a_log, d_skip, dt_bias, base_shift, conv_w, conv_b, grad_out):
    code_ids = jnp.arange(base_shift.shape[0], dtype=jnp.int32)
    param_set = (a_log, d_skip, dt_bias, base_shift, conv_w, conv_b)

    def per_window(window_args):
        x_seq, b_seq, c_seq, dt_seq, tokens_here, cotangent = window_args
        matches = tokens_here[:, None] == code_ids[None, :]
        onehot_fwd = matches.astype(jnp.float32)
        partner = lax.optimization_barrier(jnp.sum(jnp.where(matches, complement[None, :], 0), axis=1)).astype(jnp.int32)
        onehot_rev = (partner[:, None] == code_ids[None, :]).astype(jnp.float32)

        def run_layer(x_in, b_in, c_in, dt_in, params_in):
            return layer_pair(x_in, b_in, c_in, dt_in, params_in, onehot_fwd, onehot_rev)
        result, pullback = jax.vjp(run_layer, x_seq.astype(jnp.float32), b_seq.astype(jnp.float32), c_seq.astype(jnp.float32), dt_seq, param_set)
        gradients = pullback(cotangent.astype(jnp.float32))
        return (result.astype(jnp.bfloat16), gradients[0].astype(jnp.bfloat16), gradients[1], gradients[2], gradients[3], gradients[4])
    layer_out, d_hidden, d_b_proj, d_c_proj, d_dt_raw, param_grads = lax.map(per_window, (hidden, b_proj, c_proj, dt_raw, base_ids, grad_out))
    summed = [lax.optimization_barrier(jnp.sum(grad_part, axis=0)) for grad_part in param_grads]
    return (layer_out, d_hidden, d_b_proj, d_c_proj, d_dt_raw, summed[0], summed[1], summed[2], summed[3], summed[4], summed[5])
```

```python
import functools

import jax
import jax.numpy as jnp
from jax import lax
from jax.experimental import pallas as pl
from jax.experimental.pallas import tpu as pltpu
from jax.sharding import PartitionSpec as P

bf16 = jnp.bfloat16
f32 = jnp.float32

GROUP = 8
ROWS = 4
LANES = 128
HEADS = 5
WIDTH = 64
CH = HEADS * WIDTH
PACK = 928
VMEM = 58 * 1024 * 1024

Z_GROUPS = [[y * GROUP + z for z in range(GROUP)] for y in range(ROWS)]

NN = (((1,), (0,)), ((), ()))
NT = (((1,), (1,)), ((), ()))
TN = (((0,), (0,)), ((), ()))


def dot(a, b, dims):
    return lax.dot_general(a, b, dims, preferred_element_type=f32)


def split2(a):
    hi = a.astype(bf16)
    return hi, (a - hi.astype(f32)).astype(bf16)


def split3(a):
    hi = a.astype(bf16)
    rest = a - hi.astype(f32)
    mid = rest.astype(bf16)
    return hi, mid, (rest - mid.astype(f32)).astype(bf16)


def exact_dot(a, table, dims):
    hi, mid, lo = split3(a)
    return dot(hi, table, dims) + dot(mid, table, dims) + dot(lo, table, dims)


def iota(shape, axis):
    return lax.broadcasted_iota(jnp.int32, shape, axis)


def zero_one(condition):
    return jnp.where(condition, 1.0, 0.0).astype(bf16)


def square_masks():
    row, col = iota((LANES, LANES), 0), iota((LANES, LANES), 1)
    return row, col


def pack_kernel(comp_ref, hid_ref, grad_ref, b_ref, c_ref, dt_ref, ids_ref, out_ref):
    row, col = square_masks()
    eye = zero_one(row == col)
    for source, base in ((hid_ref, 0), (grad_ref, CH)):
        for block in range(GROUP * CH // LANES):
            piece = source[:, block * LANES : (block + 1) * LANES]
            flipped = dot(eye, piece, NT).astype(bf16)
            for half in range(2):
                channel = block * LANES + half * WIDTH
                target, at = channel // CH, channel % CH
                out_ref[target, base + at : base + at + WIDTH, :] = flipped[
                    half * WIDTH : (half + 1) * WIDTH
                ]
    pick_row, pick_col = iota((GROUP * 8, 40), 0), iota((GROUP * 8, 40), 1)
    pick = zero_one(
        ((pick_row % 8) < HEADS) & ((pick_row // 8) * HEADS + (pick_row % 8) == pick_col)
    )
    parts = [dot(pick, part, NT) for part in split3(dt_ref[...])]
    ids = ids_ref[...]
    partner = jnp.zeros_like(ids)
    for code in range(12):
        partner = jnp.where(ids == code, comp_ref[code], partner)
    both = jnp.concatenate([ids, partner, jnp.zeros((6, LANES), jnp.int32)], axis=0).astype(f32)
    b_rows, c_rows = b_ref[...], c_ref[...]
    for target in range(GROUP):
        out_ref[target, 2 * CH : 2 * CH + LANES, :] = b_rows
        out_ref[target, 2 * CH + LANES : 2 * CH + 2 * LANES, :] = c_rows
        tail = jnp.concatenate(
            [part[target * 8 : target * 8 + 8] for part in parts] + [both], axis=0
        )
        out_ref[target, 2 * CH + 2 * LANES : PACK, :] = tail.astype(bf16)


def pack(complement, hidden, grad, b_rows, c_rows, dt_rows, ids):
    whole = pl.BlockSpec(memory_space=pltpu.VMEM)
    return pl.pallas_call(
        pack_kernel,
        name="pack",
        out_shape=jax.ShapeDtypeStruct((GROUP, PACK, LANES), bf16),
        in_specs=[pl.BlockSpec(memory_space=pltpu.SMEM)] + [whole] * 6,
        out_specs=whole,
        compiler_params=pltpu.CompilerParams(vmem_limit_bytes=VMEM),
    )(complement, hidden, grad, b_rows, c_rows, dt_rows, ids)


(R_STEP_F, R_STEP_R, R_CUM_F, R_CUM_R, R_SIG_F, R_SIG_R, R_TOT_F, R_TOT_R,
 R_PRE_F, R_POST_F, R_PRE_R, R_POST_R) = range(12)


def code_tables(tail):
    code = iota((LANES, LANES), 0)
    tables = []
    for line in (24, 25):
        ids = (tail[line : line + 1] + 3.0).astype(jnp.int32)
        tables.append(zero_one((code == ids) | (code == 2)))
    return tables


def rows_at(slot):
    return slice(slot * 8, slot * 8 + 8)


def heads_at(head, offset=0):
    return slice(offset + head * WIDTH, offset + (head + 1) * WIDTH)


def phase_one_kernel(
    pk, before, after, cw, shift_table, rate,
    x_f, x_r, slope_f, slope_r, u_f, u_r, v_f, v_r, rows, ends_up, ends_down,
    ext, left_x, left_g, run,
):
    row, col = square_masks()
    upper = zero_one(row <= col)
    lower = zero_one(row >= col)
    ones = jnp.ones((LANES, LANES), bf16)
    lane = iota((WIDTH, LANES), 1)
    ext[0] = before[...]
    ext[GROUP + 1] = after[...]

    def chunk(k, _):
        ext[k + 1] = pk[k, :CH, :]
        tail = pk[k, 2 * CH + 2 * LANES : PACK, :].astype(f32)
        dt = tail[0:8] + tail[8:16] + tail[16:24]
        for index, table in enumerate(code_tables(tail)):
            arg = dt + exact_dot(shift_table[...], table, NN)
            decay = jnp.exp(-jnp.abs(arg))
            step = jnp.maximum(arg, 0.0) + jnp.log1p(decay)
            log_decay = rate[...] * step
            rows[k, rows_at(R_STEP_F + index), :] = step
            rows[k, rows_at(R_SIG_F + index), :] = (
                jnp.where(arg >= 0, 1.0, decay) / (1.0 + decay)
            )
            rows[k, rows_at(R_CUM_F + index), :] = exact_dot(log_decay, (upper, lower)[index], NN)
            rows[k, rows_at(R_TOT_F + index), :] = exact_dot(log_decay, ones, NN)
        return 0

    lax.fori_loop(0, GROUP, chunk, 0)

    def body(k, _):
        cums = (rows[k, rows_at(R_CUM_F), :], rows[k, rows_at(R_CUM_R), :])
        growth = [jnp.exp(c) for c in cums]
        tails = [
            jnp.exp(rows[k, rows_at(R_TOT_F + i), :] - cums[i]) * rows[k, rows_at(R_STEP_F + i), :]
            for i in range(2)
        ]
        for head in range(HEADS):
            at = heads_at(head)
            cur = ext[k + 1, at, :].astype(f32)
            prv = ext[k, at, :].astype(f32)
            nxt = ext[k + 2, at, :].astype(f32)
            base = cw[4, at, :] + cw[0, at, :] * cur
            pre_f, pre_r = base, base
            for tap in range(1, 4):
                weight = cw[tap, at, :]
                pre_f += weight * pltpu.roll(jnp.where(lane < LANES - tap, cur, prv), tap, 1)
                pre_r += weight * pltpu.roll(jnp.where(lane >= tap, cur, nxt), LANES - tap, 1)
            grads = pk[k, CH + head * WIDTH : CH + (head + 1) * WIDTH, :].astype(f32)
            for index, (pre, x_ref, slope_ref) in enumerate(
                ((pre_f, x_f, slope_f), (pre_r, x_r, slope_r))
            ):
                gate = 1.0 / (1.0 + jnp.exp(-pre))
                x = pre * gate
                x_ref[k, at, :] = x
                slope_ref[k, at, :] = gate + x * (1.0 - gate)
                hi, lo = split2(x * tails[index][head : head + 1])
                out_at = heads_at(head, index * CH)
                left_x[out_at, :LANES] = hi
                left_x[out_at, LANES:] = lo
                hi, lo = split2(grads * growth[index][head : head + 1])
                left_g[out_at, :LANES] = hi
                left_g[out_at, LANES:] = lo
        b_rows = pk[k, 2 * CH : 2 * CH + LANES, :]
        c_rows = pk[k, 2 * CH + LANES : 2 * CH + 2 * LANES, :]
        states = dot(left_x[...], jnp.concatenate([b_rows, b_rows], axis=0), NN)
        u_f[k] = states[:CH]
        u_r[k] = states[CH:]
        pulls = dot(left_g[...], jnp.concatenate([c_rows, c_rows], axis=0), NN)
        v_f[k] = pulls[:CH]
        v_r[k] = pulls[CH:]
        return 0

    lax.fori_loop(0, GROUP, body, 0)

    run[...] = jnp.zeros_like(run)

    def scan(step, logs):
        up, down = step, GROUP - 1 - step
        pre_f, pre_r, post_f, post_r = logs
        rows[up, rows_at(R_PRE_F), :] = jnp.exp(pre_f)
        rows[up, rows_at(R_PRE_R), :] = jnp.exp(pre_r)
        rows[down, rows_at(R_POST_F), :] = jnp.exp(post_f)
        rows[down, rows_at(R_POST_R), :] = jnp.exp(post_r)
        moves = ((u_f, up, R_TOT_F), (v_r, up, R_TOT_R), (u_r, down, R_TOT_R), (v_f, down, R_TOT_F))
        for slot, (ref, at_chunk, total) in enumerate(moves):
            factor = jnp.exp(rows[at_chunk, rows_at(total), :])
            for head in range(HEADS):
                at = heads_at(head)
                held = run[slot, at, :]
                own = ref[at_chunk, at, :]
                ref[at_chunk, at, :] = held
                run[slot, at, :] = factor[head : head + 1] * held + own
        return (
            pre_f + rows[up, rows_at(R_TOT_F), :],
            pre_r + rows[up, rows_at(R_TOT_R), :],
            post_f + rows[down, rows_at(R_TOT_F), :],
            post_r + rows[down, rows_at(R_TOT_R), :],
        )

    zero = jnp.zeros((8, LANES), f32)
    all_f, all_r, _, _ = lax.fori_loop(0, GROUP, scan, (zero, zero, zero, zero))
    for ends, pair in ((ends_up, (0, 1)), (ends_down, (2, 3))):
        ends[0:CH, :] = run[pair[0]]
        ends[CH : 2 * CH, :] = run[pair[1]]
        ends[2 * CH : 2 * CH + 8, :] = jnp.exp(all_f)
        ends[2 * CH + 8 : 2 * CH + 16, :] = jnp.exp(all_r)


def phase_one(pk, before, after, cw, shift_table, rate):
    whole = pl.BlockSpec(memory_space=pltpu.VMEM)
    block = jax.ShapeDtypeStruct((GROUP, CH, LANES), f32)
    ends = jax.ShapeDtypeStruct((2 * CH + 16, LANES), f32)
    return pl.pallas_call(
        phase_one_kernel,
        name="phase_one",
        out_shape=[block] * 8 + [jax.ShapeDtypeStruct((GROUP, 96, LANES), f32), ends, ends],
        in_specs=[whole] * 6,
        out_specs=[whole] * 11,
        scratch_shapes=[
            pltpu.VMEM((GROUP + 2, CH, LANES), bf16),
            pltpu.VMEM((2 * CH, 2 * LANES), bf16),
            pltpu.VMEM((2 * CH, 2 * LANES), bf16),
            pltpu.VMEM((4, CH, LANES), f32),
        ],
        compiler_params=pltpu.CompilerParams(vmem_limit_bytes=VMEM),
    )(pk, before, after, cw, shift_table, rate)


def phase_two_kernel(
    pk, before, after, cw, rate, skip,
    x_f, x_r, slope_f, slope_r, u_f, u_r, v_f, v_r, rows,
    up_1, up_2, up_3, down_1, down_2, down_3,
    layer, d_hid, spill, wide, conv_out, head_out,
    entry, states, d_states, state_bits, d_state_bits, reach, pulled, gd, xt,
    d_pre_f, d_pre_r, acc, line, acc_rows, d_g, a_hi, a_lo,
):
    row, col = square_masks()
    is_low = row >= col
    is_up = row <= col
    low_one, up_one = zero_one(is_low), zero_one(is_up)
    ones = jnp.ones((LANES, LANES), bf16)
    lane = iota((WIDTH, LANES), 1)

    for slot, (chain, part, total) in enumerate(
        (
            ((up_1, up_2, up_3), 0, 0),
            ((up_1, up_2, up_3), 1, 1),
            ((down_1, down_2, down_3), 0, 1),
            ((down_1, down_2, down_3), 1, 0),
        )
    ):
        near, middle, far = chain
        factor_at = slice(2 * CH + total * 8, 2 * CH + total * 8 + 8)
        near_total, middle_total = near[factor_at, :], middle[factor_at, :]
        for head in range(HEADS):
            at = heads_at(head, part * CH)
            inner = middle[at, :] + middle_total[head : head + 1] * far[at, :]
            entry[slot, heads_at(head), :] = near[at, :] + near_total[head : head + 1] * inner

    line[...] = jnp.zeros_like(line)
    acc[...] = jnp.zeros_like(acc)
    acc_rows[...] = jnp.zeros_like(acc_rows)
    for ref in (d_pre_f, d_pre_r):
        for edge in (0, 1, GROUP + 2, GROUP + 3):
            ref[edge] = jnp.zeros((CH, LANES), f32)

    def body(k, _):
        b_rows = pk[k, 2 * CH : 2 * CH + LANES, :]
        c_rows = pk[k, 2 * CH + LANES : 2 * CH + 2 * LANES, :]
        step = [rows[k, rows_at(R_STEP_F + i), :] for i in range(2)]
        cum = [rows[k, rows_at(R_CUM_F + i), :] for i in range(2)]
        growth = [jnp.exp(c) for c in cum]
        total = [rows[k, rows_at(R_TOT_F + i), :] for i in range(2)]
        tail = [jnp.exp(total[i] - cum[i]) for i in range(2)]
        factor = [jnp.exp(total[i]) for i in range(2)]
        columns = jnp.concatenate(
            [cum[0], cum[1], jnp.zeros((LANES - 16, LANES), f32)], axis=0
        ).T
        into = (
            (states, state_bits, 0, u_f, R_PRE_F, 0),
            (states, state_bits, 1, u_r, R_POST_R, 2),
            (d_states, d_state_bits, 0, v_f, R_POST_F, 3),
            (d_states, d_state_bits, 1, v_r, R_PRE_R, 1),
        )
        for full, bits, index, local, decay_row, slot in into:
            decay = rows[k, rows_at(decay_row), :]
            for head in range(HEADS):
                at, to = heads_at(head), heads_at(head, index * CH)
                value = local[k, at, :] + decay[head : head + 1] * entry[slot, at, :]
                full[to, :] = value
                hi, lo = split2(value)
                bits[to, :LANES] = hi
                bits[to, LANES:] = lo
        reach[...] = dot(state_bits[...], jnp.concatenate([c_rows, c_rows], axis=1), NT)
        pulled[...] = dot(d_state_bits[...], jnp.concatenate([b_rows, b_rows], axis=1), NT)
        scores = dot(c_rows, b_rows, NT)
        d_g[...] = jnp.zeros_like(d_g)
        for head in range(HEADS):
            at = heads_at(head)
            one = slice(head, head + 1)
            gap_f = columns[:, head : head + 1] - cum[0][one]
            gap_r = columns[:, 8 + head : 9 + head] - cum[1][one]
            spread = jnp.exp(jnp.where(is_low, gap_f, gap_r))
            hi, lo = split2(scores * spread)
            a_hi[:, :LANES] = hi * low_one
            a_hi[:, LANES:] = hi * up_one
            a_lo[:, :LANES] = lo * low_one
            a_lo[:, LANES:] = lo * up_one
            grad_bits = pk[k, CH + head * WIDTH : CH + (head + 1) * WIDTH, :]
            grads = grad_bits.astype(f32)
            xs, bits = [], []
            for index, x_ref in enumerate((x_f, x_r)):
                scaled = x_ref[k, at, :] * step[index][one]
                xs.append(scaled)
                bits.append(split2(scaled))
            d_a = dot(
                jnp.concatenate([grad_bits, grad_bits], axis=0),
                jnp.concatenate(
                    [
                        jnp.concatenate([bits[0][0], bits[1][0]], axis=1),
                        jnp.concatenate([bits[0][1], bits[1][1]], axis=1),
                    ],
                    axis=0,
                ),
                TN,
            )
            d_g[...] += spread * (
                jnp.where(is_low, d_a[:, :LANES], 0.0) + jnp.where(is_up, d_a[:, LANES:], 0.0)
            )
            d_xs = dot(grad_bits, a_hi[...], NN) + dot(grad_bits, a_lo[...], NN)
            out = jnp.zeros((WIDTH, LANES), f32)
            d_skip_line = jnp.zeros((WIDTH, LANES), f32)
            for index, (x_ref, slope_ref, d_pre) in enumerate(
                ((x_f, slope_f, d_pre_f), (x_r, slope_r, d_pre_r))
            ):
                to = heads_at(head, index * CH)
                half = slice(index * LANES, (index + 1) * LANES)
                hi, lo = bits[index]
                y = (
                    dot(hi, a_hi[:, half], NT)
                    + dot(lo, a_hi[:, half], NT)
                    + dot(hi, a_lo[:, half], NT)
                    + growth[index][one] * reach[to, :]
                )
                x = x_ref[k, at, :]
                out += y + skip[one, :] * x
                d_skip_line += grads * x
                from_state = tail[index][one] * pulled[to, :]
                d_x = d_xs[:, half] + from_state
                d_pre[k + 2, at, :] = (step[index][one] * d_x + skip[one, :] * grads) * slope_ref[
                    k, at, :
                ]
                own = jnp.sum(x * d_x, axis=0, keepdims=True)
                line[index, one, :] = (
                    jnp.sum(grads * y, axis=0, keepdims=True) - step[index][one] * own
                )
                line[2 + index, one, :] = jnp.sum(
                    xs[index] * from_state
                    + factor[index][one] * (d_states[to, :] * states[to, :]),
                    axis=0,
                    keepdims=True,
                )
                line[4 + index, one, :] = own
                hi, lo = split2(grads * growth[index][one])
                gd[to, :LANES] = hi
                gd[to, LANES:] = lo
                hi, lo = split2(xs[index] * tail[index][one])
                xt[to, :LANES] = hi
                xt[to, LANES:] = lo
            layer[k, at, :] = out.astype(bf16)
            line[6, one, :] = jnp.sum(d_skip_line, axis=0, keepdims=True)
        g_hi, g_lo = split2(d_g[...])
        wide_c = dot(gd[:, :LANES], state_bits[...], TN)
        wide[k, LANES : 2 * LANES, :] = (
            dot(g_hi, b_rows, NN)
            + dot(g_lo, b_rows, NN)
            + wide_c[:, :LANES]
            + wide_c[:, LANES:]
            + dot(gd[:, LANES:], state_bits[:, :LANES], TN)
        )
        wide_b = dot(xt[:, :LANES], d_state_bits[...], TN)
        wide[k, :LANES, :] = (
            dot(g_hi, c_rows, TN)
            + dot(g_lo, c_rows, TN)
            + wide_b[:, :LANES]
            + wide_b[:, LANES:]
            + dot(xt[:, LANES:], d_state_bits[:, :LANES], TN)
        )
        d_args = jnp.zeros((8, LANES), f32)
        tables = code_tables(pk[k, 2 * CH + 2 * LANES : PACK, :].astype(f32))
        for index in range(2):
            d_log = exact_dot(line[index], (low_one, up_one)[index], NN) + exact_dot(
                line[2 + index], ones, NN
            )
            d_step = line[4 + index] + rate[...] * d_log
            d_arg = d_step * rows[k, rows_at(R_SIG_F + index), :]
            d_args += d_arg
            acc_rows[0] += d_log * rate[...] * step[index]
            acc_rows[2] += exact_dot(d_arg, tables[index], NT)
        acc_rows[1] += line[6]
        wide[k, 2 * LANES : 2 * LANES + 8, :] = d_args
        return 0

    lax.fori_loop(0, GROUP, body, 0)

    def spread_taps(tile, hid_of, store):
        for head in range(HEADS):
            at = heads_at(head)
            hid = hid_of(at).astype(f32)
            own_f, own_r = d_pre_f[tile + 1, at, :], d_pre_r[tile + 1, at, :]
            later_f, earlier_r = d_pre_f[tile + 2, at, :], d_pre_r[tile, at, :]
            both = own_f + own_r
            acc[4, at, :] += both
            acc[0, at, :] += hid * both
            total = cw[0, at, :] * both
            for tap in range(1, 4):
                shifted = pltpu.roll(
                    jnp.where(lane >= tap, own_f, later_f), LANES - tap, 1
                ) + pltpu.roll(jnp.where(lane < LANES - tap, own_r, earlier_r), tap, 1)
                acc[tap, at, :] += hid * shifted
                total += cw[tap, at, :] * shifted
            store(at, total)

    def store_spill(slot):
        def put(at, total):
            spill[slot, at, :] = total
        return put

    spread_taps(0, lambda at: before[at, :], store_spill(0))
    spread_taps(GROUP + 1, lambda at: after[at, :], store_spill(1))

    def inner(k, _):
        def put(at, total):
            d_hid[k, at, :] = total
        spread_taps(k + 1, lambda at: pk[k, at, :], put)
        return 0

    lax.fori_loop(0, GROUP, inner, 0)
    line_of = iota((8, LANES), 0)
    sums = jnp.zeros((8, CH), f32)
    for tap in range(5):
        hi, mid, lo = split3(acc[tap])
        marker = zero_one(line_of == tap)
        sums += dot(marker, hi, NT) + dot(marker, mid, NT) + dot(marker, lo, NT)
    conv_out[...] = sums
    lane_col = col
    head_out[...] = (
        exact_dot(acc_rows[0], zero_one(lane_col == 0), NN)
        + exact_dot(acc_rows[1], zero_one(lane_col == 1), NN)
        + acc_rows[2]
    )


def phase_two(pk, before, after, cw, rate, skip, saved, ups, downs):
    whole = pl.BlockSpec(memory_space=pltpu.VMEM)
    wide = jax.ShapeDtypeStruct((GROUP, 2 * LANES + 8, LANES), f32)
    return pl.pallas_call(
        phase_two_kernel,
        name="phase_two",
        out_shape=[
            jax.ShapeDtypeStruct((GROUP, CH, LANES), bf16),
            jax.ShapeDtypeStruct((GROUP, CH, LANES), f32),
            jax.ShapeDtypeStruct((2, CH, LANES), f32),
            wide,
            jax.ShapeDtypeStruct((8, CH), f32),
            jax.ShapeDtypeStruct((8, LANES), f32),
        ],
        in_specs=[whole] * 21,
        out_specs=[whole] * 6,
        scratch_shapes=[
            pltpu.VMEM((4, CH, LANES), f32),
            pltpu.VMEM((2 * CH, LANES), f32),
            pltpu.VMEM((2 * CH, LANES), f32),
            pltpu.VMEM((2 * CH, 2 * LANES), bf16),
            pltpu.VMEM((2 * CH, 2 * LANES), bf16),
            pltpu.VMEM((2 * CH, LANES), f32),
            pltpu.VMEM((2 * CH, LANES), f32),
            pltpu.VMEM((2 * CH, 2 * LANES), bf16),
            pltpu.VMEM((2 * CH, 2 * LANES), bf16),
            pltpu.VMEM((GROUP + 4, CH, LANES), f32),
            pltpu.VMEM((GROUP + 4, CH, LANES), f32),
            pltpu.VMEM((5, CH, LANES), f32),
            pltpu.VMEM((7, 8, LANES), f32),
            pltpu.VMEM((3, 8, LANES), f32),
            pltpu.VMEM((LANES, LANES), f32),
            pltpu.VMEM((LANES, 2 * LANES), bf16),
            pltpu.VMEM((LANES, 2 * LANES), bf16),
        ],
        compiler_params=pltpu.CompilerParams(vmem_limit_bytes=VMEM),
    )(pk, before, after, cw, rate, skip, *saved, *ups, *downs)


def unpack_kernel(layer, d_hid, wide, layer_out, hid_out, b_out, c_out, dt_out):
    row, col = square_masks()
    eye = zero_one(row == col)
    for source, target in ((layer, layer_out), (d_hid, hid_out)):
        for block in range(GROUP * CH // LANES):
            pieces = []
            for half in range(2):
                channel = block * LANES + half * WIDTH
                group, at = channel // CH, channel % CH
                pieces.append(source[group, at : at + WIDTH, :])
            both = jnp.concatenate(pieces, axis=0)
            target[:, block * LANES : (block + 1) * LANES] = dot(eye, both, NT).astype(bf16)
    for base, target in ((0, b_out), (LANES, c_out)):
        total = wide[0, base : base + LANES, :]
        for group in range(1, GROUP):
            total += wide[group, base : base + LANES, :]
        target[...] = total
    lines = jnp.concatenate(
        [wide[group, 2 * LANES : 2 * LANES + 8, :] for group in range(GROUP)]
        + [jnp.zeros((LANES - 8 * GROUP, LANES), f32)],
        axis=0,
    ).T
    pick_row, pick_col = iota((LANES, 40), 0), iota((LANES, 40), 1)
    pick = zero_one(
        ((pick_row % 8) < HEADS) & ((pick_row // 8) * HEADS + (pick_row % 8) == pick_col)
    )
    dt_out[...] = exact_dot(lines, pick, NN)


def unpack(layer, d_hid, wide):
    whole = pl.BlockSpec(memory_space=pltpu.VMEM)
    rows = jax.ShapeDtypeStruct((LANES, GROUP * CH), bf16)
    square = jax.ShapeDtypeStruct((LANES, LANES), f32)
    return pl.pallas_call(
        unpack_kernel,
        name="unpack",
        out_shape=[rows, rows, square, square, jax.ShapeDtypeStruct((LANES, 40), f32)],
        in_specs=[whole] * 3,
        out_specs=[whole] * 5,
        compiler_params=pltpu.CompilerParams(vmem_limit_bytes=VMEM),
    )(layer, d_hid, wide)


def exchange(array):
    return lax.all_to_all(array, "seq", 0, 0, axis_index_groups=Z_GROUPS)


def along_y(array, by):
    pairs = [
        (y * GROUP + z, (y + by) * GROUP + z)
        for y in range(ROWS)
        for z in range(GROUP)
        if 0 <= y + by < ROWS
    ]
    return lax.ppermute(array, "seq", pairs)


def flip_bit(array, axis, bit):
    count = lax.axis_size(axis)
    return lax.ppermute(array, axis, [(i, i ^ bit) for i in range(count)])


def total_over_all(array):
    for axis, bit in (("dp", 1), ("dp", 2), ("dp", 4), ("seq", 8), ("seq", 16)):
        array = array + flip_bit(array, axis, bit)
    array = array[None]
    place = lax.axis_index("seq")
    for bit in (1, 2, 4):
        other = flip_bit(array, "seq", bit)
        is_high = (place & bit) != 0
        array = jnp.concatenate(
            [jnp.where(is_high, other, array), jnp.where(is_high, array, other)], axis=0
        )
    return array


def per_device(
    hidden, b_proj, c_proj, dt_raw, base_ids, complement,
    a_log, d_skip, dt_bias, base_shift, conv_w, conv_b, grad_out,
):
    group = lax.axis_index("seq") % GROUP
    taps = jnp.concatenate([conv_w, conv_b[None]], axis=0).reshape(5, GROUP, CH)
    taps = lax.dynamic_index_in_dim(taps, group, 1, keepdims=False)
    cw = jnp.broadcast_to(taps[:, :, None], (5, CH, LANES))
    per_head = jnp.stack([-jnp.exp(a_log), d_skip], axis=0)
    tables = jnp.concatenate([dt_bias[None], base_shift], axis=0)
    tables = jnp.concatenate([per_head, tables], axis=0).reshape(15, GROUP, HEADS)
    tables = lax.dynamic_index_in_dim(tables, group, 1, keepdims=False)
    tables = jnp.pad(tables, ((0, 0), (0, 8 - HEADS)))
    rate = jnp.broadcast_to(tables[0][:, None], (8, LANES))
    skip = jnp.broadcast_to(tables[1][:, None], (8, LANES))
    shift_table = jnp.pad(tables[2:].T, ((0, 0), (2, LANES - 15)))

    packed = pack(complement, hidden[0], grad_out[0], b_proj[0], c_proj[0], dt_raw[0], base_ids)
    pk = exchange(packed)
    before = along_y(pk[GROUP - 1, :CH], 1)
    after = along_y(pk[0, :CH], -1)
    *saved, ends_up, ends_down = phase_one(pk, before, after, cw, shift_table, rate)
    ups = [along_y(ends_up, by) for by in (1, 2, 3)]
    downs = [along_y(ends_down, -by) for by in (1, 2, 3)]
    layer, d_hid, spill, wide, conv_sum, head_sum = phase_two(
        pk, before, after, cw, rate, skip, saved, ups, downs
    )
    from_next = along_y(spill[0], -1)
    from_prev = along_y(spill[1], 1)
    sums = total_over_all(jnp.concatenate([conv_sum, head_sum], axis=1))
    layer = exchange(layer)
    wide = exchange(wide)
    d_hid = jnp.concatenate(
        [
            (d_hid[:1] + from_prev[None]),
            d_hid[1 : GROUP - 1],
            (d_hid[GROUP - 1 :] + from_next[None]),
        ],
        axis=0,
    ).astype(bf16)
    d_hid = exchange(d_hid)
    layer_out, d_hidden, d_b, d_c, d_dt = unpack(layer, d_hid, wide)

    conv_all = sums[:, :5, :CH].transpose(1, 0, 2).reshape(5, GROUP * CH)
    head_all = sums[:, :HEADS, CH : CH + 15].reshape(GROUP * HEADS, 15)
    return (
        layer_out[None], d_hidden[None], d_b[None], d_c[None], d_dt[None],
        head_all[:, 0], head_all[:, 1], head_all[:, 2], head_all[:, 3:].T,
        conv_all[:4], conv_all[4],
    )


def solution(mesh):
    rows = P("dp", "seq", None)
    placed = (rows, rows, rows, rows, P("dp", "seq"), P(), P(), P(), P(), P(), P(), P(), rows)
    return jax.shard_map(
        per_device,
        mesh=mesh,
        in_specs=placed,
        out_specs=(rows,) * 5 + (P(),) * 6,
        check_vma=False,
    )
```

```python
import functools

import jax
import jax.numpy as jnp
from jax import lax
from jax.experimental import pallas as pl
from jax.experimental.pallas import tpu as pltpu
from jax.sharding import PartitionSpec as P

bf16 = jnp.bfloat16
f32 = jnp.float32

GROUP = 8
ROWS = 4
LANES = 128
HEADS = 5
WIDTH = 64
CH = HEADS * WIDTH
SETS = ((0, 2), (2, 5))
SHARED = 2 * SETS[0][1] * WIDTH
TAIL = SHARED + 2 * LANES
PACK = TAIL + 64
PACK_2 = 2 * (SETS[1][1] - SETS[1][0]) * WIDTH
EDGE = 2 * LANES + 8
WIDE = EDGE + 24
VMEM = 58 * 1024 * 1024

Y_GROUPS = [[y * GROUP + z for y in range(ROWS)] for z in range(GROUP)]
Z_GROUPS = [[y * GROUP + z for z in range(GROUP)] for y in range(ROWS)]

NN = (((1,), (0,)), ((), ()))
NT = (((1,), (1,)), ((), ()))
TN = (((0,), (0,)), ((), ()))


def dot(a, b, dims):
    return lax.dot_general(a, b, dims, preferred_element_type=f32)


def split2(a):
    hi = a.astype(bf16)
    return hi, (a - hi.astype(f32)).astype(bf16)


def split3(a):
    hi = a.astype(bf16)
    rest = a - hi.astype(f32)
    mid = rest.astype(bf16)
    return hi, mid, (rest - mid.astype(f32)).astype(bf16)


def exact_dot(a, table, dims):
    hi, mid, lo = split3(a)
    return dot(hi, table, dims) + dot(mid, table, dims) + dot(lo, table, dims)


def iota(shape, axis):
    return lax.broadcasted_iota(jnp.int32, shape, axis)


def zero_one(condition):
    return jnp.where(condition, 1.0, 0.0).astype(bf16)


def square_masks():
    row, col = iota((LANES, LANES), 0), iota((LANES, LANES), 1)
    return row, col


def pack_kernel(
    comp_ref, hid_ref, grad_ref, b_ref, c_ref, dt_ref, ids_ref, before_ref, after_ref, out_1, out_2
):
    row, col = square_masks()
    eye = zero_one(row == col)
    cut = SETS[0][1] * WIDTH
    for source, order in ((hid_ref, 0), (grad_ref, 1)):
        for block in range(GROUP * CH // LANES):
            piece = source[:, block * LANES : (block + 1) * LANES]
            flipped = dot(eye, piece, NT).astype(bf16)
            for half in range(2):
                channel = block * LANES + half * WIDTH
                target, at = channel // CH, channel % CH
                out, at = (out_1, at + order * cut) if at < cut else (
                    out_2, at - cut + order * (CH - cut)
                )
                out[target, at : at + WIDTH, :] = flipped[half * WIDTH : (half + 1) * WIDTH]
    pick_row, pick_col = iota((GROUP * 8, 40), 0), iota((GROUP * 8, 40), 1)
    pick = zero_one(
        ((pick_row % 8) < HEADS) & ((pick_row // 8) * HEADS + (pick_row % 8) == pick_col)
    )
    parts = [dot(pick, part, NT) for part in split3(dt_ref[...])]
    ids = ids_ref[...]
    partner = jnp.zeros_like(ids)
    for code in range(12):
        partner = jnp.where(ids == code, comp_ref[code], partner)
    both = jnp.concatenate([ids, partner, jnp.zeros((6, LANES), jnp.int32)], axis=0).astype(f32)
    beside = jnp.where(
        iota((8, GROUP * CH), 0) >= 5, before_ref[...].astype(f32), after_ref[...].astype(f32)
    )
    b_rows, c_rows = b_ref[...], c_ref[...]
    for target in range(GROUP):
        out_1[target, SHARED : SHARED + LANES, :] = b_rows
        out_1[target, SHARED + LANES : SHARED + 2 * LANES, :] = c_rows
        mine = beside[:, target * CH : (target + 1) * CH]
        mine = jnp.concatenate([mine, jnp.zeros((8, 3 * LANES - CH), f32)], axis=1)
        tail = jnp.concatenate(
            [part[target * 8 : target * 8 + 8] for part in parts]
            + [both]
            + [mine[:, j * LANES : (j + 1) * LANES] for j in range(3)]
            + [jnp.zeros((8, LANES), f32)],
            axis=0,
        )
        out_1[target, TAIL:PACK, :] = tail.astype(bf16)


WHOLE = pl.BlockSpec(memory_space=pltpu.VMEM)


def pack(complement, hidden, grad, b_rows, c_rows, dt_rows, ids, before, after):
    return pl.pallas_call(
        pack_kernel,
        name="pack",
        out_shape=[
            jax.ShapeDtypeStruct((GROUP, PACK, LANES), bf16),
            jax.ShapeDtypeStruct((GROUP, PACK_2, LANES), bf16),
        ],
        in_specs=[pl.BlockSpec(memory_space=pltpu.SMEM)] + [WHOLE] * 8,
        out_specs=[WHOLE] * 2,
        compiler_params=pltpu.CompilerParams(vmem_limit_bytes=VMEM),
    )(complement, hidden, grad, b_rows, c_rows, dt_rows, ids, before, after)


def cost(heads):
    return pl.CostEstimate(flops=heads * 4_000_000_000, bytes_accessed=8_000_000, transcendentals=0)


def kept(shape):
    return pl.BlockSpec(shape, lambda k: (0,) * len(shape))


def chunked(shape):
    return pl.BlockSpec((1,) + shape, lambda k: (k, 0, 0))


(R_STEP_F, R_STEP_R, R_CUM_F, R_CUM_R, R_SIG_F, R_SIG_R, R_TOT_F, R_TOT_R,
 R_PRE_F, R_POST_F, R_PRE_R, R_POST_R) = range(12)


def code_tables(tail):
    code = iota((LANES, LANES), 0)
    tables = []
    for line in (24, 25):
        ids = (tail[line : line + 1] + 3.0).astype(jnp.int32)
        tables.append(zero_one((code == ids) | (code == 2)))
    return tables


def rows_at(slot):
    return slice(slot * 8, slot * 8 + 8)


def heads_at(head, offset=0):
    return slice(offset + head * WIDTH, offset + (head + 1) * WIDTH)


def beside_chunk(pk1, which, place, block):
    tail = pk1[which, TAIL:PACK, :].astype(f32)
    lines = tail[32 + 8 * block : 40 + 8 * block]
    lines = jnp.concatenate([lines, jnp.zeros((8, LANES), f32)], axis=0).astype(bf16)
    return dot(lines, place, TN).astype(bf16)


def fill_edges(ext, pk1, first):
    token, place = iota((16, LANES), 0), iota((16, LANES), 1)
    before = zero_one((token >= 5) & (token < 8) & (place == token + LANES - 8))
    after = zero_one((token < 3) & (place == token))
    count = ext.shape[1]
    for start in range(0, count, LANES):
        size = min(LANES, count - start)
        block = (first * WIDTH + start) // LANES
        ext[0, start : start + size, :] = beside_chunk(pk1, 0, before, block)[:size]
        ext[GROUP + 1, start : start + size, :] = beside_chunk(pk1, GROUP - 1, after, block)[:size]


def phase_one_kernel(first, heads, *refs):
    if first == 0:
        pk1, cw, shift_table, rate = refs[:4]
        pk, refs = pk1, refs[4:]
        rows = refs[8]
        x_f, x_r, slope_f, slope_r, u_f, u_r, v_f, v_r = refs[:8]
        refs = refs[9:]
    else:
        pk1, pk, cw, rows = refs[:4]
        x_f, x_r, slope_f, slope_r, u_f, u_r, v_f, v_r = refs[4:12]
        refs = refs[12:]
    ends_up, ends_down, ext, left_x, left_g, run = refs
    width = heads * WIDTH
    k = pl.program_id(0)
    lane = iota((WIDTH, LANES), 1)

    @pl.when(k == 0)
    def _():
        fill_edges(ext, pk1, first)
        for chunk in range(GROUP):
            ext[chunk + 1] = pk[chunk, :width, :]
        if first == 0:
            row, col = square_masks()
            upper = zero_one(row <= col)
            lower = zero_one(row >= col)
            ones = jnp.ones((LANES, LANES), bf16)
            pre = [jnp.zeros((8, LANES), f32)] * 2
            for chunk in range(GROUP):
                tail = pk1[chunk, TAIL:PACK, :].astype(f32)
                dt = tail[0:8] + tail[8:16] + tail[16:24]
                for index, table in enumerate(code_tables(tail)):
                    arg = dt + exact_dot(shift_table[...], table, NN)
                    decay = jnp.exp(-jnp.abs(arg))
                    step = jnp.maximum(arg, 0.0) + jnp.log1p(decay)
                    log_decay = rate[...] * step
                    total = exact_dot(log_decay, ones, NN)
                    rows[chunk, rows_at(R_STEP_F + index), :] = step
                    rows[chunk, rows_at(R_SIG_F + index), :] = (
                        jnp.where(arg >= 0, 1.0, decay) / (1.0 + decay)
                    )
                    rows[chunk, rows_at(R_CUM_F + index), :] = exact_dot(
                        log_decay, (upper, lower)[index], NN
                    )
                    rows[chunk, rows_at(R_TOT_F + index), :] = total
                    rows[chunk, rows_at((R_PRE_F, R_PRE_R)[index]), :] = jnp.exp(pre[index])
                    pre[index] = pre[index] + total
            post = [jnp.zeros((8, LANES), f32)] * 2
            for chunk in reversed(range(GROUP)):
                for index in range(2):
                    rows[chunk, rows_at((R_POST_F, R_POST_R)[index]), :] = jnp.exp(post[index])
                    post[index] = post[index] + rows[chunk, rows_at(R_TOT_F + index), :]

    cums = (rows[k, rows_at(R_CUM_F), :], rows[k, rows_at(R_CUM_R), :])
    growth = [jnp.exp(c) for c in cums]
    tails = [
        jnp.exp(rows[k, rows_at(R_TOT_F + i), :] - cums[i]) * rows[k, rows_at(R_STEP_F + i), :]
        for i in range(2)
    ]
    for head in range(heads):
        at = heads_at(head)
        one = slice(first + head, first + head + 1)
        cur = ext[k + 1, at, :].astype(f32)
        prv = ext[k, at, :].astype(f32)
        nxt = ext[k + 2, at, :].astype(f32)
        base = cw[4, at, :] + cw[0, at, :] * cur
        pre_f, pre_r = base, base
        for tap in range(1, 4):
            weight = cw[tap, at, :]
            pre_f += weight * pltpu.roll(jnp.where(lane < LANES - tap, cur, prv), tap, 1)
            pre_r += weight * pltpu.roll(jnp.where(lane >= tap, cur, nxt), LANES - tap, 1)
        grads = pk[k, width + head * WIDTH : width + (head + 1) * WIDTH, :].astype(f32)
        for index, (pre_act, x_ref, slope_ref) in enumerate(
            ((pre_f, x_f, slope_f), (pre_r, x_r, slope_r))
        ):
            gate = 1.0 / (1.0 + jnp.exp(-pre_act))
            x = pre_act * gate
            x_ref[0, at, :] = x
            slope_ref[0, at, :] = gate + x * (1.0 - gate)
            hi, lo = split2(x * tails[index][one])
            out_at = heads_at(head, index * width)
            left_x[out_at, :LANES] = hi
            left_x[out_at, LANES:] = lo
            hi, lo = split2(grads * growth[index][one])
            left_g[out_at, :LANES] = hi
            left_g[out_at, LANES:] = lo
    b_rows = pk1[k, SHARED : SHARED + LANES, :]
    c_rows = pk1[k, SHARED + LANES : SHARED + 2 * LANES, :]
    states = dot(left_x[...], jnp.concatenate([b_rows, b_rows], axis=0), NN)
    u_f[k] = states[:width]
    u_r[k] = states[width:]
    pulls = dot(left_g[...], jnp.concatenate([c_rows, c_rows], axis=0), NN)
    v_f[k] = pulls[:width]
    v_r[k] = pulls[width:]

    @pl.when(k == GROUP - 1)
    def _():
        run[...] = jnp.zeros_like(run)

        def scan(step, _):
            up, down = step, GROUP - 1 - step
            moves = (
                (u_f, up, R_TOT_F), (v_r, up, R_TOT_R), (u_r, down, R_TOT_R), (v_f, down, R_TOT_F)
            )
            for slot, (ref, at_chunk, total) in enumerate(moves):
                factor = jnp.exp(rows[at_chunk, rows_at(total), :])
                for head in range(heads):
                    at = heads_at(head)
                    held = run[slot, at, :]
                    own = ref[at_chunk, at, :]
                    ref[at_chunk, at, :] = held
                    run[slot, at, :] = factor[first + head : first + head + 1] * held + own
            return 0

        lax.fori_loop(0, GROUP, scan, 0)
        whole = [
            rows[GROUP - 1, rows_at(pre), :] * jnp.exp(rows[GROUP - 1, rows_at(total), :])
            for pre, total in ((R_PRE_F, R_TOT_F), (R_PRE_R, R_TOT_R))
        ]
        for ends, pair in ((ends_up, (0, 1)), (ends_down, (2, 3))):
            ends[0:width, :] = run[pair[0]]
            ends[width : 2 * width, :] = run[pair[1]]
            ends[2 * width : 2 * width + 8, :] = whole[0]
            ends[2 * width + 8 : 2 * width + 16, :] = whole[1]


def phase_one(which, pk1, pk, cw, extra):
    first, last = SETS[which]
    heads = last - first
    width = heads * WIDTH
    block = jax.ShapeDtypeStruct((GROUP, width, LANES), f32)
    rows = jax.ShapeDtypeStruct((GROUP, 96, LANES), f32)
    ends = jax.ShapeDtypeStruct((2 * width + 16, LANES), f32)
    outs = [block] * 8 + ([rows] if which == 0 else []) + [ends, ends]
    specs = [chunked((width, LANES))] * 4 + [kept(out.shape) for out in outs[4:]]
    operands = [pk1, cw, *extra] if which == 0 else [pk1, pk, cw, *extra]
    return pl.pallas_call(
        functools.partial(phase_one_kernel, first, heads),
        name=f"phase_one_{which}",
        grid=(GROUP,),
        out_shape=outs,
        in_specs=[kept(operand.shape) for operand in operands],
        out_specs=specs,
        scratch_shapes=[
            pltpu.VMEM((GROUP + 2, width, LANES), bf16),
            pltpu.VMEM((2 * width, 2 * LANES), bf16),
            pltpu.VMEM((2 * width, 2 * LANES), bf16),
            pltpu.VMEM((4, width, LANES), f32),
        ],
        cost_estimate=cost(heads),
        compiler_params=pltpu.CompilerParams(vmem_limit_bytes=VMEM),
    )(*operands)


def phase_two_kernel(first, heads, *refs):
    (
        place_y, pk1, pk, cw, rate, skip,
        x_f, x_r, slope_f, slope_r, u_f, u_r, v_f, v_r, rows, ends,
    ) = refs[:16]
    refs = refs[16:]
    if first:
        wide_in, edges_in = refs[:2]
        refs = refs[2:]
    (
        rows_out, wide, edges, conv_out, head_out,
        ext, entry, states, d_states, state_bits, d_state_bits, reach, pulled, gd, xt,
        d_pre_f, d_pre_r, acc, line, acc_rows, d_g, a_hi, a_lo,
    ) = refs
    width = heads * WIDTH
    k = pl.program_id(0)
    row, col = square_masks()
    is_low = row >= col
    is_up = row <= col
    low_one, up_one = zero_one(is_low), zero_one(is_up)
    ones = jnp.ones((LANES, LANES), bf16)
    lane = iota((WIDTH, LANES), 1)

    def held(start, stop):
        return wide_in[0, start:stop, :] if first else 0.0

    @pl.when(k == 0)
    def _():
        fill_edges(ext, pk1, first)
        entry[...] = jnp.zeros_like(entry)
        here = place_y[0]
        for order in range(ROWS - 1):
            for other, slots, reached in (
                (order, ((0, 0, 0), (1, 1, 1)), order < here),
                (ROWS - 1 - order, ((2, 0, 1), (3, 1, 0)), ROWS - 1 - order > here),
            ):

                @pl.when(reached)
                def _(other=other, slots=slots):
                    for slot, part, total in slots:
                        start = 2 * width + total * 8
                        factor = ends[other, start : start + 8, :]
                        for head in range(heads):
                            at = heads_at(head)
                            entry[slot, at, :] = (
                                factor[first + head : first + head + 1] * entry[slot, at, :]
                                + ends[other, heads_at(head, part * width), :]
                            )

        line[...] = jnp.zeros_like(line)
        acc[...] = jnp.zeros_like(acc)
        acc_rows[...] = jnp.zeros_like(acc_rows)
        for ref in (d_pre_f, d_pre_r):
            for edge in (0, 1, GROUP + 2, GROUP + 3):
                ref[edge] = jnp.zeros((width, LANES), f32)

    b_rows = pk1[k, SHARED : SHARED + LANES, :]
    c_rows = pk1[k, SHARED + LANES : SHARED + 2 * LANES, :]
    step = [rows[0, rows_at(R_STEP_F + i), :] for i in range(2)]
    cum = [rows[0, rows_at(R_CUM_F + i), :] for i in range(2)]
    growth = [jnp.exp(c) for c in cum]
    total = [rows[0, rows_at(R_TOT_F + i), :] for i in range(2)]
    tail = [jnp.exp(total[i] - cum[i]) for i in range(2)]
    factor = [jnp.exp(total[i]) for i in range(2)]
    columns = jnp.concatenate(
        [cum[0], cum[1], jnp.zeros((LANES - 16, LANES), f32)], axis=0
    ).T
    into = (
        (states, state_bits, 0, u_f, R_PRE_F, 0),
        (states, state_bits, 1, u_r, R_POST_R, 2),
        (d_states, d_state_bits, 0, v_f, R_POST_F, 3),
        (d_states, d_state_bits, 1, v_r, R_PRE_R, 1),
    )
    for full, bits, index, local, decay_row, slot in into:
        decay = rows[0, rows_at(decay_row), :]
        for head in range(heads):
            at, to = heads_at(head), heads_at(head, index * width)
            value = local[0, at, :] + decay[first + head : first + head + 1] * entry[slot, at, :]
            full[to, :] = value
            hi, lo = split2(value)
            bits[to, :LANES] = hi
            bits[to, LANES:] = lo
    reach[...] = dot(state_bits[...], jnp.concatenate([c_rows, c_rows], axis=1), NT)
    pulled[...] = dot(d_state_bits[...], jnp.concatenate([b_rows, b_rows], axis=1), NT)
    scores = dot(c_rows, b_rows, NT)
    d_g[...] = jnp.zeros_like(d_g)
    for head in range(heads):
        at = heads_at(head)
        one = slice(first + head, first + head + 1)
        gap_f = columns[:, first + head : first + head + 1] - cum[0][one]
        gap_r = columns[:, 8 + first + head : 9 + first + head] - cum[1][one]
        spread = jnp.exp(jnp.where(is_low, gap_f, gap_r))
        hi, lo = split2(scores * spread)
        a_hi[:, :LANES] = hi * low_one
        a_hi[:, LANES:] = hi * up_one
        a_lo[:, :LANES] = lo * low_one
        a_lo[:, LANES:] = lo * up_one
        grad_bits = pk[k, width + head * WIDTH : width + (head + 1) * WIDTH, :]
        grads = grad_bits.astype(f32)
        xs, bits = [], []
        for index, x_ref in enumerate((x_f, x_r)):
            scaled = x_ref[0, at, :] * step[index][one]
            xs.append(scaled)
            bits.append(split2(scaled))
        d_a = dot(
            jnp.concatenate([grad_bits, grad_bits], axis=0),
            jnp.concatenate(
                [
                    jnp.concatenate([bits[0][0], bits[1][0]], axis=1),
                    jnp.concatenate([bits[0][1], bits[1][1]], axis=1),
                ],
                axis=0,
            ),
            TN,
        )
        d_g[...] += spread * (
            jnp.where(is_low, d_a[:, :LANES], 0.0) + jnp.where(is_up, d_a[:, LANES:], 0.0)
        )
        d_xs = dot(grad_bits, a_hi[...], NN) + dot(grad_bits, a_lo[...], NN)
        out = jnp.zeros((WIDTH, LANES), f32)
        d_skip_line = jnp.zeros((WIDTH, LANES), f32)
        for index, (x_ref, slope_ref, d_pre) in enumerate(
            ((x_f, slope_f, d_pre_f), (x_r, slope_r, d_pre_r))
        ):
            to = heads_at(head, index * width)
            half = slice(index * LANES, (index + 1) * LANES)
            hi, lo = bits[index]
            y = (
                dot(hi, a_hi[:, half], NT)
                + dot(lo, a_hi[:, half], NT)
                + dot(hi, a_lo[:, half], NT)
                + growth[index][one] * reach[to, :]
            )
            x = x_ref[0, at, :]
            out += y + skip[one, :] * x
            d_skip_line += grads * x
            from_state = tail[index][one] * pulled[to, :]
            d_x = d_xs[:, half] + from_state
            d_pre[k + 2, at, :] = (step[index][one] * d_x + skip[one, :] * grads) * slope_ref[
                0, at, :
            ]
            own = jnp.sum(x * d_x, axis=0, keepdims=True)
            line[index, one, :] = (
                jnp.sum(grads * y, axis=0, keepdims=True) - step[index][one] * own
            )
            line[2 + index, one, :] = jnp.sum(
                xs[index] * from_state
                + factor[index][one] * (d_states[to, :] * states[to, :]),
                axis=0,
                keepdims=True,
            )
            line[4 + index, one, :] = own
            hi, lo = split2(grads * growth[index][one])
            gd[to, :LANES] = hi
            gd[to, LANES:] = lo
            hi, lo = split2(xs[index] * tail[index][one])
            xt[to, :LANES] = hi
            xt[to, LANES:] = lo
        rows_out[k, at, :] = out.astype(bf16)
        line[6, one, :] = jnp.sum(d_skip_line, axis=0, keepdims=True)
    g_hi, g_lo = split2(d_g[...])
    wide_c = dot(gd[:, :LANES], state_bits[...], TN)
    wide[0, LANES : 2 * LANES, :] = held(LANES, 2 * LANES) + (
        dot(g_hi, b_rows, NN)
        + dot(g_lo, b_rows, NN)
        + wide_c[:, :LANES]
        + wide_c[:, LANES:]
        + dot(gd[:, LANES:], state_bits[:, :LANES], TN)
    )
    wide_b = dot(xt[:, :LANES], d_state_bits[...], TN)
    wide[0, :LANES, :] = held(0, LANES) + (
        dot(g_hi, c_rows, TN)
        + dot(g_lo, c_rows, TN)
        + wide_b[:, :LANES]
        + wide_b[:, LANES:]
        + dot(xt[:, LANES:], d_state_bits[:, :LANES], TN)
    )
    d_args = jnp.zeros((8, LANES), f32)
    tables = code_tables(pk1[k, TAIL:PACK, :].astype(f32))
    for index in range(2):
        d_log = exact_dot(line[index], (low_one, up_one)[index], NN) + exact_dot(
            line[2 + index], ones, NN
        )
        d_step = line[4 + index] + rate[...] * d_log
        d_arg = d_step * rows[0, rows_at(R_SIG_F + index), :]
        d_args += d_arg
        acc_rows[0] += d_log * rate[...] * step[index]
        acc_rows[2] += exact_dot(d_arg, tables[index], NT)
    acc_rows[1] += line[6]
    wide[0, 2 * LANES : EDGE, :] = held(2 * LANES, EDGE) + d_args
    wide[0, EDGE:, :] = jnp.zeros((WIDE - EDGE, LANES), f32)

    @pl.when(k == GROUP - 1)
    def _():
        edges[...] = edges_in[...] if first else jnp.zeros_like(edges)
        token, place = iota((8, LANES), 0), iota((8, LANES), 1)
        first_rows = zero_one((token < 3) & (place == token))
        last_rows = zero_one((token >= 5) & (place == token + LANES - 8))

        def lines_of(marker, tile):
            hi, mid, lo = split3(tile)
            return dot(marker, hi, NT) + dot(marker, mid, NT) + dot(marker, lo, NT)

        def put_edge(slot, marker):
            def put(head, total):
                channel = (first + head) * WIDTH
                block, offset = channel // LANES, channel % LANES
                edges[slot, block * 8 : block * 8 + 8, offset : offset + WIDTH] = lines_of(
                    marker, total
                )
            return put

        def taps_of(tile, hid, puts):
            for head in range(heads):
                at = heads_at(head)
                hid_here = hid[at, :].astype(f32)
                own_f, own_r = d_pre_f[tile + 1, at, :], d_pre_r[tile + 1, at, :]
                later_f, earlier_r = d_pre_f[tile + 2, at, :], d_pre_r[tile, at, :]
                both = own_f + own_r
                acc[4, at, :] += both
                acc[0, at, :] += hid_here * both
                total = cw[0, at, :] * both
                for tap in range(1, 4):
                    shifted = pltpu.roll(
                        jnp.where(lane >= tap, own_f, later_f), LANES - tap, 1
                    ) + pltpu.roll(jnp.where(lane < LANES - tap, own_r, earlier_r), tap, 1)
                    acc[tap, at, :] += hid_here * shifted
                    total += cw[tap, at, :] * shifted
                for put in puts:
                    put(head, total)

        def keep_chunk(chunk):
            def put(head, total):
                rows_out[chunk, heads_at(head, width), :] = total.astype(bf16)
            return put

        taps_of(0, ext[0], [put_edge(2, last_rows)])
        taps_of(GROUP + 1, ext[GROUP + 1], [put_edge(3, first_rows)])
        taps_of(1, pk[0], [keep_chunk(0), put_edge(0, first_rows)])
        taps_of(GROUP, pk[GROUP - 1], [keep_chunk(GROUP - 1), put_edge(1, last_rows)])

        def inner(chunk, _):
            taps_of(chunk + 1, pk.at[chunk], [keep_chunk(chunk)])
            return 0

        lax.fori_loop(1, GROUP - 1, inner, 0)
        sums = jnp.zeros((8, width), f32)
        for tap in range(5):
            sums += lines_of(zero_one(token == tap), acc[tap])
        conv_out[...] = sums
        head_out[...] = (
            exact_dot(acc_rows[0], zero_one(col == 0), NN)
            + exact_dot(acc_rows[1], zero_one(col == 1), NN)
            + acc_rows[2]
        )


def phase_two(which, place_y, pk1, pk, cw, rate, skip, saved, rows, ends, carried):
    first, last = SETS[which]
    heads = last - first
    width = heads * WIDTH
    outs = [
        jax.ShapeDtypeStruct((GROUP, 2 * width, LANES), bf16),
        jax.ShapeDtypeStruct((GROUP, WIDE, LANES), f32),
        jax.ShapeDtypeStruct((4, 24, LANES), f32),
        jax.ShapeDtypeStruct((8, width), f32),
        jax.ShapeDtypeStruct((8, LANES), f32),
    ]
    whole = [pk1, pk, cw, rate, skip]
    in_specs = (
        [pl.BlockSpec(memory_space=pltpu.SMEM)]
        + [kept(operand.shape) for operand in whole]
        + [chunked((width, LANES))] * 8
        + [chunked((96, LANES)), kept(ends.shape)]
    )
    if which:
        in_specs += [chunked((WIDE, LANES)), kept((4, 24, LANES))]
    return pl.pallas_call(
        functools.partial(phase_two_kernel, first, heads),
        name=f"phase_two_{which}",
        grid=(GROUP,),
        out_shape=outs,
        in_specs=in_specs,
        out_specs=[kept(outs[0].shape), chunked((WIDE, LANES))] + [kept(o.shape) for o in outs[2:]],
        scratch_shapes=[
            pltpu.VMEM((GROUP + 2, width, LANES), bf16),
            pltpu.VMEM((4, width, LANES), f32),
            pltpu.VMEM((2 * width, LANES), f32),
            pltpu.VMEM((2 * width, LANES), f32),
            pltpu.VMEM((2 * width, 2 * LANES), bf16),
            pltpu.VMEM((2 * width, 2 * LANES), bf16),
            pltpu.VMEM((2 * width, LANES), f32),
            pltpu.VMEM((2 * width, LANES), f32),
            pltpu.VMEM((2 * width, 2 * LANES), bf16),
            pltpu.VMEM((2 * width, 2 * LANES), bf16),
            pltpu.VMEM((GROUP + 4, width, LANES), f32),
            pltpu.VMEM((GROUP + 4, width, LANES), f32),
            pltpu.VMEM((5, width, LANES), f32),
            pltpu.VMEM((7, 8, LANES), f32),
            pltpu.VMEM((3, 8, LANES), f32),
            pltpu.VMEM((LANES, LANES), f32),
            pltpu.VMEM((LANES, 2 * LANES), bf16),
            pltpu.VMEM((LANES, 2 * LANES), bf16),
        ],
        cost_estimate=cost(2 * heads),
        compiler_params=pltpu.CompilerParams(vmem_limit_bytes=VMEM),
    )(place_y, *whole, *saved, rows, ends, *carried)


def unpack_kernel(place_z, rows_1, rows_2, wide, layer_out, hid_out, b_out, c_out, dt_out):
    row, col = square_masks()
    eye = zero_one(row == col)
    cut = SETS[0][1] * WIDTH
    line = iota((16, LANES), 0)
    at_start = (line < 3) & (place_z[0] == 0)
    at_end = (line >= 13) & (place_z[0] == GROUP - 1)
    blank = jnp.zeros((8, LANES), f32)
    for order, target in enumerate((layer_out, hid_out)):
        for block in range(GROUP * CH // LANES):
            pieces, edge = [], []
            for half in range(2):
                channel = block * LANES + half * WIDTH
                group, at = channel // CH, channel % CH
                offset = at % LANES
                start = EDGE + at // LANES * 8
                edge.append(wide[group, start : start + 8, offset : offset + WIDTH])
                ref, at = (rows_1, at + order * cut) if at < cut else (
                    rows_2, at - cut + order * (CH - cut)
                )
                pieces.append(ref[group, at : at + WIDTH, :])
            lanes = slice(block * LANES, (block + 1) * LANES)
            flipped = dot(eye, jnp.concatenate(pieces, axis=0), NT)
            if order:
                edge = jnp.concatenate(edge, axis=1)
                head = jnp.where(at_start, jnp.concatenate([edge, blank], axis=0), flipped[:16])
                tail = jnp.where(
                    at_end, jnp.concatenate([blank, edge], axis=0), flipped[LANES - 16 :]
                )
                flipped = jnp.concatenate([head, flipped[16 : LANES - 16], tail], axis=0)
            target[:, lanes] = flipped.astype(bf16)
    for base, target in ((0, b_out), (LANES, c_out)):
        total = wide[0, base : base + LANES, :]
        for group in range(1, GROUP):
            total += wide[group, base : base + LANES, :]
        target[...] = total
    lines = jnp.concatenate(
        [wide[group, 2 * LANES : 2 * LANES + 8, :] for group in range(GROUP)]
        + [jnp.zeros((LANES - 8 * GROUP, LANES), f32)],
        axis=0,
    ).T
    pick_row, pick_col = iota((LANES, 40), 0), iota((LANES, 40), 1)
    pick = zero_one(
        ((pick_row % 8) < HEADS) & ((pick_row // 8) * HEADS + (pick_row % 8) == pick_col)
    )
    dt_out[...] = exact_dot(lines, pick, NN)


def unpack(place_z, rows_1, rows_2, wide):
    rows = jax.ShapeDtypeStruct((LANES, GROUP * CH), bf16)
    square = jax.ShapeDtypeStruct((LANES, LANES), f32)
    return pl.pallas_call(
        unpack_kernel,
        name="unpack",
        out_shape=[rows, rows, square, square, jax.ShapeDtypeStruct((LANES, 40), f32)],
        in_specs=[pl.BlockSpec(memory_space=pltpu.SMEM)] + [WHOLE] * 3,
        out_specs=[WHOLE] * 5,
        compiler_params=pltpu.CompilerParams(vmem_limit_bytes=VMEM),
    )(place_z, rows_1, rows_2, wide)


def exchange(array):
    return lax.all_to_all(array, "seq", 0, 0, axis_index_groups=Z_GROUPS)


def along_y(array, by):
    pairs = [
        (y * GROUP + z, (y + by) * GROUP + z)
        for y in range(ROWS)
        for z in range(GROUP)
        if 0 <= y + by < ROWS
    ]
    return lax.ppermute(array, "seq", pairs)


def beside(array, by):
    count = lax.axis_size("seq")
    return lax.ppermute(array, "seq", [(i, i + by) for i in range(count) if 0 <= i + by < count])


def cross_y(up, down, run):
    later = (jnp.arange(ROWS) > run)[:, None, None]
    return lax.all_to_all(
        jnp.where(later, up[None], down[None]), "seq", 0, 0, axis_index_groups=Y_GROUPS
    )


def flip_bit(array, axis, bit):
    count = lax.axis_size(axis)
    return lax.ppermute(array, axis, [(i, i ^ bit) for i in range(count)])


def total_over_all(array):
    for axis, bit in (("dp", 1), ("dp", 2), ("dp", 4), ("seq", 8), ("seq", 16)):
        array = array + flip_bit(array, axis, bit)
    array = array[None]
    place = lax.axis_index("seq")
    for bit in (1, 2, 4):
        other = flip_bit(array, "seq", bit)
        is_high = (place & bit) != 0
        array = jnp.concatenate(
            [jnp.where(is_high, other, array), jnp.where(is_high, array, other)], axis=0
        )
    return array


def per_device(
    hidden, b_proj, c_proj, dt_raw, base_ids, complement,
    a_log, d_skip, dt_bias, base_shift, conv_w, conv_b, grad_out,
):
    place = lax.axis_index("seq")
    group, run = place % GROUP, place // GROUP
    here_z, here_y = group[None].astype(jnp.int32), run[None].astype(jnp.int32)
    before = beside(hidden[0, -8:], 1)
    after = beside(hidden[0, :8], -1)
    taps = jnp.concatenate([conv_w, conv_b[None]], axis=0).reshape(5, GROUP, CH)
    taps = lax.dynamic_index_in_dim(taps, group, 1, keepdims=False)
    cw = jnp.broadcast_to(taps[:, :, None], (5, CH, LANES))
    per_head = jnp.stack([-jnp.exp(a_log), d_skip], axis=0)
    tables = jnp.concatenate([dt_bias[None], base_shift], axis=0)
    tables = jnp.concatenate([per_head, tables], axis=0).reshape(15, GROUP, HEADS)
    tables = lax.dynamic_index_in_dim(tables, group, 1, keepdims=False)
    tables = jnp.pad(tables, ((0, 0), (0, 8 - HEADS)))
    rate = jnp.broadcast_to(tables[0][:, None], (8, LANES))
    skip = jnp.broadcast_to(tables[1][:, None], (8, LANES))
    shift_table = jnp.pad(tables[2:].T, ((0, 0), (2, LANES - 15)))

    cut = SETS[0][1] * WIDTH
    taps = (cw[:, :cut], cw[:, cut:])

    packed = pack(
        complement, hidden[0], grad_out[0], b_proj[0], c_proj[0], dt_raw[0], base_ids, before, after
    )
    pk = [exchange(part) for part in packed]
    *saved_0, rows, up_0, down_0 = phase_one(0, pk[0], pk[0], taps[0], (shift_table, rate))
    ends_0 = cross_y(up_0, down_0, run)
    *saved_1, up_1, down_1 = phase_one(1, pk[0], pk[1], taps[1], (rows,))
    ends_1 = cross_y(up_1, down_1, run)
    rows_0, wide, edges, conv_0, head_0 = phase_two(
        0, here_y, pk[0], pk[0], taps[0], rate, skip, saved_0, rows, ends_0, ()
    )
    rows_0 = exchange(rows_0)
    rows_1, wide, edges, conv_1, head_1 = phase_two(
        1, here_y, pk[0], pk[1], taps[1], rate, skip, saved_1, rows, ends_1, (wide, edges)
    )
    rows_1 = exchange(rows_1)
    from_next = along_y(edges[2], -1)
    from_prev = along_y(edges[3], 1)
    wide = wide.at[0, EDGE:].set(edges[0] + from_prev)
    wide = wide.at[GROUP - 1, EDGE:].set(edges[1] + from_next)
    wide = exchange(wide)
    sums = total_over_all(jnp.concatenate([conv_0, conv_1, head_0 + head_1], axis=1))
    layer_out, d_hidden, d_b, d_c, d_dt = unpack(here_z, rows_0, rows_1, wide)

    conv_all = sums[:, :5, :CH].transpose(1, 0, 2).reshape(5, GROUP * CH)
    head_all = sums[:, :HEADS, CH : CH + 15].reshape(GROUP * HEADS, 15)
    return (
        layer_out[None], d_hidden[None], d_b[None], d_c[None], d_dt[None],
        head_all[:, 0], head_all[:, 1], head_all[:, 2], head_all[:, 3:].T,
        conv_all[:4], conv_all[4],
    )


def solution(mesh):
    rows = P("dp", "seq", None)
    placed = (rows, rows, rows, rows, P("dp", "seq"), P(), P(), P(), P(), P(), P(), P(), rows)
    return jax.shard_map(
        per_device,
        mesh=mesh,
        in_specs=placed,
        out_specs=(rows,) * 5 + (P(),) * 6,
        check_vma=False,
    )
```

```python
import functools

import jax
import jax.numpy as jnp
from jax import lax
from jax.experimental import pallas as pl
from jax.experimental.pallas import tpu as pltpu
from jax.sharding import PartitionSpec as P

bf16 = jnp.bfloat16
f32 = jnp.float32

GROUP = 8
ROWS = 4
LANES = 128
HEADS = 5
WIDTH = 64
CH = HEADS * WIDTH
SETS = ((0, 2), (2, 5))
SHARED = 2 * SETS[0][1] * WIDTH
TAIL = SHARED + 2 * LANES
PACK = TAIL + 64
EDGE = 2 * LANES + 8
PARAMS = EDGE + 24
WIDE = PARAMS + 32
UNROLL = 2
VMEM = 58 * 1024 * 1024

Z_GROUPS = [[y * GROUP + z for z in range(GROUP)] for y in range(ROWS)]

NN = (((1,), (0,)), ((), ()))
NT = (((1,), (1,)), ((), ()))
TN = (((0,), (0,)), ((), ()))


def dot(a, b, dims):
    return lax.dot_general(a, b, dims, preferred_element_type=f32)


def split2(a):
    hi = a.astype(bf16)
    return hi, (a - hi.astype(f32)).astype(bf16)


def split3(a):
    hi = a.astype(bf16)
    rest = a - hi.astype(f32)
    mid = rest.astype(bf16)
    return hi, mid, (rest - mid.astype(f32)).astype(bf16)


def exact_dot(a, table, dims):
    count = a.shape[0]
    hi = a.astype(bf16).astype(f32)
    rest = a - hi
    mid = rest.astype(bf16).astype(f32)
    out = dot(jnp.concatenate([hi, mid, rest - mid], axis=0).astype(bf16), table, dims)
    return out[:count] + out[count : 2 * count] + out[2 * count :]


def iota(shape, axis):
    return lax.broadcasted_iota(jnp.int32, shape, axis)


def zero_one(condition):
    return jnp.where(condition, 1.0, 0.0).astype(bf16)


def square_masks():
    row, col = iota((LANES, LANES), 0), iota((LANES, LANES), 1)
    return row, col


def set_row(channel, order):
    for which, (first, last) in enumerate(SETS):
        if channel < last * WIDTH:
            return which, channel - first * WIDTH + order * (last - first) * WIDTH


def pack_kernel(comp_ref, hid_ref, grad_ref, b_ref, c_ref, dt_ref, ids_ref, *outs):
    out_1 = outs[0]
    row, col = square_masks()
    eye = zero_one(row == col)
    for source, order in ((hid_ref, 0), (grad_ref, 1)):
        for block in range(GROUP * CH // LANES):
            piece = source[:, block * LANES : (block + 1) * LANES]
            flipped = dot(eye, piece, NT).astype(bf16)
            for half in range(2):
                channel = block * LANES + half * WIDTH
                target, at = channel // CH, channel % CH
                which, at = set_row(at, order)
                outs[which][target, at : at + WIDTH, :] = flipped[half * WIDTH : (half + 1) * WIDTH]
    pick_row, pick_col = iota((GROUP * 8, 40), 0), iota((GROUP * 8, 40), 1)
    pick = zero_one(
        ((pick_row % 8) < HEADS) & ((pick_row // 8) * HEADS + (pick_row % 8) == pick_col)
    )
    parts = [dot(pick, part, NN) for part in split3(dt_ref[...])]
    ids = ids_ref[...]
    partner = jnp.zeros_like(ids)
    for code in range(12):
        partner = jnp.where(ids == code, comp_ref[code], partner)
    both = jnp.concatenate([ids, partner, jnp.zeros((6, LANES), jnp.int32)], axis=0).astype(f32)
    b_rows, c_rows = b_ref[...], c_ref[...]
    for target in range(GROUP):
        out_1[target, SHARED : SHARED + LANES, :] = b_rows
        out_1[target, SHARED + LANES : SHARED + 2 * LANES, :] = c_rows
        tail = jnp.concatenate(
            [part[target * 8 : target * 8 + 8] for part in parts] + [both], axis=0
        )
        out_1[target, TAIL : TAIL + 32, :] = tail.astype(bf16)


def rows_beside_kernel(before_ref, after_ref, _, out, lines, sem):
    beside = jnp.where(
        iota((8, GROUP * CH), 0) >= 5, before_ref[...].astype(f32), after_ref[...].astype(f32)
    )
    for target in range(GROUP):
        mine = beside[:, target * CH : (target + 1) * CH]
        mine = jnp.concatenate([mine, jnp.zeros((8, 4 * LANES - CH), f32)], axis=1)
        lines[target] = jnp.concatenate(
            [mine[:, j * LANES : (j + 1) * LANES] for j in range(4)], axis=0
        ).astype(bf16)
    copy = pltpu.make_async_copy(lines, out.at[:, TAIL + 32 : PACK, :], sem)
    copy.start()
    copy.wait()


WHOLE = pl.BlockSpec(memory_space=pltpu.VMEM)


def pack(complement, hidden, grad, b_rows, c_rows, dt_rows, ids):
    rows = [PACK] + [2 * (last - first) * WIDTH for first, last in SETS[1:]]
    return pl.pallas_call(
        pack_kernel,
        name="pack",
        out_shape=[jax.ShapeDtypeStruct((GROUP, count, LANES), bf16) for count in rows],
        in_specs=[pl.BlockSpec(memory_space=pltpu.SMEM)] + [WHOLE] * 6,
        out_specs=[WHOLE] * len(SETS),
        compiler_params=pltpu.CompilerParams(vmem_limit_bytes=VMEM),
    )(complement, hidden, grad, b_rows, c_rows, dt_rows, ids)


def add_rows_beside(before, after, packed):
    anywhere = pl.BlockSpec(memory_space=pl.ANY)
    return pl.pallas_call(
        rows_beside_kernel,
        name="rows_beside",
        out_shape=jax.ShapeDtypeStruct(packed.shape, bf16),
        in_specs=[WHOLE, WHOLE, anywhere],
        out_specs=anywhere,
        scratch_shapes=[
            pltpu.VMEM((GROUP, PACK - TAIL - 32, LANES), bf16),
            pltpu.SemaphoreType.DMA,
        ],
        input_output_aliases={2: 0},
        compiler_params=pltpu.CompilerParams(vmem_limit_bytes=VMEM),
    )(before, after, packed)


def cost(heads):
    return pl.CostEstimate(flops=heads * 4_000_000_000, bytes_accessed=8_000_000, transcendentals=0)


def kept(shape):
    return pl.BlockSpec(shape, lambda k: (0,) * len(shape))


def chunked(shape):
    return pl.BlockSpec((UNROLL,) + shape, lambda k: (k, 0, 0))


(R_STEP_F, R_STEP_R, R_CUM_F, R_CUM_R, R_SIG_F, R_SIG_R, R_TOT_F, R_TOT_R,
 R_PRE_F, R_POST_F, R_PRE_R, R_POST_R) = range(12)


def code_tables(tail):
    code = iota((LANES, LANES), 0)
    tables = []
    for line in (24, 25):
        ids = (tail[line : line + 1] + 3.0).astype(jnp.int32)
        tables.append(zero_one((code == ids) | (code == 2)))
    return tables


def rows_at(slot):
    return slice(slot * 8, slot * 8 + 8)


def heads_at(head, offset=0):
    return slice(offset + head * WIDTH, offset + (head + 1) * WIDTH)


def beside_chunk(pk1, which, place, block):
    tail = pk1[which, TAIL:PACK, :].astype(f32)
    lines = tail[32 + 8 * block : 40 + 8 * block]
    lines = jnp.concatenate([lines, jnp.zeros((8, LANES), f32)], axis=0).astype(bf16)
    return dot(lines, place, TN).astype(bf16)


def fill_edges(ext, pk1, first):
    token, place = iota((16, LANES), 0), iota((16, LANES), 1)
    before = zero_one((token >= 5) & (token < 8) & (place == token + LANES - 8))
    after = zero_one((token < 3) & (place == token))
    count = ext.shape[1]
    for start in range(0, count, LANES):
        size = min(LANES, count - start)
        block = (first * WIDTH + start) // LANES
        ext[0, start : start + size, :] = beside_chunk(pk1, 0, before, block)[:size]
        ext[GROUP + 1, start : start + size, :] = beside_chunk(pk1, GROUP - 1, after, block)[:size]


def phase_one_kernel(first, heads, *refs):
    if first == 0:
        pk1, cw, shift_table, rate = refs[:4]
        pk, refs = pk1, refs[4:]
        rows = refs[8]
        x_f, x_r, slope_f, slope_r, u_f, u_r, v_f, v_r = refs[:8]
        refs = refs[9:]
    else:
        pk1, pk, cw, rows = refs[:4]
        x_f, x_r, slope_f, slope_r, u_f, u_r, v_f, v_r = refs[4:12]
        refs = refs[12:]
    ends_up, ends_down, ext, left_x, left_g, run = refs
    width = heads * WIDTH
    pair = pl.program_id(0)
    lane = iota((WIDTH, LANES), 1)

    @pl.when(pair == 0)
    def _():
        fill_edges(ext, pk1, first)
        for chunk in range(GROUP):
            ext[chunk + 1] = pk[chunk, :width, :]
        if first == 0:
            row, col = square_masks()
            upper = zero_one(row <= col)
            lower = zero_one(row >= col)
            ones = jnp.ones((LANES, LANES), bf16)
            logs = [[], []]
            for chunk in range(GROUP):
                tail = pk1[chunk, TAIL:PACK, :].astype(f32)
                dt = tail[0:8] + tail[8:16] + tail[16:24]
                for index, table in enumerate(code_tables(tail)):
                    arg = dt + exact_dot(shift_table[...], table, NN)
                    decay = jnp.exp(-jnp.abs(arg))
                    step = jnp.maximum(arg, 0.0) + jnp.log1p(decay)
                    logs[index].append(rate[...] * step)
                    rows[chunk, rows_at(R_STEP_F + index), :] = step
                    rows[chunk, rows_at(R_SIG_F + index), :] = (
                        jnp.where(arg >= 0, 1.0, decay) / (1.0 + decay)
                    )
            totals = exact_dot(jnp.concatenate(logs[0] + logs[1], axis=0), ones, NN)
            for index in range(2):
                sums = exact_dot(jnp.concatenate(logs[index], axis=0), (upper, lower)[index], NN)
                pre = jnp.zeros((8, LANES), f32)
                post = jnp.zeros((8, LANES), f32)
                offset = index * GROUP * 8
                for chunk in range(GROUP):
                    rows[chunk, rows_at(R_CUM_F + index), :] = sums[chunk * 8 : chunk * 8 + 8]
                    total = totals[offset + chunk * 8 : offset + chunk * 8 + 8]
                    rows[chunk, rows_at(R_TOT_F + index), :] = total
                    rows[chunk, rows_at((R_PRE_F, R_PRE_R)[index]), :] = jnp.exp(pre)
                    pre = pre + total
                for chunk in reversed(range(GROUP)):
                    rows[chunk, rows_at((R_POST_F, R_POST_R)[index]), :] = jnp.exp(post)
                    post = post + totals[offset + chunk * 8 : offset + chunk * 8 + 8]

    for sub in range(UNROLL):
        k = pair * UNROLL + sub
        cums = (rows[k, rows_at(R_CUM_F), :], rows[k, rows_at(R_CUM_R), :])
        growth = [jnp.exp(c) for c in cums]
        tails = [
            jnp.exp(rows[k, rows_at(R_TOT_F + i), :] - cums[i]) * rows[k, rows_at(R_STEP_F + i), :]
            for i in range(2)
        ]
        for head in range(heads):
            at = heads_at(head)
            one = slice(first + head, first + head + 1)
            cur = ext[k + 1, at, :].astype(f32)
            prv = ext[k, at, :].astype(f32)
            nxt = ext[k + 2, at, :].astype(f32)
            base = cw[4, at, :] + cw[0, at, :] * cur
            pre_f, pre_r = base, base
            for tap in range(1, 4):
                weight = cw[tap, at, :]
                pre_f += weight * pltpu.roll(jnp.where(lane < LANES - tap, cur, prv), tap, 1)
                pre_r += weight * pltpu.roll(jnp.where(lane >= tap, cur, nxt), LANES - tap, 1)
            grads = pk[k, width + head * WIDTH : width + (head + 1) * WIDTH, :].astype(f32)
            for index, (pre_act, x_ref, slope_ref) in enumerate(
                ((pre_f, x_f, slope_f), (pre_r, x_r, slope_r))
            ):
                gate = 1.0 / (1.0 + jnp.exp(-pre_act))
                x = pre_act * gate
                x_ref[sub, at, :] = x
                slope_ref[sub, at, :] = gate + x * (1.0 - gate)
                hi, lo = split2(x * tails[index][one])
                out_at = heads_at(head, index * width)
                left_x[sub, out_at, :LANES] = hi
                left_x[sub, out_at, LANES:] = lo
                hi, lo = split2(grads * growth[index][one])
                left_g[sub, out_at, :LANES] = hi
                left_g[sub, out_at, LANES:] = lo
        b_rows = pk1[k, SHARED : SHARED + LANES, :]
        c_rows = pk1[k, SHARED + LANES : SHARED + 2 * LANES, :]
        states = dot(left_x[sub], jnp.concatenate([b_rows, b_rows], axis=0), NN)
        u_f[k] = states[:width]
        u_r[k] = states[width:]
        pulls = dot(left_g[sub], jnp.concatenate([c_rows, c_rows], axis=0), NN)
        v_f[k] = pulls[:width]
        v_r[k] = pulls[width:]

    @pl.when(pair == GROUP // UNROLL - 1)
    def _():
        run[...] = jnp.zeros_like(run)

        def scan(step, _):
            up, down = step, GROUP - 1 - step
            moves = (
                (u_f, up, R_TOT_F), (v_r, up, R_TOT_R), (u_r, down, R_TOT_R), (v_f, down, R_TOT_F)
            )
            for slot, (ref, at_chunk, total) in enumerate(moves):
                factor = jnp.exp(rows[at_chunk, rows_at(total), :])
                for head in range(heads):
                    at = heads_at(head)
                    held = run[slot, at, :]
                    own = ref[at_chunk, at, :]
                    ref[at_chunk, at, :] = held
                    run[slot, at, :] = factor[first + head : first + head + 1] * held + own
            return 0

        lax.fori_loop(0, GROUP, scan, 0)
        whole = [
            rows[GROUP - 1, rows_at(pre), :] * jnp.exp(rows[GROUP - 1, rows_at(total), :])
            for pre, total in ((R_PRE_F, R_TOT_F), (R_PRE_R, R_TOT_R))
        ]
        for ends, pair in ((ends_up, (0, 1)), (ends_down, (2, 3))):
            ends[0:width, :] = run[pair[0]]
            ends[width : 2 * width, :] = run[pair[1]]
            ends[2 * width : 2 * width + 8, :] = whole[0]
            ends[2 * width + 8 : 2 * width + 16, :] = whole[1]


def phase_one(which, pk1, pk, cw, extra):
    first, last = SETS[which]
    heads = last - first
    width = heads * WIDTH
    block = jax.ShapeDtypeStruct((GROUP, width, LANES), f32)
    rows = jax.ShapeDtypeStruct((GROUP, 96, LANES), f32)
    ends = jax.ShapeDtypeStruct((2 * width + 16, LANES), f32)
    outs = [block] * 8 + ([rows] if which == 0 else []) + [ends, ends]
    specs = [chunked((width, LANES))] * 4 + [kept(out.shape) for out in outs[4:]]
    operands = [pk1, cw, *extra] if which == 0 else [pk1, pk, cw, *extra]
    return pl.pallas_call(
        functools.partial(phase_one_kernel, first, heads),
        name=f"phase_one_{which}",
        grid=(GROUP // UNROLL,),
        out_shape=outs,
        in_specs=[kept(operand.shape) for operand in operands],
        out_specs=specs,
        scratch_shapes=[
            pltpu.VMEM((GROUP + 2, width, LANES), bf16),
            pltpu.VMEM((UNROLL, 2 * width, 2 * LANES), bf16),
            pltpu.VMEM((UNROLL, 2 * width, 2 * LANES), bf16),
            pltpu.VMEM((4, width, LANES), f32),
        ],
        cost_estimate=cost(heads),
        compiler_params=pltpu.CompilerParams(vmem_limit_bytes=VMEM),
    )(*operands)


def phase_two_kernel(first, heads, *refs):
    (
        place_y, pk1, pk, cw, rate, skip,
        x_f, x_r, slope_f, slope_r, u_f, u_r, v_f, v_r, rows, *ends,
    ) = refs[:18]
    refs = refs[18:]
    if first:
        wide_in, edges_in, params_in = refs[:3]
        refs = refs[3:]
    (
        rows_out, wide, edges, params,
        ext, entry, d_pre_f, d_pre_r, acc, lines, *of_chunk,
    ) = refs
    width = heads * WIDTH
    pair = pl.program_id(0)
    row, col = square_masks()
    is_low = row >= col
    is_up = row <= col
    low_one, up_one = zero_one(is_low), zero_one(is_up)
    ones = jnp.ones((LANES, LANES), bf16)
    lane = iota((WIDTH, LANES), 1)

    def held(sub, start, stop):
        return wide_in[sub, start:stop, :] if first else 0.0

    @pl.when(pair == 0)
    def _():
        fill_edges(ext, pk1, first)
        entry[...] = jnp.zeros_like(entry)
        here = place_y[0]
        for away in (3, 2, 1):
            for shift, slots, reached in (
                (away, ((0, 0, 0), (1, 1, 1)), here >= away),
                (ROWS - away, ((2, 0, 1), (3, 1, 0)), here + away < ROWS),
            ):

                @pl.when(reached)
                def _(came=ends[shift - 1], slots=slots):
                    for slot, part, total in slots:
                        start = 2 * width + total * 8
                        factor = came[start : start + 8, :]
                        for head in range(heads):
                            at = heads_at(head)
                            entry[slot, at, :] = (
                                factor[first + head : first + head + 1] * entry[slot, at, :]
                                + came[heads_at(head, part * width), :]
                            )

        of_chunk[8][...] = jnp.zeros_like(of_chunk[8])
        acc[...] = jnp.zeros_like(acc)
        for ref in (d_pre_f, d_pre_r):
            for edge in (0, 1, GROUP + 2, GROUP + 3):
                ref[edge] = jnp.zeros((width, LANES), f32)

    for sub in range(UNROLL):
        k = pair * UNROLL + sub
        (
            states, d_states, state_bits, d_state_bits, reach, pulled, gd, xt, line, a_hi, a_lo,
        ) = [ref.at[sub] for ref in of_chunk]
        b_rows = pk1[k, SHARED : SHARED + LANES, :]
        c_rows = pk1[k, SHARED + LANES : SHARED + 2 * LANES, :]
        step = [rows[k, rows_at(R_STEP_F + i), :] for i in range(2)]
        cum = [rows[k, rows_at(R_CUM_F + i), :] for i in range(2)]
        growth = [jnp.exp(c) for c in cum]
        total = [rows[k, rows_at(R_TOT_F + i), :] for i in range(2)]
        tail = [jnp.exp(total[i] - cum[i]) for i in range(2)]
        factor = [jnp.exp(total[i]) for i in range(2)]
        columns = jnp.concatenate(
            [cum[0], cum[1], jnp.zeros((LANES - 16, LANES), f32)], axis=0
        ).T
        into = (
            (states, state_bits, 0, u_f, R_PRE_F, 0),
            (states, state_bits, 1, u_r, R_POST_R, 2),
            (d_states, d_state_bits, 0, v_f, R_POST_F, 3),
            (d_states, d_state_bits, 1, v_r, R_PRE_R, 1),
        )
        for full, bits, index, local, decay_row, slot in into:
            decay = rows[k, rows_at(decay_row), :]
            for head in range(heads):
                at, to = heads_at(head), heads_at(head, index * width)
                value = local[sub, at, :] + decay[first + head : first + head + 1] * entry[slot, at, :]
                full[to, :] = value
                hi, lo = split2(value)
                bits[to, :LANES] = hi
                bits[to, LANES:] = lo
        reach[...] = dot(state_bits[...], jnp.concatenate([c_rows, c_rows], axis=1), NT)
        pulled[...] = dot(d_state_bits[...], jnp.concatenate([b_rows, b_rows], axis=1), NT)
        scores = dot(c_rows, b_rows, NT)
        d_g = jnp.zeros((LANES, LANES), f32)
        for head in range(heads):
            at = heads_at(head)
            one = slice(first + head, first + head + 1)
            gap_f = columns[:, first + head : first + head + 1] - cum[0][one]
            gap_r = columns[:, 8 + first + head : 9 + first + head] - cum[1][one]
            spread = jnp.exp(jnp.where(is_low, gap_f, gap_r))
            hi, lo = split2(scores * spread)
            a_hi[head, :, :LANES] = hi * low_one
            a_hi[head, :, LANES:] = hi * up_one
            a_lo[head, :, :LANES] = lo * low_one
            a_lo[head, :, LANES:] = lo * up_one
            grad_bits = pk[k, width + head * WIDTH : width + (head + 1) * WIDTH, :]
            grads = grad_bits.astype(f32)
            xs, bits = [], []
            for index, x_ref in enumerate((x_f, x_r)):
                scaled = x_ref[sub, at, :] * step[index][one]
                xs.append(scaled)
                bits.append(split2(scaled))
            d_a = dot(
                jnp.concatenate([grad_bits, grad_bits], axis=0),
                jnp.concatenate(
                    [
                        jnp.concatenate([bits[0][0], bits[1][0]], axis=1),
                        jnp.concatenate([bits[0][1], bits[1][1]], axis=1),
                    ],
                    axis=0,
                ),
                TN,
            )
            d_g += spread * (
                jnp.where(is_low, d_a[:, :LANES], 0.0) + jnp.where(is_up, d_a[:, LANES:], 0.0)
            )
            d_xs = dot(grad_bits, a_hi[head], NN) + dot(grad_bits, a_lo[head], NN)
            out = jnp.zeros((WIDTH, LANES), f32)
            d_skip_line = jnp.zeros((WIDTH, LANES), f32)
            for index, (x_ref, slope_ref, d_pre) in enumerate(
                ((x_f, slope_f, d_pre_f), (x_r, slope_r, d_pre_r))
            ):
                to = heads_at(head, index * width)
                half = slice(index * LANES, (index + 1) * LANES)
                hi, lo = bits[index]
                y = (
                    dot(hi, a_hi[head, :, half], NT)
                    + dot(lo, a_hi[head, :, half], NT)
                    + dot(hi, a_lo[head, :, half], NT)
                    + growth[index][one] * reach[to, :]
                )
                x = x_ref[sub, at, :]
                out += y + skip[one, :] * x
                d_skip_line += grads * x
                from_state = tail[index][one] * pulled[to, :]
                d_x = d_xs[:, half] + from_state
                d_pre[k + 2, at, :] = (step[index][one] * d_x + skip[one, :] * grads) * slope_ref[
                    sub, at, :
                ]
                own = jnp.sum(x * d_x, axis=0, keepdims=True)
                line[index, one, :] = (
                    jnp.sum(grads * y, axis=0, keepdims=True) - step[index][one] * own
                )
                line[2 + index, one, :] = jnp.sum(
                    xs[index] * from_state
                    + factor[index][one] * (d_states[to, :] * states[to, :]),
                    axis=0,
                    keepdims=True,
                )
                line[4 + index, one, :] = own
                hi, lo = split2(grads * growth[index][one])
                gd[to, :LANES] = hi
                gd[to, LANES:] = lo
                hi, lo = split2(xs[index] * tail[index][one])
                xt[to, :LANES] = hi
                xt[to, LANES:] = lo
            rows_out[k, at, :] = out.astype(bf16)
            line[6, one, :] = jnp.sum(d_skip_line, axis=0, keepdims=True)
        g_hi, g_lo = split2(d_g)
        wide_c = dot(gd[:, :LANES], state_bits[...], TN)
        wide[k, LANES : 2 * LANES, :] = held(sub, LANES, 2 * LANES) + (
            dot(g_hi, b_rows, NN)
            + dot(g_lo, b_rows, NN)
            + wide_c[:, :LANES]
            + wide_c[:, LANES:]
            + dot(gd[:, LANES:], state_bits[:, :LANES], TN)
        )
        wide_b = dot(xt[:, :LANES], d_state_bits[...], TN)
        wide[k, :LANES, :] = held(sub, 0, LANES) + (
            dot(g_hi, c_rows, TN)
            + dot(g_lo, c_rows, TN)
            + wide_b[:, :LANES]
            + wide_b[:, LANES:]
            + dot(xt[:, LANES:], d_state_bits[:, :LANES], TN)
        )
        wide[k, 2 * LANES : EDGE, :] = jnp.zeros((8, LANES), f32) + held(sub, 2 * LANES, EDGE)
        lines[:, pl.ds(pl.multiple_of(k * 8, 8), 8), :] = line[...]

    @pl.when(pair == GROUP // UNROLL - 1)
    def _():
        edges[...] = edges_in[...] if first else jnp.zeros_like(edges)
        token, place = iota((8, LANES), 0), iota((8, LANES), 1)
        first_rows = zero_one((token < 3) & (place == token))
        last_rows = zero_one((token >= 5) & (place == token + LANES - 8))

        def lines_of(marker, tile):
            hi, mid, lo = split3(tile)
            return dot(marker, hi, NT) + dot(marker, mid, NT) + dot(marker, lo, NT)

        def put_edge(slot, marker):
            def put(head, total):
                channel = (first + head) * WIDTH
                block, offset = channel // LANES, channel % LANES
                edges[slot, block * 8 : block * 8 + 8, offset : offset + WIDTH] = lines_of(
                    marker, total
                )
            return put

        def taps_of(tile, hid, puts):
            for head in range(heads):
                at = heads_at(head)
                hid_here = hid[at, :].astype(f32)
                own_f, own_r = d_pre_f[tile + 1, at, :], d_pre_r[tile + 1, at, :]
                later_f, earlier_r = d_pre_f[tile + 2, at, :], d_pre_r[tile, at, :]
                both = own_f + own_r
                acc[4, at, :] += both
                acc[0, at, :] += hid_here * both
                total = cw[0, at, :] * both
                for tap in range(1, 4):
                    shifted = pltpu.roll(
                        jnp.where(lane >= tap, own_f, later_f), LANES - tap, 1
                    ) + pltpu.roll(jnp.where(lane < LANES - tap, own_r, earlier_r), tap, 1)
                    acc[tap, at, :] += hid_here * shifted
                    total += cw[tap, at, :] * shifted
                for put in puts:
                    put(head, total)

        def keep_chunk(chunk):
            def put(head, total):
                rows_out[chunk, heads_at(head, width), :] = total.astype(bf16)
            return put

        taps_of(0, ext[0], [put_edge(2, last_rows)])
        taps_of(GROUP + 1, ext[GROUP + 1], [put_edge(3, first_rows)])
        taps_of(1, pk[0], [keep_chunk(0), put_edge(0, first_rows)])
        taps_of(GROUP, pk[GROUP - 1], [keep_chunk(GROUP - 1), put_edge(1, last_rows)])

        def inner(chunk, _):
            taps_of(chunk + 1, pk.at[chunk], [keep_chunk(chunk)])
            return 0

        lax.fori_loop(1, GROUP - 1, inner, 0)
        sums = jnp.zeros((8, width), f32)
        for tap in range(5):
            sums += lines_of(zero_one(token == tap), acc[tap])
        params[...] = params_in[...] if first else jnp.zeros_like(params)
        for start in range(0, width, LANES):
            size = min(LANES, width - start)
            block = (first * WIDTH + start) // LANES
            params[block * 8 : block * 8 + 8, :size] = sums[:, start : start + size]
        def all_rows(slot):
            return jnp.concatenate([rows[c, rows_at(slot), :] for c in range(GROUP)], axis=0)

        def over_chunks(value):
            total = value[0:8]
            for c in range(1, GROUP):
                total = total + value[c * 8 : c * 8 + 8]
            return total

        rates = jnp.concatenate([rate[...]] * GROUP, axis=0)
        tails_here = exact_dot(jnp.concatenate([lines[2], lines[3]], axis=0), ones, NN)
        d_args, d_rate = [], jnp.zeros((GROUP * 8, LANES), f32)
        for index in range(2):
            offset = index * GROUP * 8
            d_log = exact_dot(lines[index], (low_one, up_one)[index], NN) + tails_here[
                offset : offset + GROUP * 8
            ]
            d_args.append((lines[4 + index] + rates * d_log) * all_rows(R_SIG_F + index))
            d_rate += d_log * rates * all_rows(R_STEP_F + index)
        by_code = jnp.zeros((8, LANES), f32)
        for c in range(GROUP):
            own = slice(c * 8, c * 8 + 8)
            wide[c, 2 * LANES : EDGE, :] += d_args[0][own] + d_args[1][own]
            for index, table in enumerate(code_tables(pk1[c, TAIL:PACK, :].astype(f32))):
                by_code += exact_dot(d_args[index][own], table, NT)
        params[24:32, :] += (
            exact_dot(over_chunks(d_rate), zero_one(col == 0), NN)
            + exact_dot(over_chunks(lines[6]), zero_one(col == 1), NN)
            + by_code
        )


def phase_two(which, place_y, pk1, pk, cw, rate, skip, saved, rows, ends, carried):
    first, last = SETS[which]
    heads = last - first
    width = heads * WIDTH
    outs = [
        jax.ShapeDtypeStruct((GROUP, 2 * width, LANES), bf16),
        jax.ShapeDtypeStruct((GROUP, WIDE, LANES), f32),
        jax.ShapeDtypeStruct((4, 24, LANES), f32),
        jax.ShapeDtypeStruct((32, LANES), f32),
    ]
    whole = [pk1, pk, cw, rate, skip]
    in_specs = (
        [pl.BlockSpec(memory_space=pltpu.SMEM)]
        + [kept(operand.shape) for operand in whole]
        + [chunked((width, LANES))] * 8
        + [kept(rows.shape)] + [kept(end.shape) for end in ends]
    )
    if which:
        in_specs += [chunked((WIDE, LANES)), kept((4, 24, LANES)), kept((32, LANES))]
    return pl.pallas_call(
        functools.partial(phase_two_kernel, first, heads),
        name=f"phase_two_{which}",
        grid=(GROUP // UNROLL,),
        out_shape=outs,
        in_specs=in_specs,
        out_specs=[kept(out.shape) for out in outs],
        scratch_shapes=[
            pltpu.VMEM((GROUP + 2, width, LANES), bf16),
            pltpu.VMEM((4, width, LANES), f32),
            pltpu.VMEM((GROUP + 4, width, LANES), f32),
            pltpu.VMEM((GROUP + 4, width, LANES), f32),
            pltpu.VMEM((5, width, LANES), f32),
            pltpu.VMEM((7, GROUP * 8, LANES), f32),
            pltpu.VMEM((UNROLL, 2 * width, LANES), f32),
            pltpu.VMEM((UNROLL, 2 * width, LANES), f32),
            pltpu.VMEM((UNROLL, 2 * width, 2 * LANES), bf16),
            pltpu.VMEM((UNROLL, 2 * width, 2 * LANES), bf16),
            pltpu.VMEM((UNROLL, 2 * width, LANES), f32),
            pltpu.VMEM((UNROLL, 2 * width, LANES), f32),
            pltpu.VMEM((UNROLL, 2 * width, 2 * LANES), bf16),
            pltpu.VMEM((UNROLL, 2 * width, 2 * LANES), bf16),
            pltpu.VMEM((UNROLL, 7, 8, LANES), f32),
            pltpu.VMEM((UNROLL, heads, LANES, 2 * LANES), bf16),
            pltpu.VMEM((UNROLL, heads, LANES, 2 * LANES), bf16),
        ],
        cost_estimate=cost(2 * heads),
        compiler_params=pltpu.CompilerParams(vmem_limit_bytes=VMEM),
    )(place_y, *whole, *saved, rows, *ends, *carried)


def finish_kernel(edges, from_prev, from_next, sums, _, out, lines, sem):
    for target in range(GROUP):
        lines[target, :24, :] = jnp.zeros((24, LANES), f32)
        lines[target, 24:, :] = sums[...]
    lines[0, :24, :] = edges[0] + from_prev[...]
    lines[GROUP - 1, :24, :] = edges[1] + from_next[...]
    copy = pltpu.make_async_copy(lines, out.at[:, EDGE:WIDE, :], sem)
    copy.start()
    copy.wait()


def finish(edges, from_prev, from_next, sums, wide):
    anywhere = pl.BlockSpec(memory_space=pl.ANY)
    return pl.pallas_call(
        finish_kernel,
        name="finish",
        out_shape=jax.ShapeDtypeStruct(wide.shape, f32),
        in_specs=[WHOLE] * 4 + [anywhere],
        out_specs=anywhere,
        scratch_shapes=[pltpu.VMEM((GROUP, WIDE - EDGE, LANES), f32), pltpu.SemaphoreType.DMA],
        input_output_aliases={4: 0},
        compiler_params=pltpu.CompilerParams(vmem_limit_bytes=VMEM),
    )(edges, from_prev, from_next, sums, wide)


def unpack_kernel(place_z, *refs):
    sets, wide = refs[: len(SETS)], refs[len(SETS)]
    (
        layer_out, hid_out, b_out, c_out, dt_out, taps_out, bias_out, rate_out, skip_out, shift_out, code_out,
    ) = refs[len(SETS) + 1 :]
    row, col = square_masks()
    eye = zero_one(row == col)
    line = iota((16, LANES), 0)
    at_start = (line < 3) & (place_z[0] == 0)
    at_end = (line >= 13) & (place_z[0] == GROUP - 1)
    blank = jnp.zeros((8, LANES), f32)
    for order, target in enumerate((layer_out, hid_out)):
        for block in range(GROUP * CH // LANES):
            pieces, edge, taps = [], [], []
            for half in range(2):
                channel = block * LANES + half * WIDTH
                group, at = channel // CH, channel % CH
                offset = at % LANES
                start = EDGE + at // LANES * 8
                taps.append(wide[group, start + 24 : start + 32, offset : offset + WIDTH])
                edge.append(wide[group, start : start + 8, offset : offset + WIDTH])
                which, at = set_row(at, order)
                pieces.append(sets[which][group, at : at + WIDTH, :])
            lanes = slice(block * LANES, (block + 1) * LANES)
            flipped = dot(eye, jnp.concatenate(pieces, axis=0), NT)
            if order:
                taps = jnp.concatenate(taps, axis=1)
                taps_out[:, lanes] = taps[:4]
                bias_out[:, lanes] = taps[4:5]
                edge = jnp.concatenate(edge, axis=1)
                head = jnp.where(at_start, jnp.concatenate([edge, blank], axis=0), flipped[:16])
                tail = jnp.where(
                    at_end, jnp.concatenate([blank, edge], axis=0), flipped[LANES - 16 :]
                )
                flipped = jnp.concatenate([head, flipped[16 : LANES - 16], tail], axis=0)
            target[:, lanes] = flipped.astype(bf16)
    for base, target in ((0, b_out), (LANES, c_out)):
        total = wide[0, base : base + LANES, :]
        for group in range(1, GROUP):
            total += wide[group, base : base + LANES, :]
        target[...] = total
    lines = jnp.concatenate(
        [wide[group, 2 * LANES : EDGE, :] for group in range(GROUP)], axis=0
    )
    pick_row, pick_col = iota((40, GROUP * 8), 0), iota((40, GROUP * 8), 1)
    pick = zero_one(
        ((pick_col % 8) < HEADS) & ((pick_col // 8) * HEADS + (pick_col % 8) == pick_row)
    )
    hi, mid, lo = split3(lines)
    dt_out[...] = dot(pick, hi, NN) + dot(pick, mid, NN) + dot(pick, lo, NN)
    heads = jnp.concatenate([wide[group, WIDE - 8 : WIDE, :] for group in range(GROUP)], axis=0)
    by_head = sum(
        lax.dot_general(part, pick, (((0,), (1,)), ((), ())), preferred_element_type=f32)
        for part in split3(heads)
    )
    rate_out[...] = by_head[0:1]
    skip_out[...] = by_head[1:2]
    shift_out[...] = by_head[2:3]
    code_out[...] = by_head[3:15]


def unpack(place_z, sets, wide):
    rows = jax.ShapeDtypeStruct((LANES, GROUP * CH), bf16)
    square = jax.ShapeDtypeStruct((LANES, LANES), f32)
    return pl.pallas_call(
        unpack_kernel,
        name="unpack",
        out_shape=[rows, rows, square, square, jax.ShapeDtypeStruct((40, LANES), f32)]
        + [
            jax.ShapeDtypeStruct(shape, f32)
            for shape in ((4, GROUP * CH), (1, GROUP * CH), (1, 40), (1, 40), (1, 40), (12, 40))
        ],
        in_specs=[pl.BlockSpec(memory_space=pltpu.SMEM)] + [WHOLE] * (len(SETS) + 1),
        out_specs=[WHOLE] * 11,
        compiler_params=pltpu.CompilerParams(vmem_limit_bytes=VMEM),
    )(place_z, *sets, wide)


def exchange(array):
    return lax.all_to_all(array, "seq", 0, 0, axis_index_groups=Z_GROUPS)


def along_y(array, by):
    pairs = [
        (y * GROUP + z, (y + by) * GROUP + z)
        for y in range(ROWS)
        for z in range(GROUP)
        if 0 <= y + by < ROWS
    ]
    return lax.ppermute(array, "seq", pairs)


def beside(array, by):
    count = lax.axis_size("seq")
    return lax.ppermute(array, "seq", [(i, i + by) for i in range(count) if 0 <= i + by < count])


def cross_y(up, down, run):
    came = []
    for shift in range(1, ROWS):
        pairs = [
            (y * GROUP + z, (y + shift) % ROWS * GROUP + z) for y in range(ROWS) for z in range(GROUP)
        ]
        came.append(lax.ppermute(jnp.where(run + shift < ROWS, up, down), "seq", pairs))
    return came


def flip_bit(array, axis, bit):
    count = lax.axis_size(axis)
    return lax.ppermute(array, axis, [(i, i ^ bit) for i in range(count)])


def total_over_runs(array):
    for axis, bit in (("dp", 1), ("dp", 2), ("dp", 4), ("seq", 8), ("seq", 16)):
        array = array + flip_bit(array, axis, bit)
    return array


def per_device(
    hidden, b_proj, c_proj, dt_raw, base_ids, complement,
    a_log, d_skip, dt_bias, base_shift, conv_w, conv_b, grad_out,
):
    place = lax.axis_index("seq")
    group, run = place % GROUP, place // GROUP
    here_z, here_y = group[None].astype(jnp.int32), run[None].astype(jnp.int32)
    before = beside(hidden[0, -8:], 1)
    after = beside(hidden[0, :8], -1)
    taps = jnp.concatenate([conv_w, conv_b[None]], axis=0).reshape(5, GROUP, CH)
    taps = lax.dynamic_index_in_dim(taps, group, 1, keepdims=False)
    cw = jnp.broadcast_to(taps[:, :, None], (5, CH, LANES))
    per_head = jnp.stack([-jnp.exp(a_log), d_skip], axis=0)
    tables = jnp.concatenate([dt_bias[None], base_shift], axis=0)
    tables = jnp.concatenate([per_head, tables], axis=0).reshape(15, GROUP, HEADS)
    tables = lax.dynamic_index_in_dim(tables, group, 1, keepdims=False)
    tables = jnp.pad(tables, ((0, 0), (0, 8 - HEADS)))
    rate = jnp.broadcast_to(tables[0][:, None], (8, LANES))
    skip = jnp.broadcast_to(tables[1][:, None], (8, LANES))
    shift_table = jnp.pad(tables[2:].T, ((0, 0), (2, LANES - 15)))

    taps = [cw[:, first * WIDTH : last * WIDTH] for first, last in SETS]

    packed = pack(
        complement, hidden[0], grad_out[0], b_proj[0], c_proj[0], dt_raw[0].T, base_ids
    )
    packed = [add_rows_beside(before, after, packed[0]), *packed[1:]]
    pk = [exchange(part) for part in packed]
    saved, ends, sets, carried = [], [], [], ()
    for which, tap in enumerate(taps):
        *blocks, up, down = phase_one(
            which, pk[0], pk[which], tap, (rows,) if which else (shift_table, rate)
        )
        if not which:
            rows = blocks.pop()
        saved.append(blocks)
        ends.append(cross_y(up, down, run))
    for which, tap in enumerate(taps):
        out, *carried = phase_two(
            which, here_y, pk[0], pk[which], tap, rate, skip, saved[which], rows, ends[which], carried
        )
        sets.append(exchange(out))
    wide, edges, sums = carried
    from_next = along_y(edges[2], -1)
    from_prev = along_y(edges[3], 1)
    wide = exchange(finish(edges, from_prev, from_next, total_over_runs(sums), wide))
    layer_out, d_hidden, d_b, d_c, d_dt, taps, bias, rates, skips, shifts, codes = unpack(
        here_z, sets, wide
    )
    return (
        layer_out[None], d_hidden[None], d_b[None], d_c[None], d_dt.T[None],
        rates[0], skips[0], shifts[0], codes, taps, bias[0],
    )


def solution(mesh):
    rows = P("dp", "seq", None)
    placed = (rows, rows, rows, rows, P("dp", "seq"), P(), P(), P(), P(), P(), P(), P(), rows)
    return jax.shard_map(
        per_device,
        mesh=mesh,
        in_specs=placed,
        out_specs=(rows,) * 5 + (P(),) * 6,
        check_vma=False,
    )
```

```python
import functools

import jax
import jax.numpy as jnp
from jax import lax
from jax.experimental import pallas as pl
from jax.experimental.pallas import tpu as pltpu
from jax.sharding import PartitionSpec as P

bf16 = jnp.bfloat16
f32 = jnp.float32

GROUP = 8
ROWS = 4
LANES = 128
HEADS = 5
WIDTH = 64
CH = HEADS * WIDTH
SETS = ((0, 2), (2, 5))
SHARED = 2 * SETS[0][1] * WIDTH
TAIL = SHARED + 2 * LANES
PACK = TAIL + 32
SECOND = 2 * (SETS[1][1] - SETS[1][0]) * WIDTH
PACK_2 = SECOND + 16
EDGE = 2 * LANES + 8
PARAMS = EDGE + 24
WIDE = PARAMS + 32
UNROLL = 2
VMEM = 58 * 1024 * 1024

Z_GROUPS = [[y * GROUP + z for z in range(GROUP)] for y in range(ROWS)]

NN = (((1,), (0,)), ((), ()))
NT = (((1,), (1,)), ((), ()))
TN = (((0,), (0,)), ((), ()))


def dot(a, b, dims):
    return lax.dot_general(a, b, dims, preferred_element_type=f32)


def split2(a):
    hi = a.astype(bf16)
    return hi, (a - hi.astype(f32)).astype(bf16)


def split3(a):
    hi = a.astype(bf16)
    rest = a - hi.astype(f32)
    mid = rest.astype(bf16)
    return hi, mid, (rest - mid.astype(f32)).astype(bf16)


def exact_dot(a, table, dims):
    count = a.shape[0]
    hi = a.astype(bf16).astype(f32)
    rest = a - hi
    mid = rest.astype(bf16).astype(f32)
    out = dot(jnp.concatenate([hi, mid, rest - mid], axis=0).astype(bf16), table, dims)
    return out[:count] + out[count : 2 * count] + out[2 * count :]


def iota(shape, axis):
    return lax.broadcasted_iota(jnp.int32, shape, axis)


def zero_one(condition):
    return jnp.where(condition, 1.0, 0.0).astype(bf16)


def square_masks():
    row, col = iota((LANES, LANES), 0), iota((LANES, LANES), 1)
    return row, col


def set_row(channel, order):
    for which, (first, last) in enumerate(SETS):
        if channel < last * WIDTH:
            return which, channel - first * WIDTH + order * (last - first) * WIDTH


def pack_kernel(comp_ref, hid_ref, grad_ref, b_ref, c_ref, dt_ref, ids_ref, *outs):
    out_1 = outs[0]
    row, col = square_masks()
    eye = zero_one(row == col)
    for source, order in ((hid_ref, 0), (grad_ref, 1)):
        for block in range(GROUP * CH // LANES):
            piece = source[:, block * LANES : (block + 1) * LANES]
            flipped = dot(eye, piece, NT).astype(bf16)
            for half in range(2):
                channel = block * LANES + half * WIDTH
                target, at = channel // CH, channel % CH
                which, at = set_row(at, order)
                outs[which][target, at : at + WIDTH, :] = flipped[half * WIDTH : (half + 1) * WIDTH]
    pick_row, pick_col = iota((GROUP * 8, 40), 0), iota((GROUP * 8, 40), 1)
    pick = zero_one(
        ((pick_row % 8) < HEADS) & ((pick_row // 8) * HEADS + (pick_row % 8) == pick_col)
    )
    parts = [dot(pick, part, NN) for part in split3(dt_ref[...])]
    ids = ids_ref[...]
    partner = jnp.zeros_like(ids)
    for code in range(12):
        partner = jnp.where(ids == code, comp_ref[code], partner)
    both = jnp.concatenate([ids, partner, jnp.zeros((6, LANES), jnp.int32)], axis=0).astype(f32)
    b_rows, c_rows = b_ref[...], c_ref[...]
    for target in range(GROUP):
        out_1[target, SHARED : SHARED + LANES, :] = b_rows
        out_1[target, SHARED + LANES : SHARED + 2 * LANES, :] = c_rows
        tail = jnp.concatenate(
            [part[target * 8 : target * 8 + 8] for part in parts] + [both], axis=0
        )
        out_1[target, TAIL:PACK, :] = tail.astype(bf16)


def rows_beside_kernel(before_ref, after_ref, _, out, lines, sem):
    beside = jnp.where(
        iota((8, GROUP * CH), 0) >= 5, before_ref[...].astype(f32), after_ref[...].astype(f32)
    )
    for target in range(GROUP):
        start = target * CH + SETS[1][0] * WIDTH
        mine = beside[:, start : (target + 1) * CH]
        mine = jnp.concatenate([mine, jnp.zeros((8, 2 * LANES - mine.shape[1]), f32)], axis=1)
        lines[target] = jnp.concatenate([mine[:, :LANES], mine[:, LANES:]], axis=0).astype(bf16)
    copy = pltpu.make_async_copy(lines, out.at[:, SECOND:PACK_2, :], sem)
    copy.start()
    copy.wait()


WHOLE = pl.BlockSpec(memory_space=pltpu.VMEM)


def pack(complement, hidden, grad, b_rows, c_rows, dt_rows, ids):
    return pl.pallas_call(
        pack_kernel,
        name="pack",
        out_shape=[jax.ShapeDtypeStruct((GROUP, count, LANES), bf16) for count in (PACK, PACK_2)],
        in_specs=[pl.BlockSpec(memory_space=pltpu.SMEM)] + [WHOLE] * 6,
        out_specs=[WHOLE] * len(SETS),
        compiler_params=pltpu.CompilerParams(vmem_limit_bytes=VMEM),
    )(complement, hidden, grad, b_rows, c_rows, dt_rows, ids)


def add_rows_beside(before, after, packed):
    anywhere = pl.BlockSpec(memory_space=pl.ANY)
    return pl.pallas_call(
        rows_beside_kernel,
        name="rows_beside",
        out_shape=jax.ShapeDtypeStruct(packed.shape, bf16),
        in_specs=[WHOLE, WHOLE, anywhere],
        out_specs=anywhere,
        scratch_shapes=[
            pltpu.VMEM((GROUP, PACK_2 - SECOND, LANES), bf16),
            pltpu.SemaphoreType.DMA,
        ],
        input_output_aliases={2: 0},
        compiler_params=pltpu.CompilerParams(vmem_limit_bytes=VMEM),
    )(before, after, packed)


def cost(heads):
    return pl.CostEstimate(flops=heads * 4_000_000_000, bytes_accessed=8_000_000, transcendentals=0)


def kept(shape):
    return pl.BlockSpec(shape, lambda k: (0,) * len(shape))


def chunked(shape):
    return pl.BlockSpec((UNROLL,) + shape, lambda k: (k, 0, 0))


(R_STEP_F, R_STEP_R, R_CUM_F, R_CUM_R, R_SIG_F, R_SIG_R, R_TOT_F, R_TOT_R,
 R_PRE_F, R_POST_F, R_PRE_R, R_POST_R) = range(12)


def code_tables(tail):
    code = iota((LANES, LANES), 0)
    tables = []
    for line in (24, 25):
        ids = (tail[line : line + 1] + 3.0).astype(jnp.int32)
        tables.append(zero_one((code == ids) | (code == 2)))
    return tables


def rows_at(slot):
    return slice(slot * 8, slot * 8 + 8)


def heads_at(head, offset=0):
    return slice(offset + head * WIDTH, offset + (head + 1) * WIDTH)


def beside_chunk(pk, which, place, block):
    lines = pk[which, SECOND:PACK_2, :].astype(f32)[8 * block : 8 * block + 8]
    lines = jnp.concatenate([lines, jnp.zeros((8, LANES), f32)], axis=0).astype(bf16)
    return dot(lines, place, TN).astype(bf16)


def fill_edges(ext, pk, beside):
    if beside:
        ext[0] = beside[0][...]
        ext[GROUP + 1] = beside[1][...]
        return
    token, place = iota((16, LANES), 0), iota((16, LANES), 1)
    before = zero_one((token >= 5) & (token < 8) & (place == token + LANES - 8))
    after = zero_one((token < 3) & (place == token))
    count = ext.shape[1]
    for start in range(0, count, LANES):
        size = min(LANES, count - start)
        block = start // LANES
        ext[0, start : start + size, :] = beside_chunk(pk, 0, before, block)[:size]
        ext[GROUP + 1, start : start + size, :] = beside_chunk(pk, GROUP - 1, after, block)[:size]


def phase_one_kernel(first, heads, *refs):
    beside = ()
    if first == 0:
        pk1, cw, shift_table, rate, *beside = refs[:6]
        pk, refs = pk1, refs[6:]
        rows = refs[8]
        x_f, x_r, slope_f, slope_r, u_f, u_r, v_f, v_r = refs[:8]
        refs = refs[9:]
    else:
        pk1, pk, cw, rows = refs[:4]
        x_f, x_r, slope_f, slope_r, u_f, u_r, v_f, v_r = refs[4:12]
        refs = refs[12:]
    ends_up, ends_down, ext, left_x, left_g, run = refs
    width = heads * WIDTH
    pair = pl.program_id(0)
    lane = iota((WIDTH, LANES), 1)

    @pl.when(pair == 0)
    def _():
        fill_edges(ext, pk, beside)
        for chunk in range(GROUP):
            ext[chunk + 1] = pk[chunk, :width, :]
        if first == 0:
            row, col = square_masks()
            upper = zero_one(row <= col)
            lower = zero_one(row >= col)
            ones = jnp.ones((LANES, LANES), bf16)
            logs = [[], []]
            for chunk in range(GROUP):
                tail = pk1[chunk, TAIL:PACK, :].astype(f32)
                dt = tail[0:8] + tail[8:16] + tail[16:24]
                for index, table in enumerate(code_tables(tail)):
                    arg = dt + exact_dot(shift_table[...], table, NN)
                    decay = jnp.exp(-jnp.abs(arg))
                    step = jnp.maximum(arg, 0.0) + jnp.log1p(decay)
                    logs[index].append(rate[...] * step)
                    rows[chunk, rows_at(R_STEP_F + index), :] = step
                    rows[chunk, rows_at(R_SIG_F + index), :] = (
                        jnp.where(arg >= 0, 1.0, decay) / (1.0 + decay)
                    )
            totals = exact_dot(jnp.concatenate(logs[0] + logs[1], axis=0), ones, NN)
            for index in range(2):
                sums = exact_dot(jnp.concatenate(logs[index], axis=0), (upper, lower)[index], NN)
                pre = jnp.zeros((8, LANES), f32)
                post = jnp.zeros((8, LANES), f32)
                offset = index * GROUP * 8
                for chunk in range(GROUP):
                    rows[chunk, rows_at(R_CUM_F + index), :] = sums[chunk * 8 : chunk * 8 + 8]
                    total = totals[offset + chunk * 8 : offset + chunk * 8 + 8]
                    rows[chunk, rows_at(R_TOT_F + index), :] = total
                    rows[chunk, rows_at((R_PRE_F, R_PRE_R)[index]), :] = jnp.exp(pre)
                    pre = pre + total
                for chunk in reversed(range(GROUP)):
                    rows[chunk, rows_at((R_POST_F, R_POST_R)[index]), :] = jnp.exp(post)
                    post = post + totals[offset + chunk * 8 : offset + chunk * 8 + 8]

    for sub in range(UNROLL):
        k = pair * UNROLL + sub
        cums = (rows[k, rows_at(R_CUM_F), :], rows[k, rows_at(R_CUM_R), :])
        growth = [jnp.exp(c) for c in cums]
        tails = [
            jnp.exp(rows[k, rows_at(R_TOT_F + i), :] - cums[i]) * rows[k, rows_at(R_STEP_F + i), :]
            for i in range(2)
        ]
        for head in range(heads):
            at = heads_at(head)
            one = slice(first + head, first + head + 1)
            cur = ext[k + 1, at, :].astype(f32)
            prv = ext[k, at, :].astype(f32)
            nxt = ext[k + 2, at, :].astype(f32)
            base = cw[4, at, :] + cw[0, at, :] * cur
            pre_f, pre_r = base, base
            for tap in range(1, 4):
                weight = cw[tap, at, :]
                pre_f += weight * pltpu.roll(jnp.where(lane < LANES - tap, cur, prv), tap, 1)
                pre_r += weight * pltpu.roll(jnp.where(lane >= tap, cur, nxt), LANES - tap, 1)
            grads = pk[k, width + head * WIDTH : width + (head + 1) * WIDTH, :].astype(f32)
            for index, (pre_act, x_ref, slope_ref) in enumerate(
                ((pre_f, x_f, slope_f), (pre_r, x_r, slope_r))
            ):
                gate = 1.0 / (1.0 + jnp.exp(-pre_act))
                x = pre_act * gate
                x_ref[sub, at, :] = x
                slope_ref[sub, at, :] = gate + x * (1.0 - gate)
                hi, lo = split2(x * tails[index][one])
                out_at = heads_at(head, index * width)
                left_x[sub, out_at, :LANES] = hi
                left_x[sub, out_at, LANES:] = lo
                hi, lo = split2(grads * growth[index][one])
                left_g[sub, out_at, :LANES] = hi
                left_g[sub, out_at, LANES:] = lo
        b_rows = pk1[k, SHARED : SHARED + LANES, :]
        c_rows = pk1[k, SHARED + LANES : SHARED + 2 * LANES, :]
        states = dot(left_x[sub], jnp.concatenate([b_rows, b_rows], axis=0), NN)
        u_f[k] = states[:width]
        u_r[k] = states[width:]
        pulls = dot(left_g[sub], jnp.concatenate([c_rows, c_rows], axis=0), NN)
        v_f[k] = pulls[:width]
        v_r[k] = pulls[width:]

    @pl.when(pair == GROUP // UNROLL - 1)
    def _():
        run[...] = jnp.zeros_like(run)

        def scan(step, _):
            up, down = step, GROUP - 1 - step
            moves = (
                (u_f, up, R_TOT_F), (v_r, up, R_TOT_R), (u_r, down, R_TOT_R), (v_f, down, R_TOT_F)
            )
            for slot, (ref, at_chunk, total) in enumerate(moves):
                factor = jnp.exp(rows[at_chunk, rows_at(total), :])
                for head in range(heads):
                    at = heads_at(head)
                    held = run[slot, at, :]
                    own = ref[at_chunk, at, :]
                    ref[at_chunk, at, :] = held
                    run[slot, at, :] = factor[first + head : first + head + 1] * held + own
            return 0

        lax.fori_loop(0, GROUP, scan, 0)
        whole = [
            rows[GROUP - 1, rows_at(pre), :] * jnp.exp(rows[GROUP - 1, rows_at(total), :])
            for pre, total in ((R_PRE_F, R_TOT_F), (R_PRE_R, R_TOT_R))
        ]
        for ends, pair in ((ends_up, (0, 1)), (ends_down, (2, 3))):
            ends[0:width, :] = run[pair[0]]
            ends[width : 2 * width, :] = run[pair[1]]
            ends[2 * width : 2 * width + 8, :] = whole[0]
            ends[2 * width + 8 : 2 * width + 16, :] = whole[1]


def phase_one(which, pk1, pk, cw, extra):
    first, last = SETS[which]
    heads = last - first
    width = heads * WIDTH
    block = jax.ShapeDtypeStruct((GROUP, width, LANES), f32)
    rows = jax.ShapeDtypeStruct((GROUP, 96, LANES), f32)
    ends = jax.ShapeDtypeStruct((2 * width + 16, LANES), f32)
    outs = [block] * 8 + ([rows] if which == 0 else []) + [ends, ends]
    specs = [chunked((width, LANES))] * 4 + [kept(out.shape) for out in outs[4:]]
    operands = [pk1, cw, *extra] if which == 0 else [pk1, pk, cw, *extra]
    return pl.pallas_call(
        functools.partial(phase_one_kernel, first, heads),
        name=f"phase_one_{which}",
        grid=(GROUP // UNROLL,),
        out_shape=outs,
        in_specs=[kept(operand.shape) for operand in operands],
        out_specs=specs,
        scratch_shapes=[
            pltpu.VMEM((GROUP + 2, width, LANES), bf16),
            pltpu.VMEM((UNROLL, 2 * width, 2 * LANES), bf16),
            pltpu.VMEM((UNROLL, 2 * width, 2 * LANES), bf16),
            pltpu.VMEM((4, width, LANES), f32),
        ],
        cost_estimate=cost(heads),
        compiler_params=pltpu.CompilerParams(vmem_limit_bytes=VMEM),
    )(*operands)


def phase_two_kernel(first, heads, *refs):
    (
        place_y, pk1, pk, cw, rate, skip,
        x_f, x_r, slope_f, slope_r, u_f, u_r, v_f, v_r, rows, *ends,
    ) = refs[:18]
    refs = refs[18:]
    beside = ()
    if first:
        wide_in, edges_in, params_in = refs[:3]
        refs = refs[3:]
    else:
        beside, refs = refs[:2], refs[2:]
    (
        rows_out, wide, edges, params,
        ext, entry, d_pre_f, d_pre_r, acc, lines, *of_chunk,
    ) = refs
    width = heads * WIDTH
    pair = pl.program_id(0)
    row, col = square_masks()
    is_low = row >= col
    is_up = row <= col
    low_one, up_one = zero_one(is_low), zero_one(is_up)
    ones = jnp.ones((LANES, LANES), bf16)
    lane = iota((WIDTH, LANES), 1)

    def held(sub, start, stop):
        return wide_in[sub, start:stop, :] if first else 0.0

    @pl.when(pair == 0)
    def _():
        fill_edges(ext, pk, beside)
        entry[...] = jnp.zeros_like(entry)
        here = place_y[0]
        for away in (3, 2, 1):
            for shift, slots, reached in (
                (away, ((0, 0, 0), (1, 1, 1)), here >= away),
                (ROWS - away, ((2, 0, 1), (3, 1, 0)), here + away < ROWS),
            ):

                @pl.when(reached)
                def _(came=ends[shift - 1], slots=slots):
                    for slot, part, total in slots:
                        start = 2 * width + total * 8
                        factor = came[start : start + 8, :]
                        for head in range(heads):
                            at = heads_at(head)
                            entry[slot, at, :] = (
                                factor[first + head : first + head + 1] * entry[slot, at, :]
                                + came[heads_at(head, part * width), :]
                            )

        of_chunk[8][...] = jnp.zeros_like(of_chunk[8])
        acc[...] = jnp.zeros_like(acc)
        for ref in (d_pre_f, d_pre_r):
            for edge in (0, 1, GROUP + 2, GROUP + 3):
                ref[edge] = jnp.zeros((width, LANES), f32)

    for sub in range(UNROLL):
        k = pair * UNROLL + sub
        (
            states, d_states, state_bits, d_state_bits, reach, pulled, gd, xt, line, a_hi, a_lo,
        ) = [ref.at[sub] for ref in of_chunk]
        b_rows = pk1[k, SHARED : SHARED + LANES, :]
        c_rows = pk1[k, SHARED + LANES : SHARED + 2 * LANES, :]
        step = [rows[k, rows_at(R_STEP_F + i), :] for i in range(2)]
        cum = [rows[k, rows_at(R_CUM_F + i), :] for i in range(2)]
        growth = [jnp.exp(c) for c in cum]
        total = [rows[k, rows_at(R_TOT_F + i), :] for i in range(2)]
        tail = [jnp.exp(total[i] - cum[i]) for i in range(2)]
        factor = [jnp.exp(total[i]) for i in range(2)]
        columns = jnp.concatenate(
            [cum[0], cum[1], jnp.zeros((LANES - 16, LANES), f32)], axis=0
        ).T
        into = (
            (states, state_bits, 0, u_f, R_PRE_F, 0),
            (states, state_bits, 1, u_r, R_POST_R, 2),
            (d_states, d_state_bits, 0, v_f, R_POST_F, 3),
            (d_states, d_state_bits, 1, v_r, R_PRE_R, 1),
        )
        for full, bits, index, local, decay_row, slot in into:
            decay = rows[k, rows_at(decay_row), :]
            for head in range(heads):
                at, to = heads_at(head), heads_at(head, index * width)
                value = local[sub, at, :] + decay[first + head : first + head + 1] * entry[slot, at, :]
                full[to, :] = value
                hi, lo = split2(value)
                bits[to, :LANES] = hi
                bits[to, LANES:] = lo
        reach[...] = dot(state_bits[...], jnp.concatenate([c_rows, c_rows], axis=1), NT)
        pulled[...] = dot(d_state_bits[...], jnp.concatenate([b_rows, b_rows], axis=1), NT)
        scores = dot(c_rows, b_rows, NT)
        d_g = jnp.zeros((LANES, LANES), f32)
        for head in range(heads):
            at = heads_at(head)
            one = slice(first + head, first + head + 1)
            gap_f = columns[:, first + head : first + head + 1] - cum[0][one]
            gap_r = columns[:, 8 + first + head : 9 + first + head] - cum[1][one]
            spread = jnp.exp(jnp.where(is_low, gap_f, gap_r))
            hi, lo = split2(scores * spread)
            a_hi[head, :, :LANES] = hi * low_one
            a_hi[head, :, LANES:] = hi * up_one
            a_lo[head, :, :LANES] = lo * low_one
            a_lo[head, :, LANES:] = lo * up_one
            grad_bits = pk[k, width + head * WIDTH : width + (head + 1) * WIDTH, :]
            grads = grad_bits.astype(f32)
            xs, bits = [], []
            for index, x_ref in enumerate((x_f, x_r)):
                scaled = x_ref[sub, at, :] * step[index][one]
                xs.append(scaled)
                bits.append(split2(scaled))
            d_a = dot(
                jnp.concatenate([grad_bits, grad_bits], axis=0),
                jnp.concatenate(
                    [
                        jnp.concatenate([bits[0][0], bits[1][0]], axis=1),
                        jnp.concatenate([bits[0][1], bits[1][1]], axis=1),
                    ],
                    axis=0,
                ),
                TN,
            )
            d_g += spread * (
                jnp.where(is_low, d_a[:, :LANES], 0.0) + jnp.where(is_up, d_a[:, LANES:], 0.0)
            )
            d_xs = dot(grad_bits, a_hi[head], NN) + dot(grad_bits, a_lo[head], NN)
            out = jnp.zeros((WIDTH, LANES), f32)
            d_skip_line = jnp.zeros((WIDTH, LANES), f32)
            for index, (x_ref, slope_ref, d_pre) in enumerate(
                ((x_f, slope_f, d_pre_f), (x_r, slope_r, d_pre_r))
            ):
                to = heads_at(head, index * width)
                half = slice(index * LANES, (index + 1) * LANES)
                hi, lo = bits[index]
                y = (
                    dot(hi, a_hi[head, :, half], NT)
                    + dot(lo, a_hi[head, :, half], NT)
                    + dot(hi, a_lo[head, :, half], NT)
                    + growth[index][one] * reach[to, :]
                )
                x = x_ref[sub, at, :]
                out += y + skip[one, :] * x
                d_skip_line += grads * x
                from_state = tail[index][one] * pulled[to, :]
                d_x = d_xs[:, half] + from_state
                d_pre[k + 2, at, :] = (step[index][one] * d_x + skip[one, :] * grads) * slope_ref[
                    sub, at, :
                ]
                own = jnp.sum(x * d_x, axis=0, keepdims=True)
                line[index, one, :] = (
                    jnp.sum(grads * y, axis=0, keepdims=True) - step[index][one] * own
                )
                line[2 + index, one, :] = jnp.sum(
                    xs[index] * from_state
                    + factor[index][one] * (d_states[to, :] * states[to, :]),
                    axis=0,
                    keepdims=True,
                )
                line[4 + index, one, :] = own
                hi, lo = split2(grads * growth[index][one])
                gd[to, :LANES] = hi
                gd[to, LANES:] = lo
                hi, lo = split2(xs[index] * tail[index][one])
                xt[to, :LANES] = hi
                xt[to, LANES:] = lo
            rows_out[k, at, :] = out.astype(bf16)
            line[6, one, :] = jnp.sum(d_skip_line, axis=0, keepdims=True)
        g_hi, g_lo = split2(d_g)
        wide_c = dot(gd[:, :LANES], state_bits[...], TN)
        wide[k, LANES : 2 * LANES, :] = held(sub, LANES, 2 * LANES) + (
            dot(g_hi, b_rows, NN)
            + dot(g_lo, b_rows, NN)
            + wide_c[:, :LANES]
            + wide_c[:, LANES:]
            + dot(gd[:, LANES:], state_bits[:, :LANES], TN)
        )
        wide_b = dot(xt[:, :LANES], d_state_bits[...], TN)
        wide[k, :LANES, :] = held(sub, 0, LANES) + (
            dot(g_hi, c_rows, TN)
            + dot(g_lo, c_rows, TN)
            + wide_b[:, :LANES]
            + wide_b[:, LANES:]
            + dot(xt[:, LANES:], d_state_bits[:, :LANES], TN)
        )
        wide[k, 2 * LANES : EDGE, :] = jnp.zeros((8, LANES), f32) + held(sub, 2 * LANES, EDGE)
        lines[:, pl.ds(pl.multiple_of(k * 8, 8), 8), :] = line[...]

    @pl.when(pair == GROUP // UNROLL - 1)
    def _():
        edges[...] = edges_in[...] if first else jnp.zeros_like(edges)
        token, place = iota((8, LANES), 0), iota((8, LANES), 1)
        first_rows = zero_one((token < 3) & (place == token))
        last_rows = zero_one((token >= 5) & (place == token + LANES - 8))

        def lines_of(marker, tile):
            hi, mid, lo = split3(tile)
            return dot(marker, hi, NT) + dot(marker, mid, NT) + dot(marker, lo, NT)

        def put_edge(slot, marker):
            def put(head, total):
                channel = (first + head) * WIDTH
                block, offset = channel // LANES, channel % LANES
                edges[slot, block * 8 : block * 8 + 8, offset : offset + WIDTH] = lines_of(
                    marker, total
                )
            return put

        def taps_of(tile, hid, puts):
            for head in range(heads):
                at = heads_at(head)
                hid_here = hid[at, :].astype(f32)
                own_f, own_r = d_pre_f[tile + 1, at, :], d_pre_r[tile + 1, at, :]
                later_f, earlier_r = d_pre_f[tile + 2, at, :], d_pre_r[tile, at, :]
                both = own_f + own_r
                acc[4, at, :] += both
                acc[0, at, :] += hid_here * both
                total = cw[0, at, :] * both
                for tap in range(1, 4):
                    shifted = pltpu.roll(
                        jnp.where(lane >= tap, own_f, later_f), LANES - tap, 1
                    ) + pltpu.roll(jnp.where(lane < LANES - tap, own_r, earlier_r), tap, 1)
                    acc[tap, at, :] += hid_here * shifted
                    total += cw[tap, at, :] * shifted
                for put in puts:
                    put(head, total)

        def keep_chunk(chunk):
            def put(head, total):
                rows_out[chunk, heads_at(head, width), :] = total.astype(bf16)
            return put

        taps_of(0, ext[0], [put_edge(2, last_rows)])
        taps_of(GROUP + 1, ext[GROUP + 1], [put_edge(3, first_rows)])
        taps_of(1, pk[0], [keep_chunk(0), put_edge(0, first_rows)])
        taps_of(GROUP, pk[GROUP - 1], [keep_chunk(GROUP - 1), put_edge(1, last_rows)])

        def inner(chunk, _):
            taps_of(chunk + 1, pk.at[chunk], [keep_chunk(chunk)])
            return 0

        lax.fori_loop(1, GROUP - 1, inner, 0)
        sums = jnp.zeros((8, width), f32)
        for tap in range(5):
            sums += lines_of(zero_one(token == tap), acc[tap])
        params[...] = params_in[...] if first else jnp.zeros_like(params)
        for start in range(0, width, LANES):
            size = min(LANES, width - start)
            block = (first * WIDTH + start) // LANES
            params[block * 8 : block * 8 + 8, :size] = sums[:, start : start + size]
        def all_rows(slot):
            return jnp.concatenate([rows[c, rows_at(slot), :] for c in range(GROUP)], axis=0)

        def over_chunks(value):
            total = value[0:8]
            for c in range(1, GROUP):
                total = total + value[c * 8 : c * 8 + 8]
            return total

        rates = jnp.concatenate([rate[...]] * GROUP, axis=0)
        tails_here = exact_dot(jnp.concatenate([lines[2], lines[3]], axis=0), ones, NN)
        d_args, d_rate = [], jnp.zeros((GROUP * 8, LANES), f32)
        for index in range(2):
            offset = index * GROUP * 8
            d_log = exact_dot(lines[index], (low_one, up_one)[index], NN) + tails_here[
                offset : offset + GROUP * 8
            ]
            d_args.append((lines[4 + index] + rates * d_log) * all_rows(R_SIG_F + index))
            d_rate += d_log * rates * all_rows(R_STEP_F + index)
        by_code = jnp.zeros((8, LANES), f32)
        for c in range(GROUP):
            own = slice(c * 8, c * 8 + 8)
            wide[c, 2 * LANES : EDGE, :] += d_args[0][own] + d_args[1][own]
            for index, table in enumerate(code_tables(pk1[c, TAIL:PACK, :].astype(f32))):
                by_code += exact_dot(d_args[index][own], table, NT)
        params[24:32, :] += (
            exact_dot(over_chunks(d_rate), zero_one(col == 0), NN)
            + exact_dot(over_chunks(lines[6]), zero_one(col == 1), NN)
            + by_code
        )


def phase_two(which, place_y, pk1, pk, cw, rate, skip, saved, rows, ends, carried):
    first, last = SETS[which]
    heads = last - first
    width = heads * WIDTH
    outs = [
        jax.ShapeDtypeStruct((GROUP, 2 * width, LANES), bf16),
        jax.ShapeDtypeStruct((GROUP, WIDE, LANES), f32),
        jax.ShapeDtypeStruct((4, 24, LANES), f32),
        jax.ShapeDtypeStruct((32, LANES), f32),
    ]
    whole = [pk1, pk, cw, rate, skip]
    in_specs = (
        [pl.BlockSpec(memory_space=pltpu.SMEM)]
        + [kept(operand.shape) for operand in whole]
        + [chunked((width, LANES))] * 8
        + [kept(rows.shape)] + [kept(end.shape) for end in ends]
    )
    if not which:
        in_specs += [kept(block.shape) for block in carried]
    else:
        in_specs += [chunked((WIDE, LANES)), kept((4, 24, LANES)), kept((32, LANES))]
    return pl.pallas_call(
        functools.partial(phase_two_kernel, first, heads),
        name=f"phase_two_{which}",
        grid=(GROUP // UNROLL,),
        out_shape=outs,
        in_specs=in_specs,
        out_specs=[kept(out.shape) for out in outs],
        scratch_shapes=[
            pltpu.VMEM((GROUP + 2, width, LANES), bf16),
            pltpu.VMEM((4, width, LANES), f32),
            pltpu.VMEM((GROUP + 4, width, LANES), f32),
            pltpu.VMEM((GROUP + 4, width, LANES), f32),
            pltpu.VMEM((5, width, LANES), f32),
            pltpu.VMEM((7, GROUP * 8, LANES), f32),
            pltpu.VMEM((UNROLL, 2 * width, LANES), f32),
            pltpu.VMEM((UNROLL, 2 * width, LANES), f32),
            pltpu.VMEM((UNROLL, 2 * width, 2 * LANES), bf16),
            pltpu.VMEM((UNROLL, 2 * width, 2 * LANES), bf16),
            pltpu.VMEM((UNROLL, 2 * width, LANES), f32),
            pltpu.VMEM((UNROLL, 2 * width, LANES), f32),
            pltpu.VMEM((UNROLL, 2 * width, 2 * LANES), bf16),
            pltpu.VMEM((UNROLL, 2 * width, 2 * LANES), bf16),
            pltpu.VMEM((UNROLL, 7, 8, LANES), f32),
            pltpu.VMEM((UNROLL, heads, LANES, 2 * LANES), bf16),
            pltpu.VMEM((UNROLL, heads, LANES, 2 * LANES), bf16),
        ],
        cost_estimate=cost(2 * heads),
        compiler_params=pltpu.CompilerParams(vmem_limit_bytes=VMEM),
    )(place_y, *whole, *saved, rows, *ends, *carried)


def finish_kernel(edges, from_prev, from_next, sums, _, out, lines, sem):
    for target in range(GROUP):
        lines[target, :24, :] = jnp.zeros((24, LANES), f32)
        lines[target, 24:, :] = sums[...]
    lines[0, :24, :] = edges[0] + from_prev[...]
    lines[GROUP - 1, :24, :] = edges[1] + from_next[...]
    copy = pltpu.make_async_copy(lines, out.at[:, EDGE:WIDE, :], sem)
    copy.start()
    copy.wait()


def finish(edges, from_prev, from_next, sums, wide):
    anywhere = pl.BlockSpec(memory_space=pl.ANY)
    return pl.pallas_call(
        finish_kernel,
        name="finish",
        out_shape=jax.ShapeDtypeStruct(wide.shape, f32),
        in_specs=[WHOLE] * 4 + [anywhere],
        out_specs=anywhere,
        scratch_shapes=[pltpu.VMEM((GROUP, WIDE - EDGE, LANES), f32), pltpu.SemaphoreType.DMA],
        input_output_aliases={4: 0},
        compiler_params=pltpu.CompilerParams(vmem_limit_bytes=VMEM),
    )(edges, from_prev, from_next, sums, wide)


def unpack_kernel(place_z, *refs):
    sets, wide = refs[: len(SETS)], refs[len(SETS)]
    (
        layer_out, hid_out, b_out, c_out, dt_out, taps_out, bias_out, rate_out, skip_out, shift_out, code_out,
    ) = refs[len(SETS) + 1 :]
    row, col = square_masks()
    eye = zero_one(row == col)
    line = iota((16, LANES), 0)
    at_start = (line < 3) & (place_z[0] == 0)
    at_end = (line >= 13) & (place_z[0] == GROUP - 1)
    blank = jnp.zeros((8, LANES), f32)
    for order, target in enumerate((layer_out, hid_out)):
        for block in range(GROUP * CH // LANES):
            pieces, edge, taps = [], [], []
            for half in range(2):
                channel = block * LANES + half * WIDTH
                group, at = channel // CH, channel % CH
                offset = at % LANES
                start = EDGE + at // LANES * 8
                taps.append(wide[group, start + 24 : start + 32, offset : offset + WIDTH])
                edge.append(wide[group, start : start + 8, offset : offset + WIDTH])
                which, at = set_row(at, order)
                pieces.append(sets[which][group, at : at + WIDTH, :])
            lanes = slice(block * LANES, (block + 1) * LANES)
            flipped = dot(eye, jnp.concatenate(pieces, axis=0), NT)
            if order:
                taps = jnp.concatenate(taps, axis=1)
                taps_out[:, lanes] = taps[:4]
                bias_out[:, lanes] = taps[4:5]
                edge = jnp.concatenate(edge, axis=1)
                head = jnp.where(at_start, jnp.concatenate([edge, blank], axis=0), flipped[:16])
                tail = jnp.where(
                    at_end, jnp.concatenate([blank, edge], axis=0), flipped[LANES - 16 :]
                )
                flipped = jnp.concatenate([head, flipped[16 : LANES - 16], tail], axis=0)
            target[:, lanes] = flipped.astype(bf16)
    for base, target in ((0, b_out), (LANES, c_out)):
        total = wide[0, base : base + LANES, :]
        for group in range(1, GROUP):
            total += wide[group, base : base + LANES, :]
        target[...] = total
    lines = jnp.concatenate(
        [wide[group, 2 * LANES : EDGE, :] for group in range(GROUP)], axis=0
    )
    pick_row, pick_col = iota((40, GROUP * 8), 0), iota((40, GROUP * 8), 1)
    pick = zero_one(
        ((pick_col % 8) < HEADS) & ((pick_col // 8) * HEADS + (pick_col % 8) == pick_row)
    )
    hi, mid, lo = split3(lines)
    dt_out[...] = dot(pick, hi, NN) + dot(pick, mid, NN) + dot(pick, lo, NN)
    heads = jnp.concatenate([wide[group, WIDE - 8 : WIDE, :] for group in range(GROUP)], axis=0)
    by_head = sum(
        lax.dot_general(part, pick, (((0,), (1,)), ((), ())), preferred_element_type=f32)
        for part in split3(heads)
    )
    rate_out[...] = by_head[0:1]
    skip_out[...] = by_head[1:2]
    shift_out[...] = by_head[2:3]
    code_out[...] = by_head[3:15]


def unpack(place_z, sets, wide):
    rows = jax.ShapeDtypeStruct((LANES, GROUP * CH), bf16)
    square = jax.ShapeDtypeStruct((LANES, LANES), f32)
    return pl.pallas_call(
        unpack_kernel,
        name="unpack",
        out_shape=[rows, rows, square, square, jax.ShapeDtypeStruct((40, LANES), f32)]
        + [
            jax.ShapeDtypeStruct(shape, f32)
            for shape in ((4, GROUP * CH), (1, GROUP * CH), (1, 40), (1, 40), (1, 40), (12, 40))
        ],
        in_specs=[pl.BlockSpec(memory_space=pltpu.SMEM)] + [WHOLE] * (len(SETS) + 1),
        out_specs=[WHOLE] * 11,
        compiler_params=pltpu.CompilerParams(vmem_limit_bytes=VMEM),
    )(place_z, *sets, wide)


def exchange(array):
    return lax.all_to_all(array, "seq", 0, 0, axis_index_groups=Z_GROUPS)


def along_y(array, by):
    pairs = [
        (y * GROUP + z, (y + by) * GROUP + z)
        for y in range(ROWS)
        for z in range(GROUP)
        if 0 <= y + by < ROWS
    ]
    return lax.ppermute(array, "seq", pairs)


def beside(array, by):
    count = lax.axis_size("seq")
    return lax.ppermute(array, "seq", [(i, i + by) for i in range(count) if 0 <= i + by < count])


def cross_y(up, down, run):
    came = []
    for shift in range(1, ROWS):
        pairs = [
            (y * GROUP + z, (y + shift) % ROWS * GROUP + z) for y in range(ROWS) for z in range(GROUP)
        ]
        came.append(lax.ppermute(jnp.where(run + shift < ROWS, up, down), "seq", pairs))
    return came


def flip_bit(array, axis, bit):
    count = lax.axis_size(axis)
    return lax.ppermute(array, axis, [(i, i ^ bit) for i in range(count)])


def total_over(array, axis, low, high):
    near, far, both = (flip_bit(array, axis, bits) for bits in (low, high, low | high))
    return (array + near) + (far + both)


def per_device(
    hidden, b_proj, c_proj, dt_raw, base_ids, complement,
    a_log, d_skip, dt_bias, base_shift, conv_w, conv_b, grad_out,
):
    place = lax.axis_index("seq")
    group, run = place % GROUP, place // GROUP
    here_z, here_y = group[None].astype(jnp.int32), run[None].astype(jnp.int32)
    before = beside(hidden[0, -8:], 1)
    after = beside(hidden[0, :8], -1)
    taps = jnp.concatenate([conv_w, conv_b[None]], axis=0).reshape(5, GROUP, CH)
    taps = lax.dynamic_index_in_dim(taps, group, 1, keepdims=False)
    cw = jnp.broadcast_to(taps[:, :, None], (5, CH, LANES))
    per_head = jnp.stack([-jnp.exp(a_log), d_skip], axis=0)
    tables = jnp.concatenate([dt_bias[None], base_shift], axis=0)
    tables = jnp.concatenate([per_head, tables], axis=0).reshape(15, GROUP, HEADS)
    tables = lax.dynamic_index_in_dim(tables, group, 1, keepdims=False)
    tables = jnp.pad(tables, ((0, 0), (0, 8 - HEADS)))
    rate = jnp.broadcast_to(tables[0][:, None], (8, LANES))
    skip = jnp.broadcast_to(tables[1][:, None], (8, LANES))
    shift_table = jnp.pad(tables[2:].T, ((0, 0), (2, LANES - 15)))

    taps = [cw[:, first * WIDTH : last * WIDTH] for first, last in SETS]

    packed = pack(
        complement, hidden[0], grad_out[0], b_proj[0], c_proj[0], dt_raw[0].T, base_ids
    )
    pk = [exchange(packed[0])]
    second = add_rows_beside(before, after, packed[1])
    second, taps, shift_table, rate, skip = lax.optimization_barrier(
        (second, taps, shift_table, rate, skip)
    )
    pk.append(exchange(second))
    cut = SETS[0][1] * WIDTH
    edge_chunks = (along_y(pk[0][GROUP - 1, :cut], 1), along_y(pk[0][0, :cut], -1))
    saved, ends, sets, carried = [], [], [], edge_chunks
    for which, tap in enumerate(taps):
        *blocks, up, down = phase_one(
            which, pk[0], pk[which], tap, (rows,) if which else (shift_table, rate, *edge_chunks)
        )
        if not which:
            rows = blocks.pop()
        saved.append(blocks)
        ends.append(cross_y(up, down, run))
    for which, tap in enumerate(taps):
        out, *carried = phase_two(
            which, here_y, pk[0], pk[which], tap, rate, skip, saved[which], rows, ends[which], carried
        )
        sets.append(exchange(out))
    wide, edges, sums = carried
    from_next = along_y(edges[2], -1)
    from_prev = along_y(edges[3], 1)
    sums = total_over(sums, "dp", 1, 2)
    sums, from_next, from_prev = lax.optimization_barrier((sums, from_next, from_prev))
    sums = total_over(sums, "seq", GROUP, 2 * GROUP)
    sums = sums + flip_bit(sums, "dp", 4)
    wide = exchange(finish(edges, from_prev, from_next, sums, wide))
    layer_out, d_hidden, d_b, d_c, d_dt, taps, bias, rates, skips, shifts, codes = unpack(
        here_z, sets, wide
    )
    return (
        layer_out[None], d_hidden[None], d_b[None], d_c[None], d_dt.T[None],
        rates[0], skips[0], shifts[0], codes, taps, bias[0],
    )


def solution(mesh):
    rows = P("dp", "seq", None)
    placed = (rows, rows, rows, rows, P("dp", "seq"), P(), P(), P(), P(), P(), P(), P(), rows)
    return jax.shard_map(
        per_device,
        mesh=mesh,
        in_specs=placed,
        out_specs=(rows,) * 5 + (P(),) * 6,
        check_vma=False,
    )
```

```python
import functools

import jax
import jax.numpy as jnp
from jax import lax
from jax.experimental import pallas as pl
from jax.experimental.pallas import tpu as pltpu
from jax.sharding import PartitionSpec as P

bf16 = jnp.bfloat16
f32 = jnp.float32

GROUP = 8
ROWS = 4
LANES = 128
HEADS = 5
WIDTH = 64
CH = HEADS * WIDTH
SETS = ((0, 2), (2, 5))
SHARED = 2 * SETS[0][1] * WIDTH
TAIL = SHARED + 2 * LANES
PACK = TAIL + 32
SECOND = 2 * (SETS[1][1] - SETS[1][0]) * WIDTH
PACK_2 = SECOND + 16
EDGE = 2 * LANES + 8
PARAMS = EDGE + 24
WIDE = PARAMS + 32
UNROLL = 2
VMEM = 58 * 1024 * 1024

Z_GROUPS = [[y * GROUP + z for z in range(GROUP)] for y in range(ROWS)]

NN = (((1,), (0,)), ((), ()))
NT = (((1,), (1,)), ((), ()))
TN = (((0,), (0,)), ((), ()))


def dot(a, b, dims):
    return lax.dot_general(a, b, dims, preferred_element_type=f32)


def split2(a):
    hi = a.astype(bf16)
    return hi, (a - hi.astype(f32)).astype(bf16)


def split3(a):
    hi = a.astype(bf16)
    rest = a - hi.astype(f32)
    mid = rest.astype(bf16)
    return hi, mid, (rest - mid.astype(f32)).astype(bf16)


def exact_dot(a, table, dims):
    count = a.shape[0]
    hi = a.astype(bf16).astype(f32)
    rest = a - hi
    mid = rest.astype(bf16).astype(f32)
    out = dot(jnp.concatenate([hi, mid, rest - mid], axis=0).astype(bf16), table, dims)
    return out[:count] + out[count : 2 * count] + out[2 * count :]


def iota(shape, axis):
    return lax.broadcasted_iota(jnp.int32, shape, axis)


def zero_one(condition):
    return jnp.where(condition, 1.0, 0.0).astype(bf16)


def square_masks():
    row, col = iota((LANES, LANES), 0), iota((LANES, LANES), 1)
    return row, col


def set_row(channel, order):
    for which, (first, last) in enumerate(SETS):
        if channel < last * WIDTH:
            return which, channel - first * WIDTH + order * (last - first) * WIDTH


def pack_kernel(comp_ref, hid_ref, grad_ref, b_ref, c_ref, dt_ref, ids_ref, *outs):
    out_1 = outs[0]
    row, col = square_masks()
    eye = zero_one(row == col)
    for source, order in ((hid_ref, 0), (grad_ref, 1)):
        for block in range(GROUP * CH // LANES):
            piece = source[:, block * LANES : (block + 1) * LANES]
            flipped = dot(eye, piece, NT).astype(bf16)
            for half in range(2):
                channel = block * LANES + half * WIDTH
                target, at = channel // CH, channel % CH
                which, at = set_row(at, order)
                outs[which][target, at : at + WIDTH, :] = flipped[half * WIDTH : (half + 1) * WIDTH]
    pick_row, pick_col = iota((GROUP * 8, 40), 0), iota((GROUP * 8, 40), 1)
    pick = zero_one(
        ((pick_row % 8) < HEADS) & ((pick_row // 8) * HEADS + (pick_row % 8) == pick_col)
    )
    parts = [dot(pick, part, NN) for part in split3(dt_ref[...])]
    ids = ids_ref[...]
    partner = jnp.zeros_like(ids)
    for code in range(12):
        partner = jnp.where(ids == code, comp_ref[code], partner)
    both = jnp.concatenate([ids, partner, jnp.zeros((6, LANES), jnp.int32)], axis=0).astype(f32)
    b_rows, c_rows = b_ref[...], c_ref[...]
    for target in range(GROUP):
        out_1[target, SHARED : SHARED + LANES, :] = b_rows
        out_1[target, SHARED + LANES : SHARED + 2 * LANES, :] = c_rows
        tail = jnp.concatenate(
            [part[target * 8 : target * 8 + 8] for part in parts] + [both], axis=0
        )
        out_1[target, TAIL:PACK, :] = tail.astype(bf16)


def rows_beside_kernel(before_ref, after_ref, _, out, lines, sem):
    beside = jnp.where(
        iota((8, GROUP * CH), 0) >= 5, before_ref[...].astype(f32), after_ref[...].astype(f32)
    )
    for target in range(GROUP):
        start = target * CH + SETS[1][0] * WIDTH
        mine = beside[:, start : (target + 1) * CH]
        mine = jnp.concatenate([mine, jnp.zeros((8, 2 * LANES - mine.shape[1]), f32)], axis=1)
        lines[target] = jnp.concatenate([mine[:, :LANES], mine[:, LANES:]], axis=0).astype(bf16)
    copy = pltpu.make_async_copy(lines, out.at[:, SECOND:PACK_2, :], sem)
    copy.start()
    copy.wait()


WHOLE = pl.BlockSpec(memory_space=pltpu.VMEM)


def pack(complement, hidden, grad, b_rows, c_rows, dt_rows, ids):
    return pl.pallas_call(
        pack_kernel,
        name="pack",
        out_shape=[jax.ShapeDtypeStruct((GROUP, count, LANES), bf16) for count in (PACK, PACK_2)],
        in_specs=[pl.BlockSpec(memory_space=pltpu.SMEM)] + [WHOLE] * 6,
        out_specs=[WHOLE] * len(SETS),
        compiler_params=pltpu.CompilerParams(vmem_limit_bytes=VMEM),
    )(complement, hidden, grad, b_rows, c_rows, dt_rows, ids)


def add_rows_beside(before, after, packed):
    anywhere = pl.BlockSpec(memory_space=pl.ANY)
    return pl.pallas_call(
        rows_beside_kernel,
        name="rows_beside",
        out_shape=jax.ShapeDtypeStruct(packed.shape, bf16),
        in_specs=[WHOLE, WHOLE, anywhere],
        out_specs=anywhere,
        scratch_shapes=[
            pltpu.VMEM((GROUP, PACK_2 - SECOND, LANES), bf16),
            pltpu.SemaphoreType.DMA,
        ],
        input_output_aliases={2: 0},
        compiler_params=pltpu.CompilerParams(vmem_limit_bytes=VMEM),
    )(before, after, packed)


def cost(heads):
    return pl.CostEstimate(flops=heads * 4_000_000_000, bytes_accessed=8_000_000, transcendentals=0)


def kept(shape):
    return pl.BlockSpec(shape, lambda k: (0,) * len(shape))


def chunked(shape):
    return pl.BlockSpec((UNROLL,) + shape, lambda k: (k, 0, 0))


(R_STEP_F, R_STEP_R, R_CUM_F, R_CUM_R, R_SIG_F, R_SIG_R, R_TOT_F, R_TOT_R,
 R_PRE_F, R_POST_F, R_PRE_R, R_POST_R) = range(12)


def code_tables(tail):
    code = iota((LANES, LANES), 0)
    tables = []
    for line in (24, 25):
        ids = (tail[line : line + 1] + 3.0).astype(jnp.int32)
        tables.append(zero_one((code == ids) | (code == 2)))
    return tables


def rows_at(slot):
    return slice(slot * 8, slot * 8 + 8)


def heads_at(head, offset=0):
    return slice(offset + head * WIDTH, offset + (head + 1) * WIDTH)


def beside_chunk(pk, which, place, block):
    lines = pk[which, SECOND:PACK_2, :].astype(f32)[8 * block : 8 * block + 8]
    lines = jnp.concatenate([lines, jnp.zeros((8, LANES), f32)], axis=0).astype(bf16)
    return dot(lines, place, TN).astype(bf16)


def fill_edges(ext, pk, beside):
    if beside:
        ext[0] = beside[0][...]
        ext[GROUP + 1] = beside[1][...]
        return
    token, place = iota((16, LANES), 0), iota((16, LANES), 1)
    before = zero_one((token >= 5) & (token < 8) & (place == token + LANES - 8))
    after = zero_one((token < 3) & (place == token))
    count = ext.shape[1]
    for start in range(0, count, LANES):
        size = min(LANES, count - start)
        block = start // LANES
        ext[0, start : start + size, :] = beside_chunk(pk, 0, before, block)[:size]
        ext[GROUP + 1, start : start + size, :] = beside_chunk(pk, GROUP - 1, after, block)[:size]


def phase_one_kernel(first, heads, *refs):
    beside = ()
    if first == 0:
        pk1, cw, shift_table, rate, *beside = refs[:6]
        pk, refs = pk1, refs[6:]
        rows = refs[8]
        x_f, x_r, slope_f, slope_r, u_f, u_r, v_f, v_r = refs[:8]
        refs = refs[9:]
    else:
        pk1, pk, cw, rows = refs[:4]
        x_f, x_r, slope_f, slope_r, u_f, u_r, v_f, v_r = refs[4:12]
        refs = refs[12:]
    ends_up, ends_down, ext, left_x, left_g, run = refs
    width = heads * WIDTH
    pair = pl.program_id(0)
    lane = iota((WIDTH, LANES), 1)

    @pl.when(pair == 0)
    def _():
        fill_edges(ext, pk, beside)
        for chunk in range(GROUP):
            ext[chunk + 1] = pk[chunk, :width, :]
        if first == 0:
            row, col = square_masks()
            upper = zero_one(row <= col)
            lower = zero_one(row >= col)
            ones = jnp.ones((LANES, LANES), bf16)
            logs = [[], []]
            for chunk in range(GROUP):
                tail = pk1[chunk, TAIL:PACK, :].astype(f32)
                dt = tail[0:8] + tail[8:16] + tail[16:24]
                for index, table in enumerate(code_tables(tail)):
                    arg = dt + exact_dot(shift_table[...], table, NN)
                    decay = jnp.exp(-jnp.abs(arg))
                    step = jnp.maximum(arg, 0.0) + jnp.log1p(decay)
                    logs[index].append(rate[...] * step)
                    rows[chunk, rows_at(R_STEP_F + index), :] = step
                    rows[chunk, rows_at(R_SIG_F + index), :] = (
                        jnp.where(arg >= 0, 1.0, decay) / (1.0 + decay)
                    )
            totals = exact_dot(jnp.concatenate(logs[0] + logs[1], axis=0), ones, NN)
            for index in range(2):
                sums = exact_dot(jnp.concatenate(logs[index], axis=0), (upper, lower)[index], NN)
                pre = jnp.zeros((8, LANES), f32)
                post = jnp.zeros((8, LANES), f32)
                offset = index * GROUP * 8
                for chunk in range(GROUP):
                    rows[chunk, rows_at(R_CUM_F + index), :] = sums[chunk * 8 : chunk * 8 + 8]
                    total = totals[offset + chunk * 8 : offset + chunk * 8 + 8]
                    rows[chunk, rows_at(R_TOT_F + index), :] = total
                    rows[chunk, rows_at((R_PRE_F, R_PRE_R)[index]), :] = jnp.exp(pre)
                    pre = pre + total
                for chunk in reversed(range(GROUP)):
                    rows[chunk, rows_at((R_POST_F, R_POST_R)[index]), :] = jnp.exp(post)
                    post = post + totals[offset + chunk * 8 : offset + chunk * 8 + 8]

    for sub in range(UNROLL):
        k = pair * UNROLL + sub
        cums = (rows[k, rows_at(R_CUM_F), :], rows[k, rows_at(R_CUM_R), :])
        growth = [jnp.exp(c) for c in cums]
        tails = [
            jnp.exp(rows[k, rows_at(R_TOT_F + i), :] - cums[i]) * rows[k, rows_at(R_STEP_F + i), :]
            for i in range(2)
        ]
        for head in range(heads):
            at = heads_at(head)
            one = slice(first + head, first + head + 1)
            cur = ext[k + 1, at, :].astype(f32)
            prv = ext[k, at, :].astype(f32)
            nxt = ext[k + 2, at, :].astype(f32)
            base = cw[4, at, :] + cw[0, at, :] * cur
            pre_f, pre_r = base, base
            for tap in range(1, 4):
                weight = cw[tap, at, :]
                pre_f += weight * pltpu.roll(jnp.where(lane < LANES - tap, cur, prv), tap, 1)
                pre_r += weight * pltpu.roll(jnp.where(lane >= tap, cur, nxt), LANES - tap, 1)
            grads = pk[k, width + head * WIDTH : width + (head + 1) * WIDTH, :].astype(f32)
            for index, (pre_act, x_ref, slope_ref) in enumerate(
                ((pre_f, x_f, slope_f), (pre_r, x_r, slope_r))
            ):
                gate = 1.0 / (1.0 + jnp.exp(-pre_act))
                x = pre_act * gate
                x_ref[sub, at, :] = x
                slope_ref[sub, at, :] = gate + x * (1.0 - gate)
                hi, lo = split2(x * tails[index][one])
                out_at = heads_at(head, index * width)
                left_x[sub, out_at, :LANES] = hi
                left_x[sub, out_at, LANES:] = lo
                hi, lo = split2(grads * growth[index][one])
                left_g[sub, out_at, :LANES] = hi
                left_g[sub, out_at, LANES:] = lo
        b_rows = pk1[k, SHARED : SHARED + LANES, :]
        c_rows = pk1[k, SHARED + LANES : SHARED + 2 * LANES, :]
        states = dot(left_x[sub], jnp.concatenate([b_rows, b_rows], axis=0), NN)
        u_f[k] = states[:width]
        u_r[k] = states[width:]
        pulls = dot(left_g[sub], jnp.concatenate([c_rows, c_rows], axis=0), NN)
        v_f[k] = pulls[:width]
        v_r[k] = pulls[width:]

    @pl.when(pair == GROUP // UNROLL - 1)
    def _():
        run[...] = jnp.zeros_like(run)

        def scan(step, _):
            up, down = step, GROUP - 1 - step
            moves = (
                (u_f, up, R_TOT_F), (v_r, up, R_TOT_R), (u_r, down, R_TOT_R), (v_f, down, R_TOT_F)
            )
            for slot, (ref, at_chunk, total) in enumerate(moves):
                factor = jnp.exp(rows[at_chunk, rows_at(total), :])
                for head in range(heads):
                    at = heads_at(head)
                    held = run[slot, at, :]
                    own = ref[at_chunk, at, :]
                    ref[at_chunk, at, :] = held
                    run[slot, at, :] = factor[first + head : first + head + 1] * held + own
            return 0

        lax.fori_loop(0, GROUP, scan, 0)
        whole = [
            rows[GROUP - 1, rows_at(pre), :] * jnp.exp(rows[GROUP - 1, rows_at(total), :])
            for pre, total in ((R_PRE_F, R_TOT_F), (R_PRE_R, R_TOT_R))
        ]
        for ends, pair in ((ends_up, (0, 1)), (ends_down, (2, 3))):
            ends[0:width, :] = run[pair[0]]
            ends[width : 2 * width, :] = run[pair[1]]
            ends[2 * width : 2 * width + 8, :] = whole[0]
            ends[2 * width + 8 : 2 * width + 16, :] = whole[1]


def phase_one(which, pk1, pk, cw, extra):
    first, last = SETS[which]
    heads = last - first
    width = heads * WIDTH
    block = jax.ShapeDtypeStruct((GROUP, width, LANES), f32)
    rows = jax.ShapeDtypeStruct((GROUP, 96, LANES), f32)
    ends = jax.ShapeDtypeStruct((2 * width + 16, LANES), f32)
    outs = [block] * 8 + ([rows] if which == 0 else []) + [ends, ends]
    specs = [chunked((width, LANES))] * 4 + [kept(out.shape) for out in outs[4:]]
    operands = [pk1, cw, *extra] if which == 0 else [pk1, pk, cw, *extra]
    return pl.pallas_call(
        functools.partial(phase_one_kernel, first, heads),
        name=f"phase_one_{which}",
        grid=(GROUP // UNROLL,),
        out_shape=outs,
        in_specs=[kept(operand.shape) for operand in operands],
        out_specs=specs,
        scratch_shapes=[
            pltpu.VMEM((GROUP + 2, width, LANES), bf16),
            pltpu.VMEM((UNROLL, 2 * width, 2 * LANES), bf16),
            pltpu.VMEM((UNROLL, 2 * width, 2 * LANES), bf16),
            pltpu.VMEM((4, width, LANES), f32),
        ],
        cost_estimate=cost(heads),
        compiler_params=pltpu.CompilerParams(vmem_limit_bytes=VMEM),
    )(*operands)


def phase_two_kernel(first, heads, *refs):
    (
        place_y, pk1, pk, cw, rate, skip,
        x_f, x_r, slope_f, slope_r, u_f, u_r, v_f, v_r, rows, *ends,
    ) = refs[:18]
    refs = refs[18:]
    beside = ()
    if first:
        wide_in, edges_in, params_in = refs[:3]
        refs = refs[3:]
    else:
        beside, refs = refs[:2], refs[2:]
    (
        rows_out, wide, edges, params,
        ext, entry, d_pre_f, d_pre_r, acc, lines, *of_chunk,
    ) = refs
    width = heads * WIDTH
    pair = pl.program_id(0)
    row, col = square_masks()
    is_low = row >= col
    is_up = row <= col
    low_one, up_one = zero_one(is_low), zero_one(is_up)
    ones = jnp.ones((LANES, LANES), bf16)
    lane = iota((WIDTH, LANES), 1)

    def held(sub, start, stop):
        return wide_in[sub, start:stop, :] if first else 0.0

    @pl.when(pair == 0)
    def _():
        fill_edges(ext, pk, beside)
        entry[...] = jnp.zeros_like(entry)
        here = place_y[0]
        for away in (3, 2, 1):
            for shift, slots, reached in (
                (away, ((0, 0, 0), (1, 1, 1)), here >= away),
                (ROWS - away, ((2, 0, 1), (3, 1, 0)), here + away < ROWS),
            ):

                @pl.when(reached)
                def _(came=ends[shift - 1], slots=slots):
                    for slot, part, total in slots:
                        start = 2 * width + total * 8
                        factor = came[start : start + 8, :]
                        for head in range(heads):
                            at = heads_at(head)
                            entry[slot, at, :] = (
                                factor[first + head : first + head + 1] * entry[slot, at, :]
                                + came[heads_at(head, part * width), :]
                            )

        of_chunk[8][...] = jnp.zeros_like(of_chunk[8])
        acc[...] = jnp.zeros_like(acc)
        for ref in (d_pre_f, d_pre_r):
            for edge in (0, 1, GROUP + 2, GROUP + 3):
                ref[edge] = jnp.zeros((width, LANES), f32)

    for sub in range(UNROLL):
        k = pair * UNROLL + sub
        (
            states, d_states, state_bits, d_state_bits, reach, pulled, gd, xt, line, a_hi, a_lo,
        ) = [ref.at[sub] for ref in of_chunk]
        b_rows = pk1[k, SHARED : SHARED + LANES, :]
        c_rows = pk1[k, SHARED + LANES : SHARED + 2 * LANES, :]
        step = [rows[k, rows_at(R_STEP_F + i), :] for i in range(2)]
        cum = [rows[k, rows_at(R_CUM_F + i), :] for i in range(2)]
        growth = [jnp.exp(c) for c in cum]
        total = [rows[k, rows_at(R_TOT_F + i), :] for i in range(2)]
        tail = [jnp.exp(total[i] - cum[i]) for i in range(2)]
        factor = [jnp.exp(total[i]) for i in range(2)]
        columns = jnp.concatenate(
            [cum[0], cum[1], jnp.zeros((LANES - 16, LANES), f32)], axis=0
        ).T
        into = (
            (states, state_bits, 0, u_f, R_PRE_F, 0),
            (states, state_bits, 1, u_r, R_POST_R, 2),
            (d_states, d_state_bits, 0, v_f, R_POST_F, 3),
            (d_states, d_state_bits, 1, v_r, R_PRE_R, 1),
        )
        for full, bits, index, local, decay_row, slot in into:
            decay = rows[k, rows_at(decay_row), :]
            for head in range(heads):
                at, to = heads_at(head), heads_at(head, index * width)
                value = local[sub, at, :] + decay[first + head : first + head + 1] * entry[slot, at, :]
                full[to, :] = value
                hi, lo = split2(value)
                bits[to, :LANES] = hi
                bits[to, LANES:] = lo
        reach[...] = dot(state_bits[...], jnp.concatenate([c_rows, c_rows], axis=1), NT)
        pulled[...] = dot(d_state_bits[...], jnp.concatenate([b_rows, b_rows], axis=1), NT)
        scores = dot(c_rows, b_rows, NT)
        d_g = jnp.zeros((LANES, LANES), f32)
        for head in range(heads):
            at = heads_at(head)
            one = slice(first + head, first + head + 1)
            gap_f = columns[:, first + head : first + head + 1] - cum[0][one]
            gap_r = columns[:, 8 + first + head : 9 + first + head] - cum[1][one]
            spread = jnp.exp(jnp.where(is_low, gap_f, gap_r))
            hi, lo = split2(scores * spread)
            a_hi[head, :, :LANES] = hi * low_one
            a_hi[head, :, LANES:] = hi * up_one
            a_lo[head, :, :LANES] = lo * low_one
            a_lo[head, :, LANES:] = lo * up_one
            grad_bits = pk[k, width + head * WIDTH : width + (head + 1) * WIDTH, :]
            grads = grad_bits.astype(f32)
            xs, bits = [], []
            for index, x_ref in enumerate((x_f, x_r)):
                scaled = x_ref[sub, at, :] * step[index][one]
                xs.append(scaled)
                bits.append(split2(scaled))
            d_a = dot(
                jnp.concatenate([grad_bits, grad_bits], axis=0),
                jnp.concatenate(
                    [
                        jnp.concatenate([bits[0][0], bits[1][0]], axis=1),
                        jnp.concatenate([bits[0][1], bits[1][1]], axis=1),
                    ],
                    axis=0,
                ),
                TN,
            )
            d_g += spread * (
                jnp.where(is_low, d_a[:, :LANES], 0.0) + jnp.where(is_up, d_a[:, LANES:], 0.0)
            )
            d_xs = dot(grad_bits, a_hi[head], NN) + dot(grad_bits, a_lo[head], NN)
            out = jnp.zeros((WIDTH, LANES), f32)
            d_skip_line = jnp.zeros((WIDTH, LANES), f32)
            for index, (x_ref, slope_ref, d_pre) in enumerate(
                ((x_f, slope_f, d_pre_f), (x_r, slope_r, d_pre_r))
            ):
                to = heads_at(head, index * width)
                half = slice(index * LANES, (index + 1) * LANES)
                hi, lo = bits[index]
                y = (
                    dot(hi, a_hi[head, :, half], NT)
                    + dot(lo, a_hi[head, :, half], NT)
                    + dot(hi, a_lo[head, :, half], NT)
                    + growth[index][one] * reach[to, :]
                )
                x = x_ref[sub, at, :]
                out += y + skip[one, :] * x
                d_skip_line += grads * x
                from_state = tail[index][one] * pulled[to, :]
                d_x = d_xs[:, half] + from_state
                d_pre[k + 2, at, :] = (step[index][one] * d_x + skip[one, :] * grads) * slope_ref[
                    sub, at, :
                ]
                own = jnp.sum(x * d_x, axis=0, keepdims=True)
                line[index, one, :] = (
                    jnp.sum(grads * y, axis=0, keepdims=True) - step[index][one] * own
                )
                line[2 + index, one, :] = jnp.sum(
                    xs[index] * from_state
                    + factor[index][one] * (d_states[to, :] * states[to, :]),
                    axis=0,
                    keepdims=True,
                )
                line[4 + index, one, :] = own
                hi, lo = split2(grads * growth[index][one])
                gd[to, :LANES] = hi
                gd[to, LANES:] = lo
                hi, lo = split2(xs[index] * tail[index][one])
                xt[to, :LANES] = hi
                xt[to, LANES:] = lo
            rows_out[k, at, :] = out.astype(bf16)
            line[6, one, :] = jnp.sum(d_skip_line, axis=0, keepdims=True)
        g_hi, g_lo = split2(d_g)
        wide_c = dot(gd[:, :LANES], state_bits[...], TN)
        wide[k, LANES : 2 * LANES, :] = held(sub, LANES, 2 * LANES) + (
            dot(g_hi, b_rows, NN)
            + dot(g_lo, b_rows, NN)
            + wide_c[:, :LANES]
            + wide_c[:, LANES:]
            + dot(gd[:, LANES:], state_bits[:, :LANES], TN)
        )
        wide_b = dot(xt[:, :LANES], d_state_bits[...], TN)
        wide[k, :LANES, :] = held(sub, 0, LANES) + (
            dot(g_hi, c_rows, TN)
            + dot(g_lo, c_rows, TN)
            + wide_b[:, :LANES]
            + wide_b[:, LANES:]
            + dot(xt[:, LANES:], d_state_bits[:, :LANES], TN)
        )
        wide[k, 2 * LANES : EDGE, :] = jnp.zeros((8, LANES), f32) + held(sub, 2 * LANES, EDGE)
        lines[:, pl.ds(pl.multiple_of(k * 8, 8), 8), :] = line[...]

    @pl.when(pair == GROUP // UNROLL - 1)
    def _():
        edges[...] = edges_in[...] if first else jnp.zeros_like(edges)
        token, place = iota((8, LANES), 0), iota((8, LANES), 1)
        first_rows = zero_one((token < 3) & (place == token))
        last_rows = zero_one((token >= 5) & (place == token + LANES - 8))

        def lines_of(marker, tile):
            hi, mid, lo = split3(tile)
            return dot(marker, hi, NT) + dot(marker, mid, NT) + dot(marker, lo, NT)

        def put_edge(slot, marker):
            def put(head, total):
                channel = (first + head) * WIDTH
                block, offset = channel // LANES, channel % LANES
                edges[slot, block * 8 : block * 8 + 8, offset : offset + WIDTH] = lines_of(
                    marker, total
                )
            return put

        def taps_of(tile, hid, puts):
            for head in range(heads):
                at = heads_at(head)
                hid_here = hid[at, :].astype(f32)
                own_f, own_r = d_pre_f[tile + 1, at, :], d_pre_r[tile + 1, at, :]
                later_f, earlier_r = d_pre_f[tile + 2, at, :], d_pre_r[tile, at, :]
                both = own_f + own_r
                acc[4, at, :] += both
                acc[0, at, :] += hid_here * both
                total = cw[0, at, :] * both
                for tap in range(1, 4):
                    shifted = pltpu.roll(
                        jnp.where(lane >= tap, own_f, later_f), LANES - tap, 1
                    ) + pltpu.roll(jnp.where(lane < LANES - tap, own_r, earlier_r), tap, 1)
                    acc[tap, at, :] += hid_here * shifted
                    total += cw[tap, at, :] * shifted
                for put in puts:
                    put(head, total)

        def keep_chunk(chunk):
            def put(head, total):
                rows_out[chunk, heads_at(head, width), :] = total.astype(bf16)
            return put

        taps_of(0, ext[0], [put_edge(2, last_rows)])
        taps_of(GROUP + 1, ext[GROUP + 1], [put_edge(3, first_rows)])
        taps_of(1, pk[0], [keep_chunk(0), put_edge(0, first_rows)])
        taps_of(GROUP, pk[GROUP - 1], [keep_chunk(GROUP - 1), put_edge(1, last_rows)])

        def inner(chunk, _):
            taps_of(chunk + 1, pk.at[chunk], [keep_chunk(chunk)])
            return 0

        lax.fori_loop(1, GROUP - 1, inner, 0)
        sums = jnp.zeros((8, width), f32)
        for tap in range(5):
            sums += lines_of(zero_one(token == tap), acc[tap])
        params[...] = params_in[...] if first else jnp.zeros_like(params)
        for start in range(0, width, LANES):
            size = min(LANES, width - start)
            block = (first * WIDTH + start) // LANES
            params[block * 8 : block * 8 + 8, :size] = sums[:, start : start + size]
        def all_rows(slot):
            return jnp.concatenate([rows[c, rows_at(slot), :] for c in range(GROUP)], axis=0)

        def over_chunks(value):
            total = value[0:8]
            for c in range(1, GROUP):
                total = total + value[c * 8 : c * 8 + 8]
            return total

        rates = jnp.concatenate([rate[...]] * GROUP, axis=0)
        tails_here = exact_dot(jnp.concatenate([lines[2], lines[3]], axis=0), ones, NN)
        d_args, d_rate = [], jnp.zeros((GROUP * 8, LANES), f32)
        for index in range(2):
            offset = index * GROUP * 8
            d_log = exact_dot(lines[index], (low_one, up_one)[index], NN) + tails_here[
                offset : offset + GROUP * 8
            ]
            d_args.append((lines[4 + index] + rates * d_log) * all_rows(R_SIG_F + index))
            d_rate += d_log * rates * all_rows(R_STEP_F + index)
        by_code = jnp.zeros((8, LANES), f32)
        for c in range(GROUP):
            own = slice(c * 8, c * 8 + 8)
            wide[c, 2 * LANES : EDGE, :] += d_args[0][own] + d_args[1][own]
            for index, table in enumerate(code_tables(pk1[c, TAIL:PACK, :].astype(f32))):
                by_code += exact_dot(d_args[index][own], table, NT)
        params[24:32, :] += (
            exact_dot(over_chunks(d_rate), zero_one(col == 0), NN)
            + exact_dot(over_chunks(lines[6]), zero_one(col == 1), NN)
            + by_code
        )


def phase_two(which, place_y, pk1, pk, cw, rate, skip, saved, rows, ends, carried):
    first, last = SETS[which]
    heads = last - first
    width = heads * WIDTH
    outs = [
        jax.ShapeDtypeStruct((GROUP, 2 * width, LANES), bf16),
        jax.ShapeDtypeStruct((GROUP, WIDE, LANES), f32),
        jax.ShapeDtypeStruct((4, 24, LANES), f32),
        jax.ShapeDtypeStruct((32, LANES), f32),
    ]
    whole = [pk1, pk, cw, rate, skip]
    in_specs = (
        [pl.BlockSpec(memory_space=pltpu.SMEM)]
        + [kept(operand.shape) for operand in whole]
        + [chunked((width, LANES))] * 8
        + [kept(rows.shape)] + [kept(end.shape) for end in ends]
    )
    if not which:
        in_specs += [kept(block.shape) for block in carried]
    else:
        in_specs += [chunked((WIDE, LANES)), kept((4, 24, LANES)), kept((32, LANES))]
    return pl.pallas_call(
        functools.partial(phase_two_kernel, first, heads),
        name=f"phase_two_{which}",
        grid=(GROUP // UNROLL,),
        out_shape=outs,
        in_specs=in_specs,
        out_specs=[kept(out.shape) for out in outs],
        scratch_shapes=[
            pltpu.VMEM((GROUP + 2, width, LANES), bf16),
            pltpu.VMEM((4, width, LANES), f32),
            pltpu.VMEM((GROUP + 4, width, LANES), f32),
            pltpu.VMEM((GROUP + 4, width, LANES), f32),
            pltpu.VMEM((5, width, LANES), f32),
            pltpu.VMEM((7, GROUP * 8, LANES), f32),
            pltpu.VMEM((UNROLL, 2 * width, LANES), f32),
            pltpu.VMEM((UNROLL, 2 * width, LANES), f32),
            pltpu.VMEM((UNROLL, 2 * width, 2 * LANES), bf16),
            pltpu.VMEM((UNROLL, 2 * width, 2 * LANES), bf16),
            pltpu.VMEM((UNROLL, 2 * width, LANES), f32),
            pltpu.VMEM((UNROLL, 2 * width, LANES), f32),
            pltpu.VMEM((UNROLL, 2 * width, 2 * LANES), bf16),
            pltpu.VMEM((UNROLL, 2 * width, 2 * LANES), bf16),
            pltpu.VMEM((UNROLL, 7, 8, LANES), f32),
            pltpu.VMEM((UNROLL, heads, LANES, 2 * LANES), bf16),
            pltpu.VMEM((UNROLL, heads, LANES, 2 * LANES), bf16),
        ],
        cost_estimate=cost(2 * heads),
        compiler_params=pltpu.CompilerParams(vmem_limit_bytes=VMEM),
    )(place_y, *whole, *saved, rows, *ends, *carried)


def finish_kernel(edges, from_prev, from_next, sums, _, out, lines, sem):
    for target in range(GROUP):
        lines[target, :24, :] = jnp.zeros((24, LANES), f32)
        lines[target, 24:, :] = sums[...]
    lines[0, :24, :] = edges[0] + from_prev[...]
    lines[GROUP - 1, :24, :] = edges[1] + from_next[...]
    copy = pltpu.make_async_copy(lines, out.at[:, EDGE:WIDE, :], sem)
    copy.start()
    copy.wait()


def finish(edges, from_prev, from_next, sums, wide):
    anywhere = pl.BlockSpec(memory_space=pl.ANY)
    return pl.pallas_call(
        finish_kernel,
        name="finish",
        out_shape=jax.ShapeDtypeStruct(wide.shape, f32),
        in_specs=[WHOLE] * 4 + [anywhere],
        out_specs=anywhere,
        scratch_shapes=[pltpu.VMEM((GROUP, WIDE - EDGE, LANES), f32), pltpu.SemaphoreType.DMA],
        input_output_aliases={4: 0},
        compiler_params=pltpu.CompilerParams(vmem_limit_bytes=VMEM),
    )(edges, from_prev, from_next, sums, wide)


def unpack_kernel(place_z, *refs):
    sets, wide = refs[: len(SETS)], refs[len(SETS)]
    (
        layer_out, hid_out, b_out, c_out, dt_out, taps_out, bias_out, rate_out, skip_out, shift_out, code_out,
    ) = refs[len(SETS) + 1 :]
    row, col = square_masks()
    eye = zero_one(row == col)
    line = iota((16, LANES), 0)
    at_start = (line < 3) & (place_z[0] == 0)
    at_end = (line >= 13) & (place_z[0] == GROUP - 1)
    blank = jnp.zeros((8, LANES), f32)
    for order, target in enumerate((layer_out, hid_out)):
        for block in range(GROUP * CH // LANES):
            pieces, edge, taps = [], [], []
            for half in range(2):
                channel = block * LANES + half * WIDTH
                group, at = channel // CH, channel % CH
                offset = at % LANES
                start = EDGE + at // LANES * 8
                taps.append(wide[group, start + 24 : start + 32, offset : offset + WIDTH])
                edge.append(wide[group, start : start + 8, offset : offset + WIDTH])
                which, at = set_row(at, order)
                pieces.append(sets[which][group, at : at + WIDTH, :])
            lanes = slice(block * LANES, (block + 1) * LANES)
            flipped = dot(eye, jnp.concatenate(pieces, axis=0), NT)
            if order:
                taps = jnp.concatenate(taps, axis=1)
                taps_out[:, lanes] = taps[:4]
                bias_out[:, lanes] = taps[4:5]
                edge = jnp.concatenate(edge, axis=1)
                head = jnp.where(at_start, jnp.concatenate([edge, blank], axis=0), flipped[:16])
                tail = jnp.where(
                    at_end, jnp.concatenate([blank, edge], axis=0), flipped[LANES - 16 :]
                )
                flipped = jnp.concatenate([head, flipped[16 : LANES - 16], tail], axis=0)
            target[:, lanes] = flipped.astype(bf16)
    for base, target in ((0, b_out), (LANES, c_out)):
        total = wide[0, base : base + LANES, :]
        for group in range(1, GROUP):
            total += wide[group, base : base + LANES, :]
        target[...] = total
    lines = jnp.concatenate(
        [wide[group, 2 * LANES : EDGE, :] for group in range(GROUP)], axis=0
    )
    pick_row, pick_col = iota((40, GROUP * 8), 0), iota((40, GROUP * 8), 1)
    pick = zero_one(
        ((pick_col % 8) < HEADS) & ((pick_col // 8) * HEADS + (pick_col % 8) == pick_row)
    )
    hi, mid, lo = split3(lines)
    dt_out[...] = dot(pick, hi, NN) + dot(pick, mid, NN) + dot(pick, lo, NN)
    heads = jnp.concatenate([wide[group, WIDE - 8 : WIDE, :] for group in range(GROUP)], axis=0)
    by_head = sum(
        lax.dot_general(part, pick, (((0,), (1,)), ((), ())), preferred_element_type=f32)
        for part in split3(heads)
    )
    rate_out[...] = by_head[0:1]
    skip_out[...] = by_head[1:2]
    shift_out[...] = by_head[2:3]
    code_out[...] = by_head[3:15]


def unpack(place_z, sets, wide):
    rows = jax.ShapeDtypeStruct((LANES, GROUP * CH), bf16)
    square = jax.ShapeDtypeStruct((LANES, LANES), f32)
    return pl.pallas_call(
        unpack_kernel,
        name="unpack",
        out_shape=[rows, rows, square, square, jax.ShapeDtypeStruct((40, LANES), f32)]
        + [
            jax.ShapeDtypeStruct(shape, f32)
            for shape in ((4, GROUP * CH), (1, GROUP * CH), (1, 40), (1, 40), (1, 40), (12, 40))
        ],
        in_specs=[pl.BlockSpec(memory_space=pltpu.SMEM)] + [WHOLE] * (len(SETS) + 1),
        out_specs=[WHOLE] * 11,
        compiler_params=pltpu.CompilerParams(vmem_limit_bytes=VMEM),
    )(place_z, *sets, wide)


def exchange(array):
    return lax.all_to_all(array, "seq", 0, 0, axis_index_groups=Z_GROUPS)


def along_y(array, by):
    pairs = [
        (y * GROUP + z, (y + by) * GROUP + z)
        for y in range(ROWS)
        for z in range(GROUP)
        if 0 <= y + by < ROWS
    ]
    return lax.ppermute(array, "seq", pairs)


def beside(array, by):
    count = lax.axis_size("seq")
    return lax.ppermute(array, "seq", [(i, i + by) for i in range(count) if 0 <= i + by < count])


def cross_y(up, down, run):
    came = []
    for shift in range(1, ROWS):
        pairs = [
            (y * GROUP + z, (y + shift) % ROWS * GROUP + z) for y in range(ROWS) for z in range(GROUP)
        ]
        came.append(lax.ppermute(jnp.where(run + shift < ROWS, up, down), "seq", pairs))
    return came


def flip_bit(array, axis, bit):
    count = lax.axis_size(axis)
    return lax.ppermute(array, axis, [(i, i ^ bit) for i in range(count)])


def total_over(array, axis, low, high):
    near, far, both = (flip_bit(array, axis, bits) for bits in (low, high, low | high))
    return (array + near) + (far + both)


def per_device(
    hidden, b_proj, c_proj, dt_raw, base_ids, complement,
    a_log, d_skip, dt_bias, base_shift, conv_w, conv_b, grad_out,
):
    place = lax.axis_index("seq")
    group, run = place % GROUP, place // GROUP
    here_z, here_y = group[None].astype(jnp.int32), run[None].astype(jnp.int32)
    taps = jnp.concatenate([conv_w, conv_b[None]], axis=0).reshape(5, GROUP, CH)
    taps = lax.dynamic_index_in_dim(taps, group, 1, keepdims=False)
    cw = jnp.broadcast_to(taps[:, :, None], (5, CH, LANES))
    per_head = jnp.stack([-jnp.exp(a_log), d_skip], axis=0)
    tables = jnp.concatenate([dt_bias[None], base_shift], axis=0)
    tables = jnp.concatenate([per_head, tables], axis=0).reshape(15, GROUP, HEADS)
    tables = lax.dynamic_index_in_dim(tables, group, 1, keepdims=False)
    tables = jnp.pad(tables, ((0, 0), (0, 8 - HEADS)))
    rate = jnp.broadcast_to(tables[0][:, None], (8, LANES))
    skip = jnp.broadcast_to(tables[1][:, None], (8, LANES))
    shift_table = jnp.pad(tables[2:].T, ((0, 0), (2, LANES - 15)))

    taps = [cw[:, first * WIDTH : last * WIDTH] for first, last in SETS]

    packed = pack(
        complement, hidden[0], grad_out[0], b_proj[0], c_proj[0], dt_raw[0].T, base_ids
    )
    pk = [exchange(packed[0])]
    last, leading, taps, shift_table, rate, skip = lax.optimization_barrier(
        (hidden[0, -8:], hidden[0, :8], taps, shift_table, rate, skip)
    )
    second = add_rows_beside(beside(last, 1), beside(leading, -1), packed[1])
    pk.append(exchange(second))
    cut = SETS[0][1] * WIDTH
    edge_chunks = (along_y(pk[0][GROUP - 1, :cut], 1), along_y(pk[0][0, :cut], -1))
    saved, ends, sets, carried = [], [], [], edge_chunks
    for which, tap in enumerate(taps):
        *blocks, up, down = phase_one(
            which, pk[0], pk[which], tap, (rows,) if which else (shift_table, rate, *edge_chunks)
        )
        if not which:
            rows = blocks.pop()
        saved.append(blocks)
        ends.append(cross_y(up, down, run))
    for which, tap in enumerate(taps):
        out, *carried = phase_two(
            which, here_y, pk[0], pk[which], tap, rate, skip, saved[which], rows, ends[which], carried
        )
        sets.append(exchange(out))
    wide, edges, sums = carried
    lines = jnp.concatenate([sums, edges[2], edges[3]], axis=0)
    near, both = flip_bit(lines, "seq", GROUP), flip_bit(lines, "seq", 3 * GROUP)
    far = flip_bit(sums, "seq", 2 * GROUP)
    odd = run % 2 == 1
    from_next = jnp.where(odd, both[32:56], near[32:56])
    from_next = jnp.where(run == ROWS - 1, 0.0, from_next)
    from_prev = jnp.where(odd, near[56:], both[56:])
    from_prev = jnp.where(run == 0, 0.0, from_prev)
    sums = (sums + near[:32]) + (far + both[:32])
    sums = total_over(sums, "dp", 1, 2)
    sums = sums + flip_bit(sums, "dp", 4)
    wide = exchange(finish(edges, from_prev, from_next, sums, wide))
    layer_out, d_hidden, d_b, d_c, d_dt, taps, bias, rates, skips, shifts, codes = unpack(
        here_z, sets, wide
    )
    return (
        layer_out[None], d_hidden[None], d_b[None], d_c[None], d_dt.T[None],
        rates[0], skips[0], shifts[0], codes, taps, bias[0],
    )


def solution(mesh):
    rows = P("dp", "seq", None)
    placed = (rows, rows, rows, rows, P("dp", "seq"), P(), P(), P(), P(), P(), P(), P(), rows)
    return jax.shard_map(
        per_device,
        mesh=mesh,
        in_specs=placed,
        out_specs=(rows,) * 5 + (P(),) * 6,
        check_vma=False,
    )
```

```python
import functools

import jax
import jax.numpy as jnp
from jax import lax
from jax.experimental import pallas as pl
from jax.experimental.pallas import tpu as pltpu
from jax.sharding import PartitionSpec as P

bf16 = jnp.bfloat16
f32 = jnp.float32

GROUP = 8
ROWS = 4
LANES = 128
HEADS = 5
WIDTH = 64
CH = HEADS * WIDTH
SETS = ((0, 2), (2, 5))
SHARED = 2 * SETS[0][1] * WIDTH
TAIL = SHARED + 2 * LANES
PACK = TAIL + 32
SECOND = 2 * (SETS[1][1] - SETS[1][0]) * WIDTH
PACK_2 = SECOND + 16
EDGE = 2 * LANES + 8
WIDE = EDGE + 32
UNROLL = 2
VMEM = 58 * 1024 * 1024

Z_GROUPS = [[y * GROUP + z for z in range(GROUP)] for y in range(ROWS)]

NN = (((1,), (0,)), ((), ()))
NT = (((1,), (1,)), ((), ()))
TN = (((0,), (0,)), ((), ()))


def dot(a, b, dims):
    return lax.dot_general(a, b, dims, preferred_element_type=f32)


def split2(a):
    hi = a.astype(bf16)
    return hi, (a - hi.astype(f32)).astype(bf16)


def split3(a):
    hi = a.astype(bf16)
    rest = a - hi.astype(f32)
    mid = rest.astype(bf16)
    return hi, mid, (rest - mid.astype(f32)).astype(bf16)


def exact_dot(a, table, dims):
    count = a.shape[0]
    hi = a.astype(bf16).astype(f32)
    rest = a - hi
    mid = rest.astype(bf16).astype(f32)
    out = dot(jnp.concatenate([hi, mid, rest - mid], axis=0).astype(bf16), table, dims)
    return out[:count] + out[count : 2 * count] + out[2 * count :]


def iota(shape, axis):
    return lax.broadcasted_iota(jnp.int32, shape, axis)


def zero_one(condition):
    return jnp.where(condition, 1.0, 0.0).astype(bf16)


def square_masks():
    row, col = iota((LANES, LANES), 0), iota((LANES, LANES), 1)
    return row, col


def set_row(channel, order):
    for which, (first, last) in enumerate(SETS):
        if channel < last * WIDTH:
            return which, channel - first * WIDTH + order * (last - first) * WIDTH


def pack_kernel(comp_ref, hid_ref, grad_ref, b_ref, c_ref, dt_ref, ids_ref, *outs):
    out_1 = outs[0]
    row, col = square_masks()
    eye = zero_one(row == col)
    for source, order in ((hid_ref, 0), (grad_ref, 1)):
        for block in range(GROUP * CH // LANES):
            piece = source[:, block * LANES : (block + 1) * LANES]
            flipped = dot(eye, piece, NT).astype(bf16)
            for half in range(2):
                channel = block * LANES + half * WIDTH
                target, at = channel // CH, channel % CH
                which, at = set_row(at, order)
                outs[which][target, at : at + WIDTH, :] = flipped[half * WIDTH : (half + 1) * WIDTH]
    pick_row, pick_col = iota((GROUP * 8, 40), 0), iota((GROUP * 8, 40), 1)
    pick = zero_one(
        ((pick_row % 8) < HEADS) & ((pick_row // 8) * HEADS + (pick_row % 8) == pick_col)
    )
    parts = [dot(pick, part, NN) for part in split3(dt_ref[...])]
    ids = ids_ref[...]
    partner = jnp.zeros_like(ids)
    for code in range(12):
        partner = jnp.where(ids == code, comp_ref[code], partner)
    both = jnp.concatenate([ids, partner, jnp.zeros((6, LANES), jnp.int32)], axis=0).astype(f32)
    b_rows, c_rows = b_ref[...], c_ref[...]
    for target in range(GROUP):
        out_1[target, SHARED : SHARED + LANES, :] = b_rows
        out_1[target, SHARED + LANES : SHARED + 2 * LANES, :] = c_rows
        tail = jnp.concatenate(
            [part[target * 8 : target * 8 + 8] for part in parts] + [both], axis=0
        )
        out_1[target, TAIL:PACK, :] = tail.astype(bf16)


def rows_beside_kernel(before_ref, after_ref, _, out, lines, sem):
    beside = jnp.where(
        iota((8, GROUP * CH), 0) >= 5, before_ref[...].astype(f32), after_ref[...].astype(f32)
    )
    for target in range(GROUP):
        start = target * CH + SETS[1][0] * WIDTH
        mine = beside[:, start : (target + 1) * CH]
        mine = jnp.concatenate([mine, jnp.zeros((8, 2 * LANES - mine.shape[1]), f32)], axis=1)
        lines[target] = jnp.concatenate([mine[:, :LANES], mine[:, LANES:]], axis=0).astype(bf16)
    copy = pltpu.make_async_copy(lines, out.at[:, SECOND:PACK_2, :], sem)
    copy.start()
    copy.wait()


WHOLE = pl.BlockSpec(memory_space=pltpu.VMEM)


def pack(complement, hidden, grad, b_rows, c_rows, dt_rows, ids):
    return pl.pallas_call(
        pack_kernel,
        name="pack",
        out_shape=[jax.ShapeDtypeStruct((GROUP, count, LANES), bf16) for count in (PACK, PACK_2)],
        in_specs=[pl.BlockSpec(memory_space=pltpu.SMEM)] + [WHOLE] * 6,
        out_specs=[WHOLE] * len(SETS),
        compiler_params=pltpu.CompilerParams(vmem_limit_bytes=VMEM),
    )(complement, hidden, grad, b_rows, c_rows, dt_rows, ids)


def add_rows_beside(before, after, packed):
    anywhere = pl.BlockSpec(memory_space=pl.ANY)
    return pl.pallas_call(
        rows_beside_kernel,
        name="rows_beside",
        out_shape=jax.ShapeDtypeStruct(packed.shape, bf16),
        in_specs=[WHOLE, WHOLE, anywhere],
        out_specs=anywhere,
        scratch_shapes=[
            pltpu.VMEM((GROUP, PACK_2 - SECOND, LANES), bf16),
            pltpu.SemaphoreType.DMA,
        ],
        input_output_aliases={2: 0},
        compiler_params=pltpu.CompilerParams(vmem_limit_bytes=VMEM),
    )(before, after, packed)


def cost(heads):
    return pl.CostEstimate(flops=heads * 4_000_000_000, bytes_accessed=8_000_000, transcendentals=0)


def kept(shape):
    return pl.BlockSpec(shape, lambda k: (0,) * len(shape))


def chunked(shape):
    return pl.BlockSpec((UNROLL,) + shape, lambda k: (k, 0, 0))


(R_STEP_F, R_STEP_R, R_CUM_F, R_CUM_R, R_SIG_F, R_SIG_R, R_TOT_F, R_TOT_R,
 R_PRE_F, R_POST_F, R_PRE_R, R_POST_R) = range(12)


def code_tables(tail):
    code = iota((LANES, LANES), 0)
    tables = []
    for line in (24, 25):
        ids = (tail[line : line + 1] + 3.0).astype(jnp.int32)
        tables.append(zero_one((code == ids) | (code == 2)))
    return tables


def rows_at(slot):
    return slice(slot * 8, slot * 8 + 8)


def heads_at(head, offset=0):
    return slice(offset + head * WIDTH, offset + (head + 1) * WIDTH)


def beside_chunk(pk, which, place, block):
    lines = pk[which, SECOND:PACK_2, :].astype(f32)[8 * block : 8 * block + 8]
    lines = jnp.concatenate([lines, jnp.zeros((8, LANES), f32)], axis=0).astype(bf16)
    return dot(lines, place, TN).astype(bf16)


def fill_edges(ext, pk, beside):
    if beside:
        ext[0] = beside[0][...]
        ext[GROUP + 1] = beside[1][...]
        return
    token, place = iota((16, LANES), 0), iota((16, LANES), 1)
    before = zero_one((token >= 5) & (token < 8) & (place == token + LANES - 8))
    after = zero_one((token < 3) & (place == token))
    count = ext.shape[1]
    for start in range(0, count, LANES):
        size = min(LANES, count - start)
        block = start // LANES
        ext[0, start : start + size, :] = beside_chunk(pk, 0, before, block)[:size]
        ext[GROUP + 1, start : start + size, :] = beside_chunk(pk, GROUP - 1, after, block)[:size]


def phase_one_kernel(first, heads, *refs):
    beside = ()
    if first == 0:
        pk1, cw, shift_table, rate, *beside = refs[:6]
        pk, refs = pk1, refs[6:]
        rows = refs[8]
        x_f, x_r, slope_f, slope_r, u_f, u_r, v_f, v_r = refs[:8]
        refs = refs[9:]
    else:
        pk1, pk, cw, rows = refs[:4]
        x_f, x_r, slope_f, slope_r, u_f, u_r, v_f, v_r = refs[4:12]
        refs = refs[12:]
    ends_up, ends_down, ext, left_x, left_g, run = refs
    width = heads * WIDTH
    pair = pl.program_id(0)
    lane = iota((WIDTH, LANES), 1)

    @pl.when(pair == 0)
    def _():
        fill_edges(ext, pk, beside)
        for chunk in range(GROUP):
            ext[chunk + 1] = pk[chunk, :width, :]
        if first == 0:
            row, col = square_masks()
            upper = zero_one(row <= col)
            lower = zero_one(row >= col)
            ones = jnp.ones((LANES, LANES), bf16)
            logs = [[], []]
            for chunk in range(GROUP):
                tail = pk1[chunk, TAIL:PACK, :].astype(f32)
                dt = tail[0:8] + tail[8:16] + tail[16:24]
                for index, table in enumerate(code_tables(tail)):
                    arg = dt + exact_dot(shift_table[...], table, NN)
                    decay = jnp.exp(-jnp.abs(arg))
                    step = jnp.maximum(arg, 0.0) + jnp.log1p(decay)
                    logs[index].append(rate[...] * step)
                    rows[chunk, rows_at(R_STEP_F + index), :] = step
                    rows[chunk, rows_at(R_SIG_F + index), :] = (
                        jnp.where(arg >= 0, 1.0, decay) / (1.0 + decay)
                    )
            totals = exact_dot(jnp.concatenate(logs[0] + logs[1], axis=0), ones, NN)
            for index in range(2):
                sums = exact_dot(jnp.concatenate(logs[index], axis=0), (upper, lower)[index], NN)
                pre = jnp.zeros((8, LANES), f32)
                post = jnp.zeros((8, LANES), f32)
                offset = index * GROUP * 8
                for chunk in range(GROUP):
                    rows[chunk, rows_at(R_CUM_F + index), :] = sums[chunk * 8 : chunk * 8 + 8]
                    total = totals[offset + chunk * 8 : offset + chunk * 8 + 8]
                    rows[chunk, rows_at(R_TOT_F + index), :] = total
                    rows[chunk, rows_at((R_PRE_F, R_PRE_R)[index]), :] = jnp.exp(pre)
                    pre = pre + total
                for chunk in reversed(range(GROUP)):
                    rows[chunk, rows_at((R_POST_F, R_POST_R)[index]), :] = jnp.exp(post)
                    post = post + totals[offset + chunk * 8 : offset + chunk * 8 + 8]

    for sub in range(UNROLL):
        k = pair * UNROLL + sub
        cums = (rows[k, rows_at(R_CUM_F), :], rows[k, rows_at(R_CUM_R), :])
        growth = [jnp.exp(c) for c in cums]
        tails = [
            jnp.exp(rows[k, rows_at(R_TOT_F + i), :] - cums[i]) * rows[k, rows_at(R_STEP_F + i), :]
            for i in range(2)
        ]
        for head in range(heads):
            at = heads_at(head)
            one = slice(first + head, first + head + 1)
            cur = ext[k + 1, at, :].astype(f32)
            prv = ext[k, at, :].astype(f32)
            nxt = ext[k + 2, at, :].astype(f32)
            base = cw[4, at, :] + cw[0, at, :] * cur
            pre_f, pre_r = base, base
            for tap in range(1, 4):
                weight = cw[tap, at, :]
                pre_f += weight * pltpu.roll(jnp.where(lane < LANES - tap, cur, prv), tap, 1)
                pre_r += weight * pltpu.roll(jnp.where(lane >= tap, cur, nxt), LANES - tap, 1)
            grads = pk[k, width + head * WIDTH : width + (head + 1) * WIDTH, :].astype(f32)
            for index, (pre_act, x_ref, slope_ref) in enumerate(
                ((pre_f, x_f, slope_f), (pre_r, x_r, slope_r))
            ):
                gate = 1.0 / (1.0 + jnp.exp(-pre_act))
                x = pre_act * gate
                x_ref[sub, at, :] = x
                slope_ref[sub, at, :] = gate + x * (1.0 - gate)
                hi, lo = split2(x * tails[index][one])
                out_at = heads_at(head, index * width)
                left_x[sub, out_at, :LANES] = hi
                left_x[sub, out_at, LANES:] = lo
                hi, lo = split2(grads * growth[index][one])
                left_g[sub, out_at, :LANES] = hi
                left_g[sub, out_at, LANES:] = lo
        b_rows = pk1[k, SHARED : SHARED + LANES, :]
        c_rows = pk1[k, SHARED + LANES : SHARED + 2 * LANES, :]
        states = dot(left_x[sub], jnp.concatenate([b_rows, b_rows], axis=0), NN)
        u_f[k] = states[:width]
        u_r[k] = states[width:]
        pulls = dot(left_g[sub], jnp.concatenate([c_rows, c_rows], axis=0), NN)
        v_f[k] = pulls[:width]
        v_r[k] = pulls[width:]

    @pl.when(pair == GROUP // UNROLL - 1)
    def _():
        run[...] = jnp.zeros_like(run)

        def scan(step, _):
            up, down = step, GROUP - 1 - step
            moves = (
                (u_f, up, R_TOT_F), (v_r, up, R_TOT_R), (u_r, down, R_TOT_R), (v_f, down, R_TOT_F)
            )
            for slot, (ref, at_chunk, total) in enumerate(moves):
                factor = jnp.exp(rows[at_chunk, rows_at(total), :])
                for head in range(heads):
                    at = heads_at(head)
                    held = run[slot, at, :]
                    own = ref[at_chunk, at, :]
                    ref[at_chunk, at, :] = held
                    run[slot, at, :] = factor[first + head : first + head + 1] * held + own
            return 0

        lax.fori_loop(0, GROUP, scan, 0)
        whole = [
            rows[GROUP - 1, rows_at(pre), :] * jnp.exp(rows[GROUP - 1, rows_at(total), :])
            for pre, total in ((R_PRE_F, R_TOT_F), (R_PRE_R, R_TOT_R))
        ]
        for ends, pair in ((ends_up, (0, 1)), (ends_down, (2, 3))):
            ends[0:width, :] = run[pair[0]]
            ends[width : 2 * width, :] = run[pair[1]]
            ends[2 * width : 2 * width + 8, :] = whole[0]
            ends[2 * width + 8 : 2 * width + 16, :] = whole[1]


def phase_one(which, pk1, pk, cw, extra):
    first, last = SETS[which]
    heads = last - first
    width = heads * WIDTH
    block = jax.ShapeDtypeStruct((GROUP, width, LANES), f32)
    rows = jax.ShapeDtypeStruct((GROUP, 96, LANES), f32)
    ends = jax.ShapeDtypeStruct((2 * width + 16, LANES), f32)
    outs = [block] * 8 + ([rows] if which == 0 else []) + [ends, ends]
    specs = [chunked((width, LANES))] * 4 + [kept(out.shape) for out in outs[4:]]
    operands = [pk1, cw, *extra] if which == 0 else [pk1, pk, cw, *extra]
    return pl.pallas_call(
        functools.partial(phase_one_kernel, first, heads),
        name=f"phase_one_{which}",
        grid=(GROUP // UNROLL,),
        out_shape=outs,
        in_specs=[kept(operand.shape) for operand in operands],
        out_specs=specs,
        scratch_shapes=[
            pltpu.VMEM((GROUP + 2, width, LANES), bf16),
            pltpu.VMEM((UNROLL, 2 * width, 2 * LANES), bf16),
            pltpu.VMEM((UNROLL, 2 * width, 2 * LANES), bf16),
            pltpu.VMEM((4, width, LANES), f32),
        ],
        cost_estimate=cost(heads),
        compiler_params=pltpu.CompilerParams(vmem_limit_bytes=VMEM),
    )(*operands)


def phase_two_kernel(first, heads, *refs):
    (
        place_y, pk1, pk, cw, rate, skip,
        x_f, x_r, slope_f, slope_r, u_f, u_r, v_f, v_r, rows, *ends,
    ) = refs[:18]
    refs = refs[18:]
    beside = ()
    if first:
        wide_in, edges_in, params_in = refs[:3]
        refs = refs[3:]
    else:
        beside, refs = refs[:2], refs[2:]
    (
        rows_out, wide, edges, params,
        ext, entry, d_pre_f, d_pre_r, acc, lines, *of_chunk,
    ) = refs
    width = heads * WIDTH
    pair = pl.program_id(0)
    row, col = square_masks()
    is_low = row >= col
    is_up = row <= col
    low_one, up_one = zero_one(is_low), zero_one(is_up)
    ones = jnp.ones((LANES, LANES), bf16)
    lane = iota((WIDTH, LANES), 1)

    def held(sub, start, stop):
        return wide_in[sub, start:stop, :] if first else 0.0

    @pl.when(pair == 0)
    def _():
        fill_edges(ext, pk, beside)
        entry[...] = jnp.zeros_like(entry)
        here = place_y[0]
        for away in (3, 2, 1):
            for shift, slots, reached in (
                (away, ((0, 0, 0), (1, 1, 1)), here >= away),
                (ROWS - away, ((2, 0, 1), (3, 1, 0)), here + away < ROWS),
            ):

                @pl.when(reached)
                def _(came=ends[shift - 1], slots=slots):
                    for slot, part, total in slots:
                        start = 2 * width + total * 8
                        factor = came[start : start + 8, :]
                        for head in range(heads):
                            at = heads_at(head)
                            entry[slot, at, :] = (
                                factor[first + head : first + head + 1] * entry[slot, at, :]
                                + came[heads_at(head, part * width), :]
                            )

        of_chunk[8][...] = jnp.zeros_like(of_chunk[8])
        acc[...] = jnp.zeros_like(acc)
        for ref in (d_pre_f, d_pre_r):
            for edge in (0, 1, GROUP + 2, GROUP + 3):
                ref[edge] = jnp.zeros((width, LANES), f32)

    for sub in range(UNROLL):
        k = pair * UNROLL + sub
        (
            states, d_states, state_bits, d_state_bits, reach, pulled, gd, xt, line, a_hi, a_lo,
        ) = [ref.at[sub] for ref in of_chunk]
        b_rows = pk1[k, SHARED : SHARED + LANES, :]
        c_rows = pk1[k, SHARED + LANES : SHARED + 2 * LANES, :]
        step = [rows[k, rows_at(R_STEP_F + i), :] for i in range(2)]
        cum = [rows[k, rows_at(R_CUM_F + i), :] for i in range(2)]
        growth = [jnp.exp(c) for c in cum]
        total = [rows[k, rows_at(R_TOT_F + i), :] for i in range(2)]
        tail = [jnp.exp(total[i] - cum[i]) for i in range(2)]
        factor = [jnp.exp(total[i]) for i in range(2)]
        columns = jnp.concatenate(
            [cum[0], cum[1], jnp.zeros((LANES - 16, LANES), f32)], axis=0
        ).T
        into = (
            (states, state_bits, 0, u_f, R_PRE_F, 0),
            (states, state_bits, 1, u_r, R_POST_R, 2),
            (d_states, d_state_bits, 0, v_f, R_POST_F, 3),
            (d_states, d_state_bits, 1, v_r, R_PRE_R, 1),
        )
        for full, bits, index, local, decay_row, slot in into:
            decay = rows[k, rows_at(decay_row), :]
            for head in range(heads):
                at, to = heads_at(head), heads_at(head, index * width)
                value = local[sub, at, :] + decay[first + head : first + head + 1] * entry[slot, at, :]
                full[to, :] = value
                hi, lo = split2(value)
                bits[to, :LANES] = hi
                bits[to, LANES:] = lo
        reach[...] = dot(state_bits[...], jnp.concatenate([c_rows, c_rows], axis=1), NT)
        pulled[...] = dot(d_state_bits[...], jnp.concatenate([b_rows, b_rows], axis=1), NT)
        scores = dot(c_rows, b_rows, NT)
        d_g = jnp.zeros((LANES, LANES), f32)
        for head in range(heads):
            at = heads_at(head)
            one = slice(first + head, first + head + 1)
            gap_f = columns[:, first + head : first + head + 1] - cum[0][one]
            gap_r = columns[:, 8 + first + head : 9 + first + head] - cum[1][one]
            spread = jnp.exp(jnp.where(is_low, gap_f, gap_r))
            hi, lo = split2(scores * spread)
            a_hi[head, :, :LANES] = hi * low_one
            a_hi[head, :, LANES:] = hi * up_one
            a_lo[head, :, :LANES] = lo * low_one
            a_lo[head, :, LANES:] = lo * up_one
            grad_bits = pk[k, width + head * WIDTH : width + (head + 1) * WIDTH, :]
            grads = grad_bits.astype(f32)
            xs, bits = [], []
            for index, x_ref in enumerate((x_f, x_r)):
                scaled = x_ref[sub, at, :] * step[index][one]
                xs.append(scaled)
                bits.append(split2(scaled))
            d_a = dot(
                jnp.concatenate([grad_bits, grad_bits], axis=0),
                jnp.concatenate(
                    [
                        jnp.concatenate([bits[0][0], bits[1][0]], axis=1),
                        jnp.concatenate([bits[0][1], bits[1][1]], axis=1),
                    ],
                    axis=0,
                ),
                TN,
            )
            d_g += spread * (
                jnp.where(is_low, d_a[:, :LANES], 0.0) + jnp.where(is_up, d_a[:, LANES:], 0.0)
            )
            d_xs = dot(grad_bits, a_hi[head], NN) + dot(grad_bits, a_lo[head], NN)
            out = jnp.zeros((WIDTH, LANES), f32)
            d_skip_line = jnp.zeros((WIDTH, LANES), f32)
            for index, (x_ref, slope_ref, d_pre) in enumerate(
                ((x_f, slope_f, d_pre_f), (x_r, slope_r, d_pre_r))
            ):
                to = heads_at(head, index * width)
                half = slice(index * LANES, (index + 1) * LANES)
                hi, lo = bits[index]
                y = (
                    dot(hi, a_hi[head, :, half], NT)
                    + dot(lo, a_hi[head, :, half], NT)
                    + dot(hi, a_lo[head, :, half], NT)
                    + growth[index][one] * reach[to, :]
                )
                x = x_ref[sub, at, :]
                out += y + skip[one, :] * x
                d_skip_line += grads * x
                from_state = tail[index][one] * pulled[to, :]
                d_x = d_xs[:, half] + from_state
                d_pre[k + 2, at, :] = (step[index][one] * d_x + skip[one, :] * grads) * slope_ref[
                    sub, at, :
                ]
                own = jnp.sum(x * d_x, axis=0, keepdims=True)
                line[index, one, :] = (
                    jnp.sum(grads * y, axis=0, keepdims=True) - step[index][one] * own
                )
                line[2 + index, one, :] = jnp.sum(
                    xs[index] * from_state
                    + factor[index][one] * (d_states[to, :] * states[to, :]),
                    axis=0,
                    keepdims=True,
                )
                line[4 + index, one, :] = own
                hi, lo = split2(grads * growth[index][one])
                gd[to, :LANES] = hi
                gd[to, LANES:] = lo
                hi, lo = split2(xs[index] * tail[index][one])
                xt[to, :LANES] = hi
                xt[to, LANES:] = lo
            rows_out[k, at, :] = out.astype(bf16)
            line[6, one, :] = jnp.sum(d_skip_line, axis=0, keepdims=True)
        g_hi, g_lo = split2(d_g)
        wide_c = dot(gd[:, :LANES], state_bits[...], TN)
        wide[k, LANES : 2 * LANES, :] = held(sub, LANES, 2 * LANES) + (
            dot(g_hi, b_rows, NN)
            + dot(g_lo, b_rows, NN)
            + wide_c[:, :LANES]
            + wide_c[:, LANES:]
            + dot(gd[:, LANES:], state_bits[:, :LANES], TN)
        )
        wide_b = dot(xt[:, :LANES], d_state_bits[...], TN)
        wide[k, :LANES, :] = held(sub, 0, LANES) + (
            dot(g_hi, c_rows, TN)
            + dot(g_lo, c_rows, TN)
            + wide_b[:, :LANES]
            + wide_b[:, LANES:]
            + dot(xt[:, LANES:], d_state_bits[:, :LANES], TN)
        )
        wide[k, 2 * LANES : EDGE, :] = jnp.zeros((8, LANES), f32) + held(sub, 2 * LANES, EDGE)
        lines[:, pl.ds(pl.multiple_of(k * 8, 8), 8), :] = line[...]

    @pl.when(pair == GROUP // UNROLL - 1)
    def _():
        edges[...] = edges_in[...] if first else jnp.zeros_like(edges)
        token, place = iota((8, LANES), 0), iota((8, LANES), 1)
        first_rows = zero_one((token >= 5) & (place == token - 5))
        last_rows = zero_one((token >= 5) & (place == token + LANES - 8))

        def lines_of(marker, tile):
            hi, mid, lo = split3(tile)
            return dot(marker, hi, NT) + dot(marker, mid, NT) + dot(marker, lo, NT)

        def put_edge(slot, marker):
            def put(head, total):
                channel = (first + head) * WIDTH
                block, offset = channel // LANES, channel % LANES
                edges[slot, block * 8 : block * 8 + 8, offset : offset + WIDTH] = lines_of(
                    marker, total
                )
            return put

        def taps_of(tile, hid, puts):
            for head in range(heads):
                at = heads_at(head)
                hid_here = hid[at, :].astype(f32)
                own_f, own_r = d_pre_f[tile + 1, at, :], d_pre_r[tile + 1, at, :]
                later_f, earlier_r = d_pre_f[tile + 2, at, :], d_pre_r[tile, at, :]
                both = own_f + own_r
                acc[4, at, :] += both
                acc[0, at, :] += hid_here * both
                total = cw[0, at, :] * both
                for tap in range(1, 4):
                    shifted = pltpu.roll(
                        jnp.where(lane >= tap, own_f, later_f), LANES - tap, 1
                    ) + pltpu.roll(jnp.where(lane < LANES - tap, own_r, earlier_r), tap, 1)
                    acc[tap, at, :] += hid_here * shifted
                    total += cw[tap, at, :] * shifted
                for put in puts:
                    put(head, total)

        def keep_chunk(chunk):
            def put(head, total):
                rows_out[chunk, heads_at(head, width), :] = total.astype(bf16)
            return put

        taps_of(0, ext[0], [put_edge(2, last_rows)])
        taps_of(GROUP + 1, ext[GROUP + 1], [put_edge(3, first_rows)])
        taps_of(1, pk[0], [keep_chunk(0), put_edge(0, first_rows)])
        taps_of(GROUP, pk[GROUP - 1], [keep_chunk(GROUP - 1), put_edge(1, last_rows)])

        def inner(chunk, _):
            taps_of(chunk + 1, pk.at[chunk], [keep_chunk(chunk)])
            return 0

        lax.fori_loop(1, GROUP - 1, inner, 0)
        sums = jnp.zeros((8, width), f32)
        for tap in range(5):
            sums += lines_of(zero_one(token == tap), acc[tap])
        params[...] = params_in[...] if first else jnp.zeros_like(params)
        for start in range(0, width, LANES):
            size = min(LANES, width - start)
            block = (first * WIDTH + start) // LANES
            params[block * 8 : block * 8 + 8, :size] = sums[:, start : start + size]
        def all_rows(slot):
            return jnp.concatenate([rows[c, rows_at(slot), :] for c in range(GROUP)], axis=0)

        def over_chunks(value):
            total = value[0:8]
            for c in range(1, GROUP):
                total = total + value[c * 8 : c * 8 + 8]
            return total

        rates = jnp.concatenate([rate[...]] * GROUP, axis=0)
        tails_here = exact_dot(jnp.concatenate([lines[2], lines[3]], axis=0), ones, NN)
        d_args, d_rate = [], jnp.zeros((GROUP * 8, LANES), f32)
        for index in range(2):
            offset = index * GROUP * 8
            d_log = exact_dot(lines[index], (low_one, up_one)[index], NN) + tails_here[
                offset : offset + GROUP * 8
            ]
            d_args.append((lines[4 + index] + rates * d_log) * all_rows(R_SIG_F + index))
            d_rate += d_log * rates * all_rows(R_STEP_F + index)
        by_code = jnp.zeros((8, LANES), f32)
        for c in range(GROUP):
            own = slice(c * 8, c * 8 + 8)
            wide[c, 2 * LANES : EDGE, :] += d_args[0][own] + d_args[1][own]
            for index, table in enumerate(code_tables(pk1[c, TAIL:PACK, :].astype(f32))):
                by_code += exact_dot(d_args[index][own], table, NT)
        params[24:32, :] += (
            exact_dot(over_chunks(d_rate), zero_one(col == 0), NN)
            + exact_dot(over_chunks(lines[6]), zero_one(col == 1), NN)
            + by_code
        )


def phase_two(which, place_y, pk1, pk, cw, rate, skip, saved, rows, ends, carried):
    first, last = SETS[which]
    heads = last - first
    width = heads * WIDTH
    outs = [
        jax.ShapeDtypeStruct((GROUP, 2 * width, LANES), bf16),
        jax.ShapeDtypeStruct((GROUP, WIDE, LANES), f32),
        jax.ShapeDtypeStruct((4, 24, LANES), f32),
        jax.ShapeDtypeStruct((32, LANES), f32),
    ]
    whole = [pk1, pk, cw, rate, skip]
    in_specs = (
        [pl.BlockSpec(memory_space=pltpu.SMEM)]
        + [kept(operand.shape) for operand in whole]
        + [chunked((width, LANES))] * 8
        + [kept(rows.shape)] + [kept(end.shape) for end in ends]
    )
    if not which:
        in_specs += [kept(block.shape) for block in carried]
    else:
        in_specs += [chunked((WIDE, LANES)), kept((4, 24, LANES)), kept((32, LANES))]
    return pl.pallas_call(
        functools.partial(phase_two_kernel, first, heads),
        name=f"phase_two_{which}",
        grid=(GROUP // UNROLL,),
        out_shape=outs,
        in_specs=in_specs,
        out_specs=[kept(out.shape) for out in outs],
        scratch_shapes=[
            pltpu.VMEM((GROUP + 2, width, LANES), bf16),
            pltpu.VMEM((4, width, LANES), f32),
            pltpu.VMEM((GROUP + 4, width, LANES), f32),
            pltpu.VMEM((GROUP + 4, width, LANES), f32),
            pltpu.VMEM((5, width, LANES), f32),
            pltpu.VMEM((7, GROUP * 8, LANES), f32),
            pltpu.VMEM((UNROLL, 2 * width, LANES), f32),
            pltpu.VMEM((UNROLL, 2 * width, LANES), f32),
            pltpu.VMEM((UNROLL, 2 * width, 2 * LANES), bf16),
            pltpu.VMEM((UNROLL, 2 * width, 2 * LANES), bf16),
            pltpu.VMEM((UNROLL, 2 * width, LANES), f32),
            pltpu.VMEM((UNROLL, 2 * width, LANES), f32),
            pltpu.VMEM((UNROLL, 2 * width, 2 * LANES), bf16),
            pltpu.VMEM((UNROLL, 2 * width, 2 * LANES), bf16),
            pltpu.VMEM((UNROLL, 7, 8, LANES), f32),
            pltpu.VMEM((UNROLL, heads, LANES, 2 * LANES), bf16),
            pltpu.VMEM((UNROLL, heads, LANES, 2 * LANES), bf16),
        ],
        cost_estimate=cost(2 * heads),
        compiler_params=pltpu.CompilerParams(vmem_limit_bytes=VMEM),
    )(place_y, *whole, *saved, rows, *ends, *carried)


def finish_kernel(edges, from_prev, from_next, sums, _, out, lines, sem):
    for target in range(GROUP):
        lines[target] = sums[...]
    lines[0, :24, :] = sums[:24, :] + (edges[0] + from_prev[...])
    lines[GROUP - 1, :24, :] = sums[:24, :] + (edges[1] + from_next[...])
    copy = pltpu.make_async_copy(lines, out.at[:, EDGE:WIDE, :], sem)
    copy.start()
    copy.wait()


def finish(edges, from_prev, from_next, sums, wide):
    anywhere = pl.BlockSpec(memory_space=pl.ANY)
    return pl.pallas_call(
        finish_kernel,
        name="finish",
        out_shape=jax.ShapeDtypeStruct(wide.shape, f32),
        in_specs=[WHOLE] * 4 + [anywhere],
        out_specs=anywhere,
        scratch_shapes=[pltpu.VMEM((GROUP, WIDE - EDGE, LANES), f32), pltpu.SemaphoreType.DMA],
        input_output_aliases={4: 0},
        compiler_params=pltpu.CompilerParams(vmem_limit_bytes=VMEM),
    )(edges, from_prev, from_next, sums, wide)


def unpack_kernel(place_z, *refs):
    sets, wide = refs[: len(SETS)], refs[len(SETS)]
    (
        layer_out, hid_out, b_out, c_out, dt_out, taps_out, bias_out, rate_out, skip_out, shift_out, code_out,
    ) = refs[len(SETS) + 1 :]
    row, col = square_masks()
    eye = zero_one(row == col)
    line = iota((16, LANES), 0)
    at_start = (line < 3) & (place_z[0] == 0)
    at_end = (line >= 13) & (place_z[0] == GROUP - 1)
    blank = jnp.zeros((8, LANES), f32)
    for order, target in enumerate((layer_out, hid_out)):
        for block in range(GROUP * CH // LANES):
            pieces, edge, taps = [], [], []
            for half in range(2):
                channel = block * LANES + half * WIDTH
                group, at = channel // CH, channel % CH
                offset = at % LANES
                start = EDGE + at // LANES * 8
                taps.append(wide[group, start : start + 8, offset : offset + WIDTH])
                edge.append(wide[group, start : start + 8, offset : offset + WIDTH])
                which, at = set_row(at, order)
                pieces.append(sets[which][group, at : at + WIDTH, :])
            lanes = slice(block * LANES, (block + 1) * LANES)
            flipped = dot(eye, jnp.concatenate(pieces, axis=0), NT)
            if order:
                taps = jnp.concatenate(taps, axis=1)
                taps_out[:, lanes] = taps[:4]
                bias_out[:, lanes] = taps[4:5]
                edge = jnp.concatenate(edge, axis=1)
                first = jnp.concatenate([pltpu.roll(edge, 3, 0), blank], axis=0)
                head = jnp.where(at_start, first, flipped[:16])
                tail = jnp.where(
                    at_end, jnp.concatenate([blank, edge], axis=0), flipped[LANES - 16 :]
                )
                flipped = jnp.concatenate([head, flipped[16 : LANES - 16], tail], axis=0)
            target[:, lanes] = flipped.astype(bf16)
    for base, target in ((0, b_out), (LANES, c_out)):
        total = wide[0, base : base + LANES, :]
        for group in range(1, GROUP):
            total += wide[group, base : base + LANES, :]
        target[...] = total
    lines = jnp.concatenate(
        [wide[group, 2 * LANES : EDGE, :] for group in range(GROUP)], axis=0
    )
    pick_row, pick_col = iota((40, GROUP * 8), 0), iota((40, GROUP * 8), 1)
    pick = zero_one(
        ((pick_col % 8) < HEADS) & ((pick_col // 8) * HEADS + (pick_col % 8) == pick_row)
    )
    hi, mid, lo = split3(lines)
    dt_out[...] = dot(pick, hi, NN) + dot(pick, mid, NN) + dot(pick, lo, NN)
    heads = jnp.concatenate([wide[group, WIDE - 8 : WIDE, :] for group in range(GROUP)], axis=0)
    by_head = sum(
        lax.dot_general(part, pick, (((0,), (1,)), ((), ())), preferred_element_type=f32)
        for part in split3(heads)
    )
    rate_out[...] = by_head[0:1]
    skip_out[...] = by_head[1:2]
    shift_out[...] = by_head[2:3]
    code_out[...] = by_head[3:15]


def unpack(place_z, sets, wide):
    rows = jax.ShapeDtypeStruct((LANES, GROUP * CH), bf16)
    square = jax.ShapeDtypeStruct((LANES, LANES), f32)
    return pl.pallas_call(
        unpack_kernel,
        name="unpack",
        out_shape=[rows, rows, square, square, jax.ShapeDtypeStruct((40, LANES), f32)]
        + [
            jax.ShapeDtypeStruct(shape, f32)
            for shape in ((4, GROUP * CH), (1, GROUP * CH), (1, 40), (1, 40), (1, 40), (12, 40))
        ],
        in_specs=[pl.BlockSpec(memory_space=pltpu.SMEM)] + [WHOLE] * (len(SETS) + 1),
        out_specs=[WHOLE] * 11,
        compiler_params=pltpu.CompilerParams(vmem_limit_bytes=VMEM),
    )(place_z, *sets, wide)


def exchange(array):
    return lax.all_to_all(array, "seq", 0, 0, axis_index_groups=Z_GROUPS)


def along_y(array, by):
    pairs = [
        (y * GROUP + z, (y + by) * GROUP + z)
        for y in range(ROWS)
        for z in range(GROUP)
        if 0 <= y + by < ROWS
    ]
    return lax.ppermute(array, "seq", pairs)


def beside(array, by):
    count = lax.axis_size("seq")
    return lax.ppermute(array, "seq", [(i, i + by) for i in range(count) if 0 <= i + by < count])


def cross_y(up, down, run):
    came = []
    for shift in range(1, ROWS):
        pairs = [
            (y * GROUP + z, (y + shift) % ROWS * GROUP + z) for y in range(ROWS) for z in range(GROUP)
        ]
        came.append(lax.ppermute(jnp.where(run + shift < ROWS, up, down), "seq", pairs))
    return came


def flip_bit(array, axis, bit):
    count = lax.axis_size(axis)
    return lax.ppermute(array, axis, [(i, i ^ bit) for i in range(count)])


def total_over(array, axis, low, high):
    near, far, both = (flip_bit(array, axis, bits) for bits in (low, high, low | high))
    return (array + near) + (far + both)


def per_device(
    hidden, b_proj, c_proj, dt_raw, base_ids, complement,
    a_log, d_skip, dt_bias, base_shift, conv_w, conv_b, grad_out,
):
    place = lax.axis_index("seq")
    group, run = place % GROUP, place // GROUP
    here_z, here_y = group[None].astype(jnp.int32), run[None].astype(jnp.int32)
    taps = jnp.concatenate([conv_w, conv_b[None]], axis=0).reshape(5, GROUP, CH)
    taps = lax.dynamic_index_in_dim(taps, group, 1, keepdims=False)
    cw = jnp.broadcast_to(taps[:, :, None], (5, CH, LANES))
    per_head = jnp.stack([-jnp.exp(a_log), d_skip], axis=0)
    tables = jnp.concatenate([dt_bias[None], base_shift], axis=0)
    tables = jnp.concatenate([per_head, tables], axis=0).reshape(15, GROUP, HEADS)
    tables = lax.dynamic_index_in_dim(tables, group, 1, keepdims=False)
    tables = jnp.pad(tables, ((0, 0), (0, 8 - HEADS)))
    rate = jnp.broadcast_to(tables[0][:, None], (8, LANES))
    skip = jnp.broadcast_to(tables[1][:, None], (8, LANES))
    shift_table = jnp.pad(tables[2:].T, ((0, 0), (2, LANES - 15)))

    taps = [cw[:, first * WIDTH : last * WIDTH] for first, last in SETS]

    packed = pack(
        complement, hidden[0], grad_out[0], b_proj[0], c_proj[0], dt_raw[0].T, base_ids
    )
    pk = [exchange(packed[0])]
    last, leading, taps, shift_table, rate, skip = lax.optimization_barrier(
        (hidden[0, -8:], hidden[0, :8], taps, shift_table, rate, skip)
    )
    second = add_rows_beside(beside(last, 1), beside(leading, -1), packed[1])
    pk.append(exchange(second))
    cut = SETS[0][1] * WIDTH
    edge_chunks = (along_y(pk[0][GROUP - 1, :cut], 1), along_y(pk[0][0, :cut], -1))
    saved, ends, sets, carried = [], [], [], edge_chunks
    for which, tap in enumerate(taps):
        *blocks, up, down = phase_one(
            which, pk[0], pk[which], tap, (rows,) if which else (shift_table, rate, *edge_chunks)
        )
        if not which:
            rows = blocks.pop()
        saved.append(blocks)
        ends.append(cross_y(up, down, run))
    for which, tap in enumerate(taps):
        out, *carried = phase_two(
            which, here_y, pk[0], pk[which], tap, rate, skip, saved[which], rows, ends[which], carried
        )
        sets.append(exchange(out))
    wide, edges, sums = carried
    lines = jnp.concatenate([sums, edges[2], edges[3]], axis=0)
    near, both = flip_bit(lines, "seq", GROUP), flip_bit(lines, "seq", 3 * GROUP)
    far = flip_bit(sums, "seq", 2 * GROUP)
    odd = run % 2 == 1
    from_next = jnp.where(odd, both[32:56], near[32:56])
    from_next = jnp.where(run == ROWS - 1, 0.0, from_next)
    from_prev = jnp.where(odd, near[56:], both[56:])
    from_prev = jnp.where(run == 0, 0.0, from_prev)
    sums = (sums + near[:32]) + (far + both[:32])
    sums = total_over(sums, "dp", 1, 2)
    sums = sums + flip_bit(sums, "dp", 4)
    wide = exchange(finish(edges, from_prev, from_next, sums, wide))
    layer_out, d_hidden, d_b, d_c, d_dt, taps, bias, rates, skips, shifts, codes = unpack(
        here_z, sets, wide
    )
    return (
        layer_out[None], d_hidden[None], d_b[None], d_c[None], d_dt.T[None],
        rates[0], skips[0], shifts[0], codes, taps, bias[0],
    )


def solution(mesh):
    rows = P("dp", "seq", None)
    placed = (rows, rows, rows, rows, P("dp", "seq"), P(), P(), P(), P(), P(), P(), P(), rows)
    return jax.shard_map(
        per_device,
        mesh=mesh,
        in_specs=placed,
        out_specs=(rows,) * 5 + (P(),) * 6,
        check_vma=False,
    )
```
